32 devices in a mesh: wide: 8 (over z, x), narrow: 4 (over y, core).
Axes of the slice: x: 2, y: 2, z: 4, core: 2. Of those that a mesh axis runs over, the one named last changes fastest.
Arguments:
- token_ids: int32 [2, 32, 256], P(None, ('wide', 'narrow')), may hold values from 0 to 50256
- doc_ids: int32 [2, 32, 256], P(None, ('wide', 'narrow')), may hold values from 0 to 7, never falling along the last dimension, each value on 1 to 128 neighbouring positions
- loss_positions: int32 [2, 32, 32], P(None, ('wide', 'narrow')), may hold values from 0 to 254
- tied_table_master: float32 [50304, 1024], P(('wide', 'narrow')), may hold values from -0.375 to 0.375
- qkv_master: float32 [1024, 3072], P(('wide', 'narrow')), may hold values from -0.1875 to 0.1875
- out_master: float32 [1024, 1024], P(('wide', 'narrow')), may hold values from -0.75 to 0.75
- up_master: float32 [1024, 4096], P(('wide', 'narrow')), may hold values from -0.1875 to 0.1875
- down_master: float32 [4096, 1024], P(('wide', 'narrow')), may hold values from -0.09375 to 0.09375
- norm_master: float32 [1024, 6], P(('wide', 'narrow')), may hold values from -1 to 1.5, as said below
- table_first_moment: float32 [50304, 1024], P(('wide', 'narrow')), may hold values from -8.34465e-07 to 8.34465e-07
- first_qkv: float32 [1024, 3072], P(('wide', 'narrow')), may hold values from -8.34465e-07 to 8.34465e-07
- first_out: float32 [1024, 1024], P(('wide', 'narrow')), may hold values from -8.34465e-07 to 8.34465e-07
- first_up: float32 [1024, 4096], P(('wide', 'narrow')), may hold values from -8.34465e-07 to 8.34465e-07
- first_down: float32 [4096, 1024], P(('wide', 'narrow')), may hold values from -8.34465e-07 to 8.34465e-07
- first_norms: float32 [1024, 6], P(('wide', 'narrow')), may hold values from -3.33786e-06 to 3.33786e-06
- table_second_moment: float32 [50304, 1024], P(('wide', 'narrow')), may hold values from 1.5600538e-15 to 6.2402154e-15
- second_qkv: float32 [1024, 3072], P(('wide', 'narrow')), may hold values from 1.5600538e-15 to 6.2402154e-15
- second_out: float32 [1024, 1024], P(('wide', 'narrow')), may hold values from 1.5600538e-15 to 6.2402154e-15
- second_up: float32 [1024, 4096], P(('wide', 'narrow')), may hold values from 1.5600538e-15 to 6.2402154e-15
- second_down: float32 [4096, 1024], P(('wide', 'narrow')), may hold values from 1.5600538e-15 to 6.2402154e-15
- second_norms: float32 [1024, 6], P(('wide', 'narrow')), may hold values from 2.4960862e-14 to 9.9843446e-14
Outputs:
- loss_value: float32 [], replicated
- grad_norm: float32 [], replicated
- matrix_norms: float32 [3, 6], replicated
- new_table: float32 [50304, 1024], P(('wide', 'narrow'))
- new_qkv: float32 [1024, 3072], P(('wide', 'narrow'))
- new_out: float32 [1024, 1024], P(('wide', 'narrow'))
- new_up: float32 [1024, 4096], P(('wide', 'narrow'))
- new_down: float32 [4096, 1024], P(('wide', 'narrow'))
- new_norms: float32 [1024, 6], P(('wide', 'narrow'))
- new_first_table: float32 [50304, 1024], P(('wide', 'narrow'))
- new_first_qkv: float32 [1024, 3072], P(('wide', 'narrow'))
- new_first_out: float32 [1024, 1024], P(('wide', 'narrow'))
- new_first_up: float32 [1024, 4096], P(('wide', 'narrow'))
- new_first_down: float32 [4096, 1024], P(('wide', 'narrow'))
- new_first_norms: float32 [1024, 6], P(('wide', 'narrow'))
- new_second_table: float32 [50304, 1024], P(('wide', 'narrow'))
- new_second_qkv: float32 [1024, 3072], P(('wide', 'narrow'))
- new_second_out: float32 [1024, 1024], P(('wide', 'narrow'))
- new_second_up: float32 [1024, 4096], P(('wide', 'narrow'))
- new_second_down: float32 [4096, 1024], P(('wide', 'narrow'))
- new_second_norms: float32 [1024, 6], P(('wide', 'narrow'))
The draws below stay inside these ranges and needn't reach their ends.
Inputs may be any that keep to these rules, and one draw needn't show every extreme that they name: `doc_ids`: within a sequence document numbers never fall. `norm_master`: columns 0, 2 and 4 are gains, columns 1, 3 and 5 shifts.
All inputs are finite; a program needn't handle non-finite values.
Results may differ from the reference program's by a relative error of at most 0.0095.
The reference program's roundings to bfloat16 on the way count: a program that leaves them out, or rounds other values in their place, can miss the bound.
Values may be sent and summed in bfloat16 or wider, within the bound.
No kernel may reach another device: no remote copies, remote signals or barrier semaphores. Data moves between devices by JAX's collectives and lax.ppermute only.
A program may use at most 384 MiB of HBM per device.

```python
import math
import jax
import jax.numpy as jnp
import numpy as np
from jax import lax

MODEL_DIMENSION = 1024
HEADS = 16
HEAD_DIM = 64
FF = 4096
VOCAB = 50257
PADDED_VOCAB = 50304
LEN = 256
PICK = 32
MICRO = 2
SEQS = 32
PARAMETER_COUNT = 64100352


def draw_norm_master(key, part):
    draw_base = jax.random.normal(key, (MODEL_DIMENSION, 6), jnp.float32)
    draw_base = jnp.clip(draw_base, -5.0, 5.0)
    column_parity = jnp.arange(6) % 2
    return jnp.where(column_parity[None, :] == 0, 1.0 + 0.1 * draw_base, 0.2 * draw_base)


def with_ends(drawn, own_key, low, high):
    dims = drawn.shape
    spot = [jax.random.randint(jax.random.fold_in(own_key, axis), (), 0, dims[axis]) for axis in range(len(dims))]
    drawn = drawn.at[tuple(spot)].set(low)
    longest = dims.index(max(dims))
    spot[longest] = (spot[longest] + 1) % dims[longest]
    return drawn.at[tuple(spot)].set(high)


def shard_levels(stream_key, shape, split, smallest, largest):
    loudness, own = 1.0, jax.random.fold_in(stream_key, 6)
    for dim, blocks in split:
        steps = jnp.exp(jax.random.uniform(jax.random.fold_in(own, dim), (blocks,), jnp.float32, smallest / len(split), largest / len(split)))
        loudness = loudness * jnp.repeat(steps, shape[dim] // blocks).reshape([-1 if axis == dim else 1 for axis in range(len(shape))])
    return loudness


def rank_bounds(count, lean):
    loads = [(1 << 20) // math.isqrt(standing ** lean) + 1 for standing in range(1, count + 1)]
    width = 1 + sum(loads) // (1 << 30)
    return np.cumsum(np.array([max(1, weight // width) for weight in loads]))


def skewed_ids(stream_key, extent, count, slope):
    listing = rank_bounds(count, slope)
    lot = jax.random.randint(jax.random.fold_in(stream_key, 1), extent, 0, int(listing[count - 1]))
    grade = jnp.searchsorted(jnp.asarray(listing, jnp.int32), lot, side="right")
    return jax.random.permutation(jax.random.fold_in(stream_key, 2), count)[grade].astype(jnp.int32)


def length_profile(amount, total, reach, lean):
    portions = [(1 << 20) // math.isqrt(rank ** lean) + 1 for rank in range(2, amount + 1)]
    spare, given = total - reach - (amount - 1), [1] * (amount - 1)
    while spare > 0:
        movable = [i for i in range(amount - 1) if given[i] < reach]
        pool, budget = sum([portions[i] for i in movable]), spare
        for i in movable:
            more = min(reach - given[i], max(1, budget * portions[i] // pool), spare)
            given[i] = given[i] + more
            spare = spare - more
    return np.array([reach] + given)


def ragged_sizes(key, number_of, total, bound, slope):
    if number_of == 2:
        one = jax.random.randint(key, (), max(1, total - bound), min(bound, total - 1) + 1)
        return jnp.stack([one, total - one])
    sizes = jnp.asarray(length_profile(number_of, total, bound, slope), jnp.int32)
    pairs = (number_of - 1) // 2
    donor, sink = sizes[1:1 + 2 * pairs:2], sizes[2:2 + 2 * pairs:2]
    room = jnp.minimum(donor - 1, bound - sink)
    moved = jax.random.randint(jax.random.fold_in(key, 1), (pairs,), 0, 1 << 20) % (room + 1)
    sizes = sizes.at[1:1 + 2 * pairs:2].set(donor - moved).at[2:2 + 2 * pairs:2].set(sink + moved)
    return sizes[jax.random.permutation(jax.random.fold_in(key, 2), number_of)]


def centred(stream_key, extent, scale, limit, pieces=(), dtype=jnp.bfloat16):
    loudness = shard_levels(stream_key, extent, pieces, -0.22, 0.18) if pieces else 1.0
    drawn = jax.random.normal(stream_key, extent, jnp.float32) * scale * loudness
    return jnp.minimum(jnp.maximum(drawn, -limit), limit).astype(dtype)


def setup_inputs(seed: int = 0) -> dict:
    key_of = jax.random.split(jax.random.key(seed), 22)
    return {
        "token_ids": with_ends(skewed_ids(key_of[0], (MICRO, SEQS, LEN), VOCAB, 0), jax.random.fold_in(key_of[0], 3), 0, VOCAB - 1).astype(jnp.int32),
        "doc_ids": jax.vmap(lambda own: jnp.searchsorted(jnp.cumsum(ragged_sizes(own, 8, LEN, LEN // 2, 1)), jnp.arange(LEN), side="right"))(jax.random.split(key_of[1], MICRO * SEQS)).reshape((MICRO, SEQS, LEN)).astype(jnp.int32),
        "loss_positions": with_ends(jax.random.randint(key_of[2], (MICRO, SEQS, PICK), 0, LEN - 1), jax.random.fold_in(key_of[2], 1), 0, (LEN - 1) - 1).astype(jnp.int32),
        "tied_table_master": centred(key_of[3], (PADDED_VOCAB, MODEL_DIMENSION), (MODEL_DIMENSION // 4) ** -0.5, 0.375, ((0, 32),), jnp.float32),
        "qkv_master": centred(key_of[4], (MODEL_DIMENSION, 3 * MODEL_DIMENSION), MODEL_DIMENSION ** -0.5, 0.1875, ((0, 32),), jnp.float32),
        "out_master": centred(key_of[5], (MODEL_DIMENSION, MODEL_DIMENSION), (max(MODEL_DIMENSION * 16 // LEN, 1)) ** -0.5, 0.75, ((0, 32),), jnp.float32),
        "up_master": centred(key_of[6], (MODEL_DIMENSION, FF), MODEL_DIMENSION ** -0.5, 0.1875, ((0, 32),), jnp.float32),
        "down_master": centred(key_of[7], (FF, MODEL_DIMENSION), FF ** -0.5, 0.09375, ((0, 32),), jnp.float32),
        "norm_master": draw_norm_master(jax.random.fold_in(key_of[21], 71), 0),
        "table_first_moment": centred(key_of[9], (PADDED_VOCAB, MODEL_DIMENSION), (0.0011 * PARAMETER_COUNT ** -0.5), 8.344650268554688e-07, ((0, 32),), jnp.float32),
        "first_qkv": centred(key_of[10], (MODEL_DIMENSION, 3 * MODEL_DIMENSION), (0.0011 * PARAMETER_COUNT ** -0.5), 8.344650268554688e-07, ((0, 32),), jnp.float32),
        "first_out": centred(key_of[11], (MODEL_DIMENSION, MODEL_DIMENSION), (0.0011 * PARAMETER_COUNT ** -0.5), 8.344650268554688e-07, ((0, 32),), jnp.float32),
        "first_up": centred(key_of[12], (MODEL_DIMENSION, FF), (0.0011 * PARAMETER_COUNT ** -0.5), 8.344650268554688e-07, ((0, 32),), jnp.float32),
        "first_down": centred(key_of[13], (FF, MODEL_DIMENSION), (0.0011 * PARAMETER_COUNT ** -0.5), 8.344650268554688e-07, ((0, 32),), jnp.float32),
        "first_norms": centred(key_of[14], (MODEL_DIMENSION, 6), (0.0044 * PARAMETER_COUNT ** -0.5), 3.337860107421875e-06, ((0, 32),), jnp.float32),
        "table_second_moment": jnp.clip(jnp.exp(math.log(6.24021538923273e-15) - 1.3862944 * jax.random.uniform(key_of[15], (PADDED_VOCAB, MODEL_DIMENSION), jnp.float32) ** shard_levels(key_of[15], (PADDED_VOCAB, MODEL_DIMENSION), ((0, 32),), -0.2, 0.2)), 1.5600538473081824e-15, 6.24021538923273e-15),
        "second_qkv": jnp.clip(jnp.exp(math.log(6.24021538923273e-15) - 1.3862944 * jax.random.uniform(key_of[16], (MODEL_DIMENSION, 3 * MODEL_DIMENSION), jnp.float32) ** shard_levels(key_of[16], (MODEL_DIMENSION, 3 * MODEL_DIMENSION), ((0, 32),), -0.2, 0.2)), 1.5600538473081824e-15, 6.24021538923273e-15),
        "second_out": jnp.clip(jnp.exp(math.log(6.24021538923273e-15) - 1.3862944 * jax.random.uniform(key_of[17], (MODEL_DIMENSION, MODEL_DIMENSION), jnp.float32) ** shard_levels(key_of[17], (MODEL_DIMENSION, MODEL_DIMENSION), ((0, 32),), -0.2, 0.2)), 1.5600538473081824e-15, 6.24021538923273e-15),
        "second_up": jnp.clip(jnp.exp(math.log(6.24021538923273e-15) - 1.3862944 * jax.random.uniform(key_of[18], (MODEL_DIMENSION, FF), jnp.float32) ** shard_levels(key_of[18], (MODEL_DIMENSION, FF), ((0, 32),), -0.2, 0.2)), 1.5600538473081824e-15, 6.24021538923273e-15),
        "second_down": jnp.clip(jnp.exp(math.log(6.24021538923273e-15) - 1.3862944 * jax.random.uniform(key_of[19], (FF, MODEL_DIMENSION), jnp.float32) ** shard_levels(key_of[19], (FF, MODEL_DIMENSION), ((0, 32),), -0.2, 0.2)), 1.5600538473081824e-15, 6.24021538923273e-15),
        "second_norms": jnp.clip(jnp.exp(math.log(9.984344622772368e-14) - 1.3862944 * jax.random.uniform(key_of[20], (MODEL_DIMENSION, 6), jnp.float32) ** shard_levels(key_of[20], (MODEL_DIMENSION, 6), ((0, 32),), -0.2, 0.2)), 2.496086155693092e-14, 9.984344622772368e-14),
    }


@jax.custom_vjp
def low(v):
    return lax.optimization_barrier(v.astype(jnp.bfloat16)).astype(jnp.float32)

@jax.custom_vjp
def low_back(v):
    return v

def low_keep(v):
    return (low(v), None)

def low_pass(kept, grad):
    return (grad,)

def back_keep(v):
    return (v, None)

def back_low(kept, grad):
    return (low(grad),)
low.defvjp(low_keep, low_pass)
low_back.defvjp(back_keep, back_low)
highest = lax.Precision.HIGHEST
neg_fill = -1e+30
beta_first = 0.9
beta_second = 0.999
adam_epsilon = 1e-12
decay_rates = (0.01, 0.01, 0.01, 0.01, 0.01, 0.0)
learn_rate = 0.5
clip_limit = 0.01
norm_epsilon = 1e-05
step_count = 5.0

def layer_norm(values, gain_row, offset):
    centered = values - lax.optimization_barrier(jnp.mean(values, axis=-1, keepdims=True))
    spread = lax.optimization_barrier(jnp.mean(centered * centered, axis=-1, keepdims=True))
    return centered * lax.rsqrt(spread + norm_epsilon) * gain_row + offset

def matmul(left_side, right_side):
    return jnp.dot(left_side, right_side, precision=highest, preferred_element_type=jnp.float32)

def sequence_loss(weights, tokens, documents, pick_rows):
    table, qkv_weight, out_weight, up_weight, down_weight, norm_params = weights
    model_width = table.shape[1]
    length = tokens.shape[0]
    x_embed = table[tokens]
    normed_one = low(layer_norm(x_embed, norm_params[:, 0], norm_params[:, 1]))
    qkv_all = low(low_back(matmul(normed_one, qkv_weight))).reshape(length, 3, HEADS, HEAD_DIM)
    queries = qkv_all[:, 0]
    keys_all = qkv_all[:, 1]
    values_all = qkv_all[:, 2]
    scores = jnp.einsum('qhd,khd->hqk', queries, keys_all, precision=highest) * HEAD_DIM ** (-0.5)
    scores = low_back(scores)
    position = jnp.arange(length)
    allowed = (position[None, :] <= position[:, None]) & (documents[None, :] == documents[:, None])
    scores = jnp.where(allowed[None], scores, neg_fill)
    top_score = lax.optimization_barrier(jnp.max(scores, axis=-1, keepdims=True))
    exp_scores = jnp.exp(scores - top_score)
    prob_low = low(exp_scores / lax.optimization_barrier(jnp.sum(exp_scores, axis=-1, keepdims=True)))
    context = jnp.einsum('hqk,khd->qhd', prob_low, values_all, precision=highest).reshape(length, model_width)
    context = low(low_back(context))
    x_attn = x_embed + low_back(matmul(context, out_weight))
    normed_two = low(layer_norm(x_attn, norm_params[:, 2], norm_params[:, 3]))
    up_value = low_back(matmul(normed_two, up_weight))
    activated = low(jax.nn.gelu(up_value, approximate=True))
    x_out = x_attn + low_back(matmul(activated, down_weight))
    final_norm = layer_norm(x_out, norm_params[:, 4], norm_params[:, 5])
    picked_rows = low(final_norm[pick_rows])
    logits = low_back(matmul(picked_rows, table.T))
    valid_cols = jnp.arange(table.shape[0]) < VOCAB
    logits = jnp.where(valid_cols[None, :], logits, neg_fill)
    top_logit = lax.optimization_barrier(jnp.max(logits, axis=-1, keepdims=True))
    log_total = top_logit[:, 0] + jnp.log(lax.optimization_barrier(jnp.sum(jnp.exp(logits - top_logit), axis=-1)))
    targets = tokens[pick_rows + 1]
    target_logit = jnp.take_along_axis(logits, targets[:, None], axis=1)[:, 0]
    return jnp.sum(log_total - target_logit)

def reference(token_ids, doc_ids, loss_positions, tied_table_master, qkv_master, out_master, up_master, down_master, norm_master, table_first_moment, first_qkv, first_out, first_up, first_down, first_norms, table_second_moment, second_qkv, second_out, second_up, second_down, second_norms):
    masters = (tied_table_master, qkv_master, out_master, up_master, down_master, norm_master)
    firsts = (table_first_moment, first_qkv, first_out, first_up, first_down, first_norms)
    seconds = (table_second_moment, second_qkv, second_out, second_up, second_down, second_norms)
    count_all = MICRO * SEQS * PICK
    flat_tokens = token_ids.reshape(MICRO * SEQS, LEN)
    flat_docs = doc_ids.reshape(MICRO * SEQS, LEN)
    flat_picks = loss_positions.reshape(MICRO * SEQS, PICK)
    piece_loss = jax.checkpoint(sequence_loss)

    def total_loss(weights):
        rounded = tuple((low(weight) for weight in weights))

        def add_one(carried, inputs):
            return (carried + piece_loss(rounded, inputs[0], inputs[1], inputs[2]), None)
        summed, unused = lax.scan(add_one, jnp.zeros((), jnp.float32), (flat_tokens, flat_docs, flat_picks))
        return summed / count_all
    loss_value, pullback = jax.vjp(total_loss, masters)
    all_grads = pullback(jnp.ones((), jnp.float32))[0]
    squares = jnp.stack([jnp.sum(gradient * gradient) for gradient in all_grads])
    grad_norm = jnp.sqrt(jnp.sum(squares))
    factor = jnp.minimum(1.0, clip_limit / grad_norm)
    new_weights = []
    new_firsts = []
    new_seconds = []
    weight_norms = []
    update_norms = []
    for group_index in range(6):
        clipped = factor * all_grads[group_index]
        first_new = beta_first * firsts[group_index] + (1.0 - beta_first) * clipped
        second_new = beta_second * seconds[group_index] + (1.0 - beta_second) * clipped * clipped
        direction = first_new / (1.0 - beta_first ** step_count) / (jnp.sqrt(second_new / (1.0 - beta_second ** step_count)) + adam_epsilon) + decay_rates[group_index] * masters[group_index]
        weight_norm = jnp.sqrt(jnp.sum(masters[group_index] * masters[group_index]))
        update_norm = jnp.sqrt(jnp.sum(direction * direction))
        new_weights.append(masters[group_index] - learn_rate * (weight_norm / update_norm) * direction)
        new_firsts.append(first_new)
        new_seconds.append(second_new)
        weight_norms.append(weight_norm)
        update_norms.append(update_norm)
    matrix_norms = jnp.stack([factor * jnp.sqrt(squares), jnp.stack(weight_norms), jnp.stack(update_norms)])
    return (loss_value, grad_norm, matrix_norms, new_weights[0], new_weights[1], new_weights[2], new_weights[3], new_weights[4], new_weights[5], new_firsts[0], new_firsts[1], new_firsts[2], new_firsts[3], new_firsts[4], new_firsts[5], new_seconds[0], new_seconds[1], new_seconds[2], new_seconds[3], new_seconds[4], new_seconds[5])
```

```python
import math

import jax
import jax.numpy as jnp
from jax import lax
from jax.sharding import PartitionSpec as P

HEAD_DIM = 64
VOCAB = 50257

neg_fill = -1e30
beta_first = 0.9
beta_second = 0.999
adam_epsilon = 1e-12
decay_rates = (0.01, 0.01, 0.01, 0.01, 0.01, 0.0)
learn_rate = 0.5
clip_limit = 0.01
norm_epsilon = 1e-05
step_count = 5.0
bf16 = jnp.bfloat16
f32 = jnp.float32


def layer_norm(values, gain_row, offset):
    centered = values - jnp.mean(values, axis=-1, keepdims=True)
    spread = jnp.mean(centered * centered, axis=-1, keepdims=True)
    return centered * lax.rsqrt(spread + norm_epsilon) * gain_row + offset


def norm_backward(values, gain_row, offset, grad_output):
    unused, pullback = jax.vjp(layer_norm, values, gain_row, offset)
    return pullback(grad_output)


def gelu_tanh(values):
    return jax.nn.gelu(values, approximate=True)


def matmul(left_side, right_side):
    return jnp.dot(left_side, right_side, preferred_element_type=f32)


def contract_rows(left_side, right_side):
    return lax.dot_general(
        left_side, right_side, (((0,), (0,)), ((), ())), preferred_element_type=f32
    )


def contract_cols(left_side, right_side):
    return lax.dot_general(
        left_side, right_side, (((1,), (1,)), ((), ())), preferred_element_type=f32
    )


class Links:
    def __init__(self):
        self.wide = lax.axis_size("wide")
        self.narrow = lax.axis_size("narrow")
        self.depth = self.wide // 2
        wide_place = lax.axis_index("wide")
        narrow_place = lax.axis_index("narrow")
        self.device = wide_place * self.narrow + narrow_place
        self.z = wide_place // 2
        self.place = {"x": wide_place % 2, "y": narrow_place // 2, "c": narrow_place % 2}

    def swap(self, values, axis):
        if axis == "x":
            return lax.ppermute(values, "wide", [(i, i ^ 1) for i in range(self.wide)])
        step = 2 if axis == "y" else 1
        return lax.ppermute(values, "narrow", [(i, i ^ step) for i in range(self.narrow)])

    def shift(self, values, step):
        pairs = [(i, (i // 2 + step) % self.depth * 2 + i % 2) for i in range(self.wide)]
        return lax.ppermute(values, "wide", pairs)

    def exchange(self, values, combine):
        for step in (1, 2):
            other = lax.ppermute(values, "narrow", [(i, i ^ step) for i in range(self.narrow)])
            values = combine(values, other)
        step = 1
        while step < self.wide:
            other = lax.ppermute(values, "wide", [(i, i ^ step) for i in range(self.wide)])
            values = combine(values, other)
            step *= 2
        return values

    def total(self, values):
        return self.exchange(values, jnp.add)

    def gather(self, shard, order):
        rows, width = shard.shape
        zero = jnp.zeros((), jnp.int32)
        whole = jnp.zeros((self.depth, 1, 1, 1, rows, width), shard.dtype)
        for step in range(self.depth):
            part = shard if step == 0 else self.shift(shard, step)
            spot = (self.z - step) % self.depth
            whole = lax.dynamic_update_slice(
                whole, part[None, None, None, None], (spot, zero, zero, zero, zero, zero)
            )
        for axis in order:
            dim = " xyc".index(axis)
            other = self.swap(whole, axis)
            shape = list(whole.shape)
            shape[dim] = 2
            both = jnp.zeros(shape, shard.dtype)
            for block, spot in ((whole, self.place[axis]), (other, 1 - self.place[axis])):
                start = [zero] * 6
                start[dim] = spot
                both = lax.dynamic_update_slice(both, block, start)
            whole = both
        return whole.reshape(-1, width)

    def scatter_sum(self, terms, order):
        parts = [
            term.reshape(self.depth, 2, 2, 2, -1, term.shape[-1]) for term in terms
        ]
        widths = [term.shape[-1] for term in terms]
        for axis in order:
            dim = " xyc".index(axis)

            def side(spot):
                picked = [lax.dynamic_slice_in_dim(part, spot, 1, dim) for part in parts]
                return picked[0] if len(picked) == 1 else jnp.concatenate(picked, axis=-1)

            other = self.swap(side(1 - self.place[axis]), axis)
            mine = side(self.place[axis])
            parts = [(mine.astype(f32) + other.astype(f32)).astype(bf16)]
        stacked = parts[0][:, 0, 0, 0]
        summed = lax.dynamic_index_in_dim(stacked, self.z, 0, keepdims=False).astype(f32)
        for step in range(1, self.depth):
            block = lax.dynamic_index_in_dim(
                stacked, (self.z + step) % self.depth, 0, keepdims=False
            )
            summed = summed + self.shift(block, step).astype(f32)
        pieces = []
        start = 0
        for width in widths:
            pieces.append(summed[:, start : start + width])
            start += width
        return pieces


def per_device(
    token_ids,
    doc_ids,
    loss_positions,
    tied_table_master,
    qkv_master,
    out_master,
    up_master,
    down_master,
    norm_master,
    table_first_moment,
    first_qkv,
    first_out,
    first_up,
    first_down,
    first_norms,
    table_second_moment,
    second_qkv,
    second_out,
    second_up,
    second_down,
    second_norms,
):
    links = Links()
    devices = links.wide * links.narrow
    micro_count, unused, length = token_ids.shape
    picked_count = loss_positions.shape[2]
    token_count = micro_count * length
    pick_total = micro_count * picked_count
    model_width = tied_table_master.shape[1]
    head_count = model_width // HEAD_DIM
    block_size = tied_table_master.shape[0]
    count_all = devices * pick_total
    shard_rows = qkv_master.shape[0]

    tokens = token_ids.reshape(token_count)
    picks = loss_positions.reshape(micro_count, picked_count)
    documents = doc_ids.reshape(micro_count, length)
    mean_load = token_count / devices
    slots = int(math.ceil((mean_load + 6.0 * math.sqrt(mean_load)) / 8.0)) * 8
    owner = tokens // block_size
    local_row = tokens % block_size
    token_place = jnp.arange(token_count)
    earlier = (owner[:, None] == owner[None, :]) & (token_place[None, :] < token_place[:, None])
    rank = jnp.sum(earlier.astype(jnp.int32), axis=1)
    most = jnp.max(rank) + 1
    slot_place = jnp.arange(devices * slots)
    line = -(-(slots + 1 + pick_total) // 128) * 128

    pick_hits = picks[:, :, None] == jnp.arange(length)[None, None, :]
    next_hits = picks[:, :, None] + 1 == jnp.arange(length)[None, None, :]
    own_targets = jnp.sum(
        jnp.where(next_hits, token_ids.reshape(micro_count, 1, length), 0), axis=2
    ).reshape(-1)
    pick_docs = jnp.sum(jnp.where(pick_hits, documents[:, None, :], 0), axis=2)

    def slot_of(round_index):
        inside = (rank >= round_index * slots) & (rank < (round_index + 1) * slots)
        return jnp.where(inside, owner * slots + rank - round_index * slots, -1)

    def ask(round_index):
        slot = slot_of(round_index)
        wanted = jnp.sum(
            jnp.where(slot[None, :] == slot_place[:, None], local_row[None, :] + 1, 0), axis=1
        ) - 1
        wanted = wanted.reshape(devices, slots)
        message = jnp.concatenate(
            [
                wanted,
                jnp.broadcast_to(most, (devices, 1)),
                jnp.broadcast_to(own_targets[None, :], (devices, pick_total)),
                jnp.zeros((devices, line - slots - 1 - pick_total), jnp.int32),
            ],
            axis=1,
        )
        answer = lax.all_to_all(message, ("wide", "narrow"), 0, 0, tiled=True)
        asked = answer[:, :slots].reshape(-1)
        return slot, asked, answer

    def fetch(slot, asked):
        row_hits = (asked[:, None] == jnp.arange(block_size)[None, :]).astype(bf16)
        found = matmul(row_hits, table_low).astype(bf16)
        landed = lax.all_to_all(found, ("wide", "narrow"), 0, 0, tiled=True)
        token_hits = (slot[:, None] == slot_place[None, :]).astype(bf16)
        return matmul(token_hits, landed).astype(bf16)

    def give_back(slot, asked, grad_low):
        token_hits = (slot[:, None] == slot_place[None, :]).astype(bf16)
        sent = contract_rows(token_hits, grad_low).astype(bf16)
        landed = lax.all_to_all(sent, ("wide", "narrow"), 0, 0, tiled=True)
        row_hits = (asked[None, :] == jnp.arange(block_size)[:, None]).astype(bf16)
        return matmul(row_hits, landed)

    table_low = tied_table_master.astype(bf16)
    slot_first, asked_first, answer = ask(0)
    rounds = (jnp.max(answer[:, slots]) + slots - 1) // slots
    targets = answer[:, slots + 1 : slots + 1 + pick_total].reshape(-1)

    gain_width = 128
    gain_shard = jnp.pad(norm_master, ((0, 0), (0, gain_width - norm_master.shape[1])))
    first_shard = jnp.concatenate([qkv_master, gain_shard, out_master], axis=1).astype(bf16)
    first_whole = links.gather(first_shard, "xyc")
    up_weight = links.gather(up_master.astype(bf16), "xyc")
    down_weight = links.gather(down_master.astype(bf16), "yxc")
    qkv_width = qkv_master.shape[1]
    qkv_weight = first_whole[:, :qkv_width]
    gain_entries = first_whole[:, qkv_width : qkv_width + 6].astype(f32).T
    out_weight = first_whole[:, qkv_width + gain_width :]

    def more_rows(state):
        round_index, embedded = state
        slot, asked, unused_answer = ask(round_index)
        return (round_index + 1, embedded + fetch(slot, asked))

    unused_round, x_low = lax.while_loop(
        lambda state: state[0] < rounds,
        more_rows,
        (jnp.ones((), jnp.int32), fetch(slot_first, asked_first)),
    )

    x_embed = x_low.astype(f32)
    normed_one = layer_norm(x_embed, gain_entries[0], gain_entries[1]).astype(bf16)
    qkv_all = matmul(normed_one, qkv_weight).astype(bf16)
    pick_rows = (
        pick_hits[:, :, None, :] & jnp.eye(micro_count, dtype=bool)[:, None, :, None]
    ).reshape(pick_total, token_count).astype(bf16)
    picked_both = matmul(
        pick_rows, jnp.concatenate([qkv_all[:, :model_width], x_low], axis=1)
    ).astype(bf16)
    heads_picked = (micro_count, picked_count, head_count, HEAD_DIM)
    heads_all = (micro_count, length, head_count, HEAD_DIM)
    queries = picked_both[:, :model_width].reshape(heads_picked)
    x_embed_picked = picked_both[:, model_width:].astype(f32)
    keys_all = qkv_all[:, model_width : 2 * model_width].reshape(heads_all)
    values_all = qkv_all[:, 2 * model_width :].reshape(heads_all)
    allowed = (jnp.arange(length)[None, None, :] <= picks[:, :, None]) & (
        documents[:, None, :] == pick_docs[:, :, None]
    )
    scale = HEAD_DIM ** (-0.5)
    scores = (
        jnp.einsum("mjhd,muhd->mhju", queries, keys_all, preferred_element_type=f32) * scale
    )
    scores = jnp.where(allowed[:, None], scores, neg_fill)
    exp_scores = jnp.exp(scores - jnp.max(scores, axis=-1, keepdims=True))
    probs = exp_scores / jnp.sum(exp_scores, axis=-1, keepdims=True)
    prob_low = probs.astype(bf16)
    context = (
        jnp.einsum("mhju,muhd->mjhd", prob_low, values_all, preferred_element_type=f32)
        .reshape(pick_total, model_width)
        .astype(bf16)
    )
    x_attn = x_embed_picked + matmul(context, out_weight)
    normed_two = layer_norm(x_attn, gain_entries[2], gain_entries[3]).astype(bf16)
    up_value = matmul(normed_two, up_weight)
    activated = gelu_tanh(up_value).astype(bf16)
    x_out = x_attn + matmul(activated, down_weight)
    picked_low = layer_norm(x_out, gain_entries[4], gain_entries[5]).astype(bf16)

    head_rows = links.gather(picked_low, "xyc")
    columns = links.device * block_size + jnp.arange(block_size)
    logits = contract_cols(head_rows, table_low)
    logits = jnp.where((columns < VOCAB)[None, :], logits, neg_fill)
    target_hits = targets[:, None] == columns[None, :]
    target_sum = jnp.sum(jnp.where(target_hits, logits, 0.0))
    local_top = jnp.max(logits, axis=1)
    local_sum = jnp.sum(jnp.exp(logits - local_top[:, None]), axis=1)

    def merge_totals(first, second):
        top = jnp.maximum(first[0], second[0])
        total = first[1] * jnp.exp(first[0] - top) + second[1] * jnp.exp(second[0] - top)
        return jnp.stack([top, total])

    merged = links.exchange(jnp.stack([local_top, local_sum]), merge_totals)
    log_total = merged[0] + jnp.log(merged[1])
    grad_logits = (
        (jnp.exp(logits - log_total[:, None]) - target_hits.astype(f32)) / count_all
    ).astype(bf16)
    (grad_picked,) = links.scatter_sum([matmul(grad_logits, table_low).astype(bf16)], "cyx")
    table_head = contract_rows(grad_logits, head_rows)

    grad_x_out, gain_last, shift_last = norm_backward(
        x_out, gain_entries[4], gain_entries[5], grad_picked
    )
    grad_mlp = grad_x_out.astype(bf16)
    grad_down = contract_rows(activated, grad_mlp).astype(bf16)
    unused, gelu_pull = jax.vjp(gelu_tanh, up_value)
    grad_up_low = gelu_pull(contract_cols(grad_mlp, down_weight))[0].astype(bf16)
    grad_up = contract_rows(normed_two, grad_up_low).astype(bf16)
    grad_x_attn, gain_two, shift_two = norm_backward(
        x_attn, gain_entries[2], gain_entries[3], contract_cols(grad_up_low, up_weight)
    )
    grad_x_attn = grad_x_out + grad_x_attn
    grad_attn_low = grad_x_attn.astype(bf16)
    grad_out_weight = contract_rows(context, grad_attn_low).astype(bf16)
    grad_context = contract_cols(grad_attn_low, out_weight).astype(bf16).reshape(heads_picked)
    grad_values = jnp.einsum(
        "mhju,mjhd->muhd", prob_low, grad_context, preferred_element_type=f32
    )
    grad_probs = jnp.einsum(
        "mjhd,muhd->mhju", grad_context, values_all, preferred_element_type=f32
    )
    inner = jnp.sum(probs * grad_probs, axis=-1, keepdims=True)
    grad_scores = (probs * (grad_probs - inner)).astype(bf16)
    grad_queries = (
        jnp.einsum("mhju,muhd->mjhd", grad_scores, keys_all, preferred_element_type=f32) * scale
    ).reshape(pick_total, model_width)
    grad_keys = (
        jnp.einsum("mhju,mjhd->muhd", grad_scores, queries, preferred_element_type=f32) * scale
    )
    grad_qkv_low = jnp.concatenate(
        [
            contract_rows(pick_rows, grad_queries.astype(bf16)).astype(bf16),
            grad_keys.reshape(token_count, model_width).astype(bf16),
            grad_values.reshape(token_count, model_width).astype(bf16),
        ],
        axis=1,
    )
    grad_qkv = contract_rows(normed_one, grad_qkv_low).astype(bf16)
    grad_x_one, gain_one, shift_one = norm_backward(
        x_embed, gain_entries[0], gain_entries[1], contract_cols(grad_qkv_low, qkv_weight)
    )
    grad_x_embed = grad_x_one + lax.dot_general(
        pick_rows.astype(f32),
        grad_x_attn,
        (((0,), (0,)), ((), ())),
        precision=lax.Precision.HIGHEST,
        preferred_element_type=f32,
    )
    grad_embed_low = grad_x_embed.astype(bf16)
    (down_grad,) = links.scatter_sum([grad_down], "cyx")
    up_grad, out_grad = links.scatter_sum([grad_up, grad_out_weight], "cxy")
    (qkv_grad,) = links.scatter_sum([grad_qkv], "cyx")
    gain_grads = links.total(
        jnp.stack([gain_one, shift_one, gain_two, shift_two, gain_last, shift_last])
    )
    gain_grad = lax.dynamic_slice_in_dim(gain_grads, links.device * shard_rows, shard_rows, 1).T

    def more_grads(state):
        round_index, earlier_grad = state
        slot, asked, unused_answer = ask(round_index)
        return (round_index + 1, earlier_grad + give_back(slot, asked, grad_embed_low))

    unused_round, table_grad = lax.while_loop(
        lambda state: state[0] < rounds,
        more_grads,
        (
            jnp.ones((), jnp.int32),
            table_head + give_back(slot_first, asked_first, grad_embed_low),
        ),
    )

    all_grads = (table_grad, qkv_grad, out_grad, up_grad, down_grad, gain_grad)
    masters = (tied_table_master, qkv_master, out_master, up_master, down_master, norm_master)
    firsts = (table_first_moment, first_qkv, first_out, first_up, first_down, first_norms)
    seconds = (table_second_moment, second_qkv, second_out, second_up, second_down, second_norms)
    squares = [jnp.sum(gradient * gradient) for gradient in all_grads]
    squares += [jnp.sum(weight * weight) for weight in masters]
    sums = links.total(jnp.stack(squares + [target_sum]).reshape(1, 13))[0]
    grad_total, weight_total, target_total = sums[:6], sums[6:12], sums[12]
    loss_value = (jnp.sum(log_total) - target_total) / count_all
    grad_norm = jnp.sqrt(jnp.sum(grad_total))
    factor = jnp.minimum(1.0, clip_limit / grad_norm)
    new_firsts = []
    new_seconds = []
    directions = []
    for group_index in range(6):
        clipped = factor * all_grads[group_index]
        first_new = beta_first * firsts[group_index] + (1.0 - beta_first) * clipped
        second_new = beta_second * seconds[group_index] + (1.0 - beta_second) * clipped * clipped
        direction = (
            first_new
            / (1.0 - beta_first**step_count)
            / (jnp.sqrt(second_new / (1.0 - beta_second**step_count)) + adam_epsilon)
            + decay_rates[group_index] * masters[group_index]
        )
        new_firsts.append(first_new)
        new_seconds.append(second_new)
        directions.append(direction)
    update_total = links.total(
        jnp.stack([jnp.sum(direction * direction) for direction in directions]).reshape(1, 6)
    )[0]
    weight_norms = jnp.sqrt(weight_total)
    update_norms = jnp.sqrt(update_total)
    new_weights = [
        masters[group_index]
        - learn_rate
        * (weight_norms[group_index] / update_norms[group_index])
        * directions[group_index]
        for group_index in range(6)
    ]
    matrix_norms = jnp.stack([factor * jnp.sqrt(grad_total), weight_norms, update_norms])
    return (
        loss_value,
        grad_norm,
        matrix_norms,
        *new_weights,
        *new_firsts,
        *new_seconds,
    )


def solution(mesh):
    rows = P(("wide", "narrow"), None)
    ids = P(None, ("wide", "narrow"), None)
    return jax.shard_map(
        per_device,
        mesh=mesh,
        in_specs=(ids,) * 3 + (rows,) * 18,
        out_specs=(P(),) * 3 + (rows,) * 18,
        check_vma=False,
    )
```

```python
import math

import jax
import jax.numpy as jnp
from jax import lax
from jax.experimental import pallas as pl
from jax.experimental.pallas import tpu as pltpu
from jax.sharding import PartitionSpec as P

HEAD_DIM = 64
VOCAB = 50257

neg_fill = -1e30
beta_first = 0.9
beta_second = 0.999
adam_epsilon = 1e-12
decay_rates = (0.01, 0.01, 0.01, 0.01, 0.01, 0.0)
learn_rate = 0.5
clip_limit = 0.01
norm_epsilon = 1e-05
step_count = 5.0
bf16 = jnp.bfloat16
f32 = jnp.float32


def layer_norm(values, gain_row, offset):
    centered = values - jnp.mean(values, axis=-1, keepdims=True)
    spread = jnp.mean(centered * centered, axis=-1, keepdims=True)
    return centered * lax.rsqrt(spread + norm_epsilon) * gain_row + offset


def norm_backward(values, gain_row, offset, grad_output):
    unused, pullback = jax.vjp(layer_norm, values, gain_row, offset)
    return pullback(grad_output)


def gelu_tanh(values):
    return jax.nn.gelu(values, approximate=True)


def matmul(left_side, right_side):
    return jnp.dot(left_side, right_side, preferred_element_type=f32)


def contract_rows(left_side, right_side):
    return lax.dot_general(
        left_side, right_side, (((0,), (0,)), ((), ())), preferred_element_type=f32
    )


def contract_cols(left_side, right_side):
    return lax.dot_general(
        left_side, right_side, (((1,), (1,)), ((), ())), preferred_element_type=f32
    )


class Links:
    def __init__(self):
        self.wide = lax.axis_size("wide")
        self.narrow = lax.axis_size("narrow")
        self.depth = self.wide // 2
        wide_place = lax.axis_index("wide")
        narrow_place = lax.axis_index("narrow")
        self.device = wide_place * self.narrow + narrow_place
        self.z = wide_place // 2
        self.place = {"x": wide_place % 2, "y": narrow_place // 2, "c": narrow_place % 2}

    def swap(self, values, axis):
        if axis == "x":
            return lax.ppermute(values, "wide", [(i, i ^ 1) for i in range(self.wide)])
        step = 2 if axis == "y" else 1
        return lax.ppermute(values, "narrow", [(i, i ^ step) for i in range(self.narrow)])

    def cross(self, values, step):
        return lax.ppermute(values, "wide", [(i, i ^ (2 * step)) for i in range(self.wide)])

    def exchange(self, values, combine):
        for step in (1, 2):
            other = lax.ppermute(values, "narrow", [(i, i ^ step) for i in range(self.narrow)])
            values = combine(values, other)
        step = 1
        while step < self.wide:
            other = lax.ppermute(values, "wide", [(i, i ^ step) for i in range(self.wide)])
            values = combine(values, other)
            step *= 2
        return values

    def to_all(self, values):
        return lax.all_to_all(values, ("wide", "narrow"), 0, 0, tiled=True)

    def gather_early(self, shard):
        near = shard[None]
        for step in self.bits()[:0:-1]:
            near = jnp.concatenate([near, self.cross(near, step)])
        return near

    def gather_late(self, near):
        return jnp.concatenate([near, self.cross(near, 1)])

    def gather_depth(self, shard):
        return self.gather_late(self.gather_early(shard))

    def bits(self):
        return [1 << number for number in range(self.depth.bit_length() - 1)]

    def steps(self):
        found = [0]
        for step in self.bits()[::-1]:
            found = found + [number ^ step for number in found]
        return found

    def plane_first(self, near):
        cut = halves(near.shape[-1])
        left, right = near[..., :cut], near[..., cut:]
        return left, right, self.swap(left, "x"), self.swap(right, "y")

    def plane_second(self, left, right, left_x, right_y):
        left, right = jnp.stack([left, left_x]), jnp.stack([right, right_y])
        return [left, self.swap(left, "y"), right, self.swap(right, "x")]

    def plane_core(self, pieces):
        return pieces + [self.swap(piece, "c") for piece in pieces]

    def gather_plane(self, near):
        return self.plane_core(self.plane_second(*self.plane_first(near)))

    def assemble(self, pieces, core_first=False):
        depth = self.depth
        unused, unused_depth, rows, cut = pieces[0].shape
        width = cut + pieces[2].shape[3]

        def kernel(place, *refs):
            sources, target = refs[:-1], refs[-1]
            x, y, c = place[0], place[1], place[2]
            for number, source in enumerate(sources):
                far_core, far, second = number // 4, number % 2, number // 2 % 2
                to_c = 1 - c if far_core else c
                columns = slice(cut, width) if second else slice(0, cut)
                for side in range(2):
                    across_x, across_y = (far, side) if second else (side, far)
                    to_x = 1 - x if across_x else x
                    to_y = 1 - y if across_y else y
                    if core_first:
                        target[to_c, to_x, to_y, 0, :, columns] = source[side, 0]
                    else:
                        target[0, to_x, to_y, to_c, :, columns] = source[side, 0]

        place = [self.place["x"], self.place["y"], self.place["c"]]
        place = jnp.stack(place + [self.z ^ step for step in self.steps()]).astype(jnp.int32)
        if core_first:
            shape = (2, 2, 2, depth, rows, width)
            target_spec = pl.BlockSpec(
                (2, 2, 2, 1, rows, width), lambda k, place: (0, 0, 0, place[3 + k], 0, 0)
            )
        else:
            shape = (depth, 2, 2, 2, rows, width)
            target_spec = pl.BlockSpec(
                (1, 2, 2, 2, rows, width), lambda k, place: (place[3 + k], 0, 0, 0, 0, 0)
            )
        whole = pl.pallas_call(
            kernel,
            out_shape=jax.ShapeDtypeStruct(shape, pieces[0].dtype),
            grid_spec=pltpu.PrefetchScalarGridSpec(
                num_scalar_prefetch=1,
                grid=(depth,),
                in_specs=[
                    pl.BlockSpec((2, 1, rows, piece.shape[3]), lambda k, place: (0, k, 0, 0))
                    for piece in pieces
                ],
                out_specs=target_spec,
            ),
            compiler_params=pltpu.CompilerParams(vmem_limit_bytes=32 * 2**20),
            name="assemble",
        )(place, *pieces)
        return whole.reshape(-1, width)

    def share_first(self, values):
        cut = halves(values.shape[-1])
        left, right = values[:, :cut], values[:, cut:]
        return left, right, self.swap(left, "x"), self.swap(right, "y")

    def share_second(self, left, right, left_x, right_y):
        left, right = jnp.stack([left, left_x]), jnp.stack([right, right_y])
        return left, right, self.swap(left, "y"), self.swap(right, "x")

    def share_last(self, *pieces):
        return list(pieces) + [self.swap(piece, "c") for piece in pieces]

    def scatter_plane(self, full):
        cut = halves(full.shape[-1])
        x, y = self.place["x"], self.place["y"]

        def pick(values, spot, dim):
            return lax.dynamic_index_in_dim(values, spot, dim, keepdims=False)

        left, right = full[..., :cut], full[..., cut:]
        from_x = self.swap(pick(left, 1 - x, 0), "x")
        from_y = self.swap(pick(right, 1 - y, 1), "y")
        left = (pick(left, x, 0).astype(f32) + from_x.astype(f32)).astype(bf16)
        right = (pick(right, y, 1).astype(f32) + from_y.astype(f32)).astype(bf16)
        from_y = self.swap(pick(left, 1 - y, 0), "y")
        from_x = self.swap(pick(right, 1 - x, 0), "x")
        left = pick(left, y, 0).astype(f32) + from_y.astype(f32)
        right = pick(right, x, 0).astype(f32) + from_x.astype(f32)
        return jnp.concatenate([left, right], axis=-1).astype(bf16)

    def scatter_depth(self, near, *before_last):
        for step in self.bits():
            if step == self.bits()[-1]:
                near = after(near, *before_last)
            pairs = near.reshape((-1, 2) + near.shape[1:])
            bit = self.z // step % 2
            other = lax.dynamic_index_in_dim(pairs, 1 - bit, 1, keepdims=False)
            mine = lax.dynamic_index_in_dim(pairs, bit, 1, keepdims=False)
            other = self.cross(other.astype(bf16), step)
            near = mine.astype(f32) + other.astype(f32)
        return near[0]


def halves(width):
    return width // 256 * 128


def tie(*values):
    return lax.optimization_barrier(values)


def after(values, *others):
    return lax.optimization_barrier((values, *others))[0]


def lane_halves(values, first):
    lane = lax.broadcasted_iota(jnp.int32, values.shape, 1)
    return jnp.where((lane < HEAD_DIM) == first, values, jnp.zeros_like(values))


def attend(qkv_all, pick_rows, allowed, micro_count):
    token_count = qkv_all.shape[0]
    width = qkv_all.shape[1] // 3
    pick_total = pick_rows.shape[0]
    length, picked = token_count // micro_count, pick_total // micro_count
    pair = 2 * HEAD_DIM
    scale = HEAD_DIM ** (-0.5)

    def kernel(qkv_ref, pick_ref, allowed_ref, context_ref, query_ref, prob_ref):
        query_ref[...] = jnp.dot(
            pick_ref[...], qkv_ref[:, :width], preferred_element_type=f32
        ).astype(bf16)
        for micro in range(micro_count):
            rows = slice(micro * picked, (micro + 1) * picked)
            keep = allowed_ref[rows] > 0.5
            keep = jnp.concatenate([keep, keep], axis=0)
            for number in range(width // pair):
                columns = slice(number * pair, (number + 1) * pair)
                keys = qkv_ref[
                    micro * length : (micro + 1) * length,
                    width + number * pair : width + (number + 1) * pair,
                ]
                values = qkv_ref[
                    micro * length : (micro + 1) * length,
                    2 * width + number * pair : 2 * width + (number + 1) * pair,
                ]
                query = query_ref[rows, columns]
                both = jnp.concatenate(
                    [lane_halves(query, True), lane_halves(query, False)], axis=0
                )
                scores = contract_cols(both, keys) * scale
                scores = jnp.where(keep, scores, neg_fill)
                shifted = jnp.exp(scores - jnp.max(scores, axis=1, keepdims=True))
                probs = shifted / jnp.sum(shifted, axis=1, keepdims=True)
                prob_ref[micro, number] = probs
                mixed = jnp.dot(probs.astype(bf16), values, preferred_element_type=f32)
                context_ref[rows, columns] = (
                    lane_halves(mixed[:picked], True) + lane_halves(mixed[picked:], False)
                ).astype(bf16)

    return pl.pallas_call(
        kernel,
        out_shape=(
            jax.ShapeDtypeStruct((pick_total, width), bf16),
            jax.ShapeDtypeStruct((pick_total, width), bf16),
            jax.ShapeDtypeStruct((micro_count, width // pair, 2 * picked, length), f32),
        ),
        compiler_params=pltpu.CompilerParams(vmem_limit_bytes=32 * 2**20),
        name="attend",
    )(qkv_all, pick_rows, allowed)


def attend_backward(qkv_all, pick_rows, query_all, probs_all, grad_context, micro_count):
    token_count = qkv_all.shape[0]
    width = qkv_all.shape[1] // 3
    pick_total = pick_rows.shape[0]
    length, picked = token_count // micro_count, pick_total // micro_count
    pair = 2 * HEAD_DIM
    scale = HEAD_DIM ** (-0.5)

    def kernel(qkv_ref, pick_ref, query_ref, prob_ref, grad_ref, out_ref, query_grad_ref):
        for micro in range(micro_count):
            rows = slice(micro * picked, (micro + 1) * picked)
            tokens = slice(micro * length, (micro + 1) * length)
            for number in range(width // pair):
                columns = slice(number * pair, (number + 1) * pair)
                key_columns = slice(width + number * pair, width + (number + 1) * pair)
                value_columns = slice(2 * width + number * pair, 2 * width + (number + 1) * pair)
                query, grad = query_ref[rows, columns], grad_ref[rows, columns]
                queries = jnp.concatenate(
                    [lane_halves(query, True), lane_halves(query, False)], axis=0
                )
                grads = jnp.concatenate(
                    [lane_halves(grad, True), lane_halves(grad, False)], axis=0
                )
                probs = prob_ref[micro, number]
                grad_probs = contract_cols(grads, qkv_ref[tokens, value_columns])
                inner = jnp.sum(probs * grad_probs, axis=1, keepdims=True)
                grad_scores = (probs * (grad_probs - inner)).astype(bf16)
                mixed = (
                    jnp.dot(
                        grad_scores, qkv_ref[tokens, key_columns], preferred_element_type=f32
                    )
                    * scale
                )
                query_grad_ref[rows, columns] = (
                    lane_halves(mixed[:picked], True) + lane_halves(mixed[picked:], False)
                ).astype(bf16)
                out_ref[tokens, key_columns] = (
                    contract_rows(grad_scores, queries) * scale
                ).astype(bf16)
                out_ref[tokens, value_columns] = contract_rows(probs.astype(bf16), grads).astype(
                    bf16
                )
        out_ref[:, :width] = contract_rows(pick_ref[...], query_grad_ref[...]).astype(bf16)

    return pl.pallas_call(
        kernel,
        out_shape=jax.ShapeDtypeStruct(qkv_all.shape, bf16),
        scratch_shapes=[pltpu.VMEM((pick_total, width), bf16)],
        compiler_params=pltpu.CompilerParams(vmem_limit_bytes=32 * 2**20),
        name="attend_backward",
    )(qkv_all, pick_rows, query_all, probs_all, grad_context)


def plane_products(known, grads, place, depth, widths):
    hidden, model = widths
    rows = known[0].shape[-2]
    width = hidden + 2 * model
    down_rows, model_rows = hidden // (8 * depth), model // (8 * depth)

    def kernel(place_ref, *refs):
        pieces, grad_pieces = refs[:8], refs[8:16]
        down_ref, up_ref, out_ref, known_ref, grads_ref, own_ref = refs[16:]
        for parts, target in ((pieces, known_ref), (grad_pieces, grads_ref)):
            cut = parts[0].shape[-1]
            for far_core in range(2):
                left, right, left_y, right_x = parts[4 * far_core : 4 * far_core + 4]
                for x in range(2):
                    for y in range(2):
                        spot = pl.ds(((far_core * 2 + x) * 2 + y) * rows, rows)
                        target[spot, :cut] = (left_y if y else left)[x]
                        target[spot, cut:] = (right_x if x else right)[y]
        place = place_ref[0]

        def own_columns(count, block_rows):
            feature = lax.broadcasted_iota(jnp.int32, (count, depth * block_rows), 0)
            own = lax.broadcasted_iota(jnp.int32, (count, depth * block_rows), 1)
            block, offset = own // block_rows, own % block_rows
            return jnp.where(
                feature == (block * 8 + place) * block_rows + offset, 1.0, 0.0
            ).astype(bf16)

        if down_rows % 128 == 0:
            for z in range(depth):
                start = pl.multiple_of((z * 8 + place) * down_rows, down_rows)
                own_ref[:, z * down_rows : (z + 1) * down_rows] = known_ref[
                    :, pl.ds(start, down_rows)
                ]
        else:
            own_ref[...] = matmul(known_ref[:, :hidden], own_columns(hidden, down_rows)).astype(
                bf16
            )
        chosen = own_columns(model, model_rows)
        down_ref[...] = contract_rows(own_ref[...], grads_ref[:, hidden : hidden + model]).astype(
            bf16
        )
        own_normed = matmul(known_ref[:, hidden : hidden + model], chosen).astype(bf16)
        up_ref[...] = contract_rows(own_normed, grads_ref[:, :hidden]).astype(bf16)
        own_context = matmul(known_ref[:, hidden + model :], chosen).astype(bf16)
        out_ref[...] = contract_rows(own_context, grads_ref[:, hidden + model :]).astype(bf16)

    in_vmem = pl.BlockSpec(memory_space=pltpu.VMEM)
    down, up, out = pl.pallas_call(
        kernel,
        in_specs=[pl.BlockSpec(memory_space=pltpu.SMEM)] + [in_vmem] * 16,
        out_shape=(
            jax.ShapeDtypeStruct((depth * down_rows, model), bf16),
            jax.ShapeDtypeStruct((depth * model_rows, hidden), bf16),
            jax.ShapeDtypeStruct((depth * model_rows, model), bf16),
        ),
        scratch_shapes=[
            pltpu.VMEM((8 * rows, width), bf16),
            pltpu.VMEM((8 * rows, width), bf16),
            pltpu.VMEM((8 * rows, depth * down_rows), bf16),
        ],
        compiler_params=pltpu.CompilerParams(vmem_limit_bytes=48 * 2**20),
        name="plane_products",
    )(place.reshape(1).astype(jnp.int32), *known, *grads)
    return (
        down.reshape(depth, down_rows, model),
        up.reshape(depth, model_rows, hidden),
        out.reshape(depth, model_rows, model),
    )


def on_lane(place, value):
    lane = lax.broadcasted_iota(jnp.int32, (1, 128), 1)
    return jnp.where(lane == place, value, 0.0)


def whole_sum(values):
    return jnp.sum(jnp.sum(values, axis=0, keepdims=True), axis=1, keepdims=True)


def sum_squares(all_grads, weight_row, target_sum, devices):
    def kernel(table_ref, target_ref, weight_ref, *refs):
        grads, rows_ref = refs[:-1], refs[-1]
        row = on_lane(0, table_ref[...])
        for place, grad in enumerate(grads):
            row = row + on_lane(place + 1, whole_sum(grad[...] * grad[...]))
        rows_ref[:, :128] = jnp.broadcast_to(row, (devices, 128))
        rows_ref[:, 128:] = jnp.broadcast_to(
            weight_ref[...] + on_lane(64, target_ref[...]), (devices, 128)
        )

    table_square = jnp.sum(all_grads[0] * all_grads[0]).reshape(1, 1)
    return pl.pallas_call(
        kernel,
        out_shape=jax.ShapeDtypeStruct((devices, 256), f32),
        name="sum_squares",
    )(table_square, target_sum.reshape(1, 1), weight_row, *all_grads[1:])


grid_steps = 8


def group_specs(arrays):
    table_rows = -(-arrays[0].shape[0] // (8 * grid_steps)) * 8
    specs = [pl.BlockSpec((table_rows, arrays[0].shape[1]), lambda k: (k, 0))]
    for array in arrays[1:5]:
        rows, width = array.shape
        specs.append(pl.BlockSpec((rows, width // grid_steps), lambda k: (0, k)))
    specs.append(pl.BlockSpec(arrays[5].shape, lambda k: (0, 0)))
    return specs


def lamb_directions(totals, all_grads, firsts, seconds, masters):
    devices = totals.shape[0]
    table_count = all_grads[0].shape[0]
    specs = group_specs(all_grads)
    table_rows = specs[0].block_shape[0]
    first_scale = 1.0 / (1.0 - beta_first**step_count)
    second_scale = 1.0 / (1.0 - beta_second**step_count)

    def kernel(totals_ref, *refs):
        grads, olds, squares, weights = refs[:6], refs[6:12], refs[12:18], refs[18:24]
        new_olds, new_squares, directions, rows_ref = refs[24:30], refs[30:36], refs[36:42], refs[42]
        step = pl.program_id(0)
        grad_total = jnp.sum(totals_ref[:, :128], axis=0, keepdims=True)
        factor = jnp.minimum(
            1.0, clip_limit * lax.rsqrt(jnp.sum(grad_total, axis=1, keepdims=True))
        )

        @pl.when(step == 0)
        def _():
            rows_ref[...] = jnp.zeros_like(rows_ref)

        def update(group, rows, live=None):
            clipped = factor * grads[group][rows]
            new_old = beta_first * olds[group][rows] + (1.0 - beta_first) * clipped
            new_square = beta_second * squares[group][rows] + (1.0 - beta_second) * clipped * clipped
            direction = (new_old * first_scale) / (
                jnp.sqrt(new_square * second_scale) + adam_epsilon
            ) + decay_rates[group] * weights[group][rows]
            new_olds[group][rows] = new_old
            new_squares[group][rows] = new_square
            directions[group][rows] = direction
            square = direction * direction
            return square if live is None else jnp.where(live, square, 0.0)

        def table_part(part, total):
            rows = pl.ds(pl.multiple_of(part * 8, 8), 8)
            place = step * table_rows + part * 8 + lax.broadcasted_iota(
                jnp.int32, (8, 1), 0
            )
            return total + update(0, (rows, slice(None)), place < table_count)

        table_total = lax.fori_loop(
            0, table_rows // 8, table_part, jnp.zeros((8, all_grads[0].shape[1]), f32)
        )
        row = on_lane(0, whole_sum(table_total))
        for group in range(1, 5):
            row = row + on_lane(group, whole_sum(update(group, (slice(None), slice(None)))))
        rows_ref[...] += jnp.broadcast_to(row, rows_ref.shape)

        @pl.when(step == 0)
        def _():
            row = on_lane(5, whole_sum(update(5, (slice(None), slice(None)))))
            rows_ref[...] += jnp.broadcast_to(row, rows_ref.shape)

    shapes = [jax.ShapeDtypeStruct(array.shape, f32) for array in all_grads]
    results = pl.pallas_call(
        kernel,
        grid=(grid_steps,),
        in_specs=[pl.BlockSpec(totals.shape, lambda k: (0, 0))] + specs * 4,
        out_specs=specs * 3 + [pl.BlockSpec((devices, 128), lambda k: (0, 0))],
        out_shape=shapes * 3 + [jax.ShapeDtypeStruct((devices, 128), f32)],
        compiler_params=pltpu.CompilerParams(vmem_limit_bytes=56 * 2**20),
        name="lamb_directions",
    )(totals, *all_grads, *firsts, *seconds, *masters)
    return results[:6], results[6:12], results[12:18], results[18]


def lamb_weights(totals, update_rows, directions, masters):
    specs = group_specs(masters)

    def kernel(totals_ref, updates_ref, *refs):
        moves, weights, news, facts_ref = refs[:6], refs[6:12], refs[12:18], refs[18]
        step = pl.program_id(0)
        lane = lax.broadcasted_iota(jnp.int32, (1, 128), 1)
        grad_total = jnp.sum(totals_ref[:, :128], axis=0, keepdims=True)
        weight_total = jnp.sum(totals_ref[:, 128:], axis=0, keepdims=True)
        update_total = jnp.sum(updates_ref[...], axis=0, keepdims=True)
        weight_norms = jnp.where(lane < 6, jnp.sqrt(jnp.maximum(weight_total, 0.0)), 0.0)
        update_norms = jnp.where(lane < 6, jnp.sqrt(update_total), 1.0)
        rates = learn_rate * weight_norms / update_norms
        for group in range(5):
            rate = jnp.sum(jnp.where(lane == group, rates, 0.0), axis=1, keepdims=True)
            news[group][...] = weights[group][...] - rate * moves[group][...]

        @pl.when(step == 0)
        def _():
            rate = jnp.sum(jnp.where(lane == 5, rates, 0.0), axis=1, keepdims=True)
            news[5][...] = weights[5][...] - rate * moves[5][...]
            grad_norm = jnp.sqrt(jnp.sum(grad_total, axis=1, keepdims=True))
            factor = jnp.minimum(1.0, clip_limit / grad_norm)
            target = jnp.sum(jnp.where(lane == 64, weight_total, 0.0), axis=1, keepdims=True)
            facts_ref[0:1] = factor * jnp.sqrt(grad_total)
            facts_ref[1:2] = weight_norms
            facts_ref[2:3] = update_norms
            facts_ref[3:4] = jnp.broadcast_to(grad_norm, (1, 128))
            facts_ref[4:5] = jnp.broadcast_to(target, (1, 128))

    results = pl.pallas_call(
        kernel,
        grid=(grid_steps,),
        in_specs=[
            pl.BlockSpec(totals.shape, lambda k: (0, 0)),
            pl.BlockSpec(update_rows.shape, lambda k: (0, 0)),
        ]
        + specs * 2,
        out_specs=specs + [pl.BlockSpec((8, 128), lambda k: (0, 0))],
        out_shape=[jax.ShapeDtypeStruct(array.shape, f32) for array in masters]
        + [jax.ShapeDtypeStruct((8, 128), f32)],
        compiler_params=pltpu.CompilerParams(vmem_limit_bytes=56 * 2**20),
        name="lamb_weights",
    )(totals, update_rows, *directions, *masters)
    return results[:6], results[6]


def per_device(
    token_ids,
    doc_ids,
    loss_positions,
    tied_table_master,
    qkv_master,
    out_master,
    up_master,
    down_master,
    norm_master,
    table_first_moment,
    first_qkv,
    first_out,
    first_up,
    first_down,
    first_norms,
    table_second_moment,
    second_qkv,
    second_out,
    second_up,
    second_down,
    second_norms,
):
    links = Links()
    devices = links.wide * links.narrow
    micro_count, unused, length = token_ids.shape
    picked_count = loss_positions.shape[2]
    token_count = micro_count * length
    pick_total = micro_count * picked_count
    model_width = tied_table_master.shape[1]
    head_count = model_width // HEAD_DIM
    block_size = tied_table_master.shape[0]
    count_all = devices * pick_total
    shard_rows = qkv_master.shape[0]

    tokens = token_ids.reshape(token_count)
    picks = loss_positions.reshape(micro_count, picked_count)
    documents = doc_ids.reshape(micro_count, length)
    mean_load = token_count / devices
    slots = int(math.ceil((mean_load + 6.0 * math.sqrt(mean_load)) / 8.0)) * 8
    owner = tokens // block_size
    local_row = tokens % block_size
    token_place = jnp.arange(token_count)
    earlier = (owner[:, None] == owner[None, :]) & (token_place[None, :] < token_place[:, None])
    rank = jnp.sum(earlier.astype(jnp.int32), axis=1)
    most = jnp.max(rank) + 1
    slot_place = jnp.arange(devices * slots)
    line = -(-(slots + 1 + pick_total) // 128) * 128

    pick_hits = picks[:, :, None] == jnp.arange(length)[None, None, :]
    next_hits = picks[:, :, None] + 1 == jnp.arange(length)[None, None, :]
    own_targets = jnp.sum(
        jnp.where(next_hits, token_ids.reshape(micro_count, 1, length), 0), axis=2
    ).reshape(-1)
    pick_docs = jnp.sum(jnp.where(pick_hits, documents[:, None, :], 0), axis=2)

    def slot_of(round_index):
        inside = (rank >= round_index * slots) & (rank < (round_index + 1) * slots)
        return jnp.where(inside, owner * slots + rank - round_index * slots, -1)

    def message_of(slot):
        wanted = jnp.sum(
            jnp.where(slot[None, :] == slot_place[:, None], local_row[None, :] + 1, 0), axis=1
        ) - 1
        wanted = wanted.reshape(devices, slots)
        return jnp.concatenate(
            [
                wanted,
                jnp.broadcast_to(most, (devices, 1)),
                jnp.broadcast_to(own_targets[None, :], (devices, pick_total)),
                jnp.zeros((devices, line - slots - 1 - pick_total), jnp.int32),
            ],
            axis=1,
        )

    def ask(round_index):
        slot = slot_of(round_index)
        return slot, links.to_all(message_of(slot))[:, :slots].reshape(-1)

    def find(asked):
        row_hits = (asked[:, None] == jnp.arange(block_size)[None, :]).astype(bf16)
        return matmul(row_hits, table_low).astype(bf16)

    def place_rows(slot, landed):
        token_hits = (slot[:, None] == slot_place[None, :]).astype(bf16)
        return matmul(token_hits, landed).astype(bf16)

    def give(slot, grad_low):
        token_hits = (slot[:, None] == slot_place[None, :]).astype(bf16)
        return contract_rows(token_hits, grad_low).astype(bf16)

    def take(asked, landed):
        row_hits = (asked[None, :] == jnp.arange(block_size)[:, None]).astype(bf16)
        return matmul(row_hits, landed)

    gain_width = 128
    qkv_width = qkv_master.shape[1]
    gain_shard = jnp.pad(norm_master, ((0, 0), (0, gain_width - norm_master.shape[1])))
    first_shard = jnp.concatenate([qkv_master, gain_shard], axis=1).astype(bf16)
    first_early = links.gather_early(first_shard)
    first_near = links.gather_late(first_early)
    slot_first = slot_of(0)
    masters = (tied_table_master, qkv_master, out_master, up_master, down_master, norm_master)
    message = message_of(slot_first)
    answer = links.to_all(message)
    second_shard = jnp.concatenate([up_master, out_master], axis=1)
    second_near = links.gather_early(after(second_shard, first_early).astype(bf16))
    down_near = links.gather_early(after(down_master, first_early).astype(bf16))
    table_low = after(tied_table_master, message).astype(bf16)
    asked_first = answer[:, :slots].reshape(-1)
    found = after(find(asked_first), first_near, second_near, down_near)
    landed = links.to_all(found)
    rounds = (jnp.max(answer[:, slots]) + slots - 1) // slots
    targets = answer[:, slots + 1 : slots + 1 + pick_total]
    targets = targets.reshape(links.depth, 2, 2, 2, pick_total).transpose(3, 1, 2, 0, 4).reshape(-1)
    first_whole = links.assemble(links.gather_plane(first_near))
    second_near = links.gather_late(second_near)
    second_parts = links.plane_first(after(second_near, first_whole))
    weight_row = sum(
        on_lane(place, after(jnp.sum(weight * weight), found))
        for place, weight in enumerate(masters)
    )
    qkv_weight = first_whole[:, :qkv_width]
    gain_entries = first_whole[:, qkv_width : qkv_width + 6].astype(f32).T

    def more_rows(state):
        round_index, embedded = state
        slot, asked = ask(round_index)
        return (round_index + 1, embedded + place_rows(slot, links.to_all(find(asked))))

    unused_round, x_low = lax.while_loop(
        lambda state: state[0] < rounds,
        more_rows,
        (jnp.ones((), jnp.int32), place_rows(slot_first, landed)),
    )

    x_embed = x_low.astype(f32)
    normed_one = layer_norm(x_embed, gain_entries[0], gain_entries[1]).astype(bf16)
    second_pieces = links.plane_second(*second_parts)
    down_parts = links.plane_first(links.gather_late(after(down_near, normed_one)))
    qkv_all = matmul(normed_one, qkv_weight).astype(bf16)
    pick_rows = (
        pick_hits[:, :, None, :] & jnp.eye(micro_count, dtype=bool)[:, None, :, None]
    ).reshape(pick_total, token_count).astype(bf16)
    x_embed_picked = matmul(pick_rows, x_low)
    allowed = (jnp.arange(length)[None, None, :] <= picks[:, :, None]) & (
        documents[:, None, :] == pick_docs[:, :, None]
    )
    context, queries, probs = attend(
        qkv_all, pick_rows, allowed.reshape(pick_total, length).astype(f32), micro_count
    )
    second_whole = links.assemble(
        links.plane_core([after(piece, context) for piece in second_pieces])
    )
    hidden = up_master.shape[1]
    up_weight, out_weight = second_whole[:, :hidden], second_whole[:, hidden:]
    down_pieces = links.plane_second(*[after(part, context) for part in down_parts])
    down_weight = links.assemble(links.plane_core(down_pieces))
    x_attn = x_embed_picked + matmul(context, out_weight)
    normed_two = layer_norm(x_attn, gain_entries[2], gain_entries[3]).astype(bf16)
    up_value = matmul(normed_two, up_weight)
    activated = gelu_tanh(up_value).astype(bf16)
    x_out = x_attn + matmul(activated, down_weight)
    picked_low = layer_norm(x_out, gain_entries[4], gain_entries[5]).astype(bf16)

    head_rows = links.assemble(
        links.gather_plane(links.gather_depth(picked_low)), core_first=True
    )
    columns = links.device * block_size + jnp.arange(block_size)
    logits = contract_cols(head_rows, table_low)
    logits = jnp.where((columns < VOCAB)[None, :], logits, neg_fill)
    target_hits = targets[:, None] == columns[None, :]
    target_sum = jnp.sum(jnp.where(target_hits, logits, 0.0))
    local_top = jnp.max(logits, axis=1)
    local_sum = jnp.sum(jnp.exp(logits - local_top[:, None]), axis=1)

    def merge_totals(first, second):
        top = jnp.maximum(first[0], second[0])
        total = first[1] * jnp.exp(first[0] - top) + second[1] * jnp.exp(second[0] - top)
        return jnp.stack([top, total])

    known = jnp.concatenate([activated, normed_two, context], axis=1)
    known, head_rows = tie(known, head_rows)
    known_parts = links.share_first(known)
    local_sum, *known_parts = tie(local_sum, *known_parts)
    known_parts = links.share_second(*known_parts)
    merged = links.exchange(jnp.stack([local_top, local_sum]), merge_totals)
    log_total = merged[0] + jnp.log(merged[1])
    grad_logits = (
        (jnp.exp(logits - log_total[:, None]) - target_hits.astype(f32)) / count_all
    ).astype(bf16)
    half_rows = head_rows.shape[0] // 2
    core = links.place["c"]

    def picked_part(spot):
        part = lax.dynamic_slice_in_dim(grad_logits, spot * half_rows, half_rows, 0)
        return matmul(part, table_low)

    to_core = picked_part(1 - core).astype(bf16)
    to_core, grad_logits = tie(to_core, grad_logits)
    from_core = links.swap(to_core, "c")
    grad_near = links.scatter_plane(
        (picked_part(core) + from_core.astype(f32))
        .astype(bf16)
        .reshape(2, 2, links.depth, pick_total, model_width)
    )
    grad_near, grad_logits = tie(grad_near, grad_logits)
    table_head = contract_rows(grad_logits, head_rows)
    known = links.share_last(*[after(part, grad_near) for part in known_parts])
    grad_picked = links.scatter_depth(grad_near)

    grad_x_out, gain_last, shift_last = norm_backward(
        x_out, gain_entries[4], gain_entries[5], grad_picked
    )
    grad_mlp = grad_x_out.astype(bf16)
    unused, gelu_pull = jax.vjp(gelu_tanh, up_value)
    grad_up_low = gelu_pull(contract_cols(grad_mlp, down_weight))[0].astype(bf16)
    grad_x_attn, gain_two, shift_two = norm_backward(
        x_attn, gain_entries[2], gain_entries[3], contract_cols(grad_up_low, up_weight)
    )
    grad_x_attn = grad_x_out + grad_x_attn
    grad_attn_low = grad_x_attn.astype(bf16)
    grad_context = contract_cols(grad_attn_low, out_weight).astype(bf16)
    grad_parts = links.share_first(
        jnp.concatenate([grad_up_low, grad_mlp, grad_attn_low], axis=1)
    )
    grad_qkv_low = attend_backward(
        qkv_all, pick_rows, queries, probs, grad_context, micro_count
    )
    late = after(grad_qkv_low, *grad_parts)
    grad_parts = links.share_second(*grad_parts)
    grad_x_one, gain_one, shift_one = norm_backward(
        x_embed, gain_entries[0], gain_entries[1], contract_cols(late, qkv_weight)
    )
    grad_x_embed = grad_x_one + lax.dot_general(
        pick_rows.astype(f32),
        grad_x_attn,
        (((0,), (0,)), ((), ())),
        precision=lax.Precision.HIGHEST,
        preferred_element_type=f32,
    )
    grad_embed_low = grad_x_embed.astype(bf16)
    sent = give(slot_first, grad_embed_low)
    grad_qkv_low = after(grad_qkv_low, sent)
    returned = links.to_all(sent)
    down_near, up_near, out_near = plane_products(
        known,
        links.share_last(*[after(part, sent) for part in grad_parts]),
        (links.place["x"] * 2 + links.place["y"]) * 2 + core,
        links.depth,
        (activated.shape[1], model_width),
    )

    half_place = jnp.arange(model_width // 2)
    half_row = half_place % shard_rows
    half_z = half_place // shard_rows % links.depth
    half_plane = half_place // shard_rows // links.depth

    def qkv_part(spot):
        source = ((half_z * 4 + half_plane) * 2 + spot) * shard_rows + half_row
        columns = (jnp.arange(model_width)[:, None] == source[None, :]).astype(bf16)
        return contract_rows(matmul(normed_one, columns).astype(bf16), grad_qkv_low)

    to_core = qkv_part(1 - core).astype(bf16)
    from_core = links.swap(to_core, "c")
    last_near = links.scatter_plane(
        (qkv_part(core) + from_core.astype(f32))
        .astype(bf16)
        .reshape(2, 2, links.depth, shard_rows, qkv_width)
    )
    last_near = jnp.concatenate([last_near, out_near], axis=-1)
    down_grad = links.scatter_depth(down_near, returned)
    up_grad = links.scatter_depth(up_near, returned)
    last_grad = links.scatter_depth(after(last_near, returned))
    qkv_grad, out_grad = last_grad[:, :qkv_width], last_grad[:, qkv_width:]
    gain_grads = jnp.stack(
        [gain_one, shift_one, gain_two, shift_two, gain_last, shift_last]
    ).reshape(6, devices, shard_rows)
    gain_grads = jnp.pad(
        gain_grads.transpose(1, 0, 2).reshape(devices, 6 * shard_rows),
        ((0, 0), (0, -6 * shard_rows % 128)),
    )
    gain_grad = jnp.sum(links.to_all(after(gain_grads, returned)), axis=0)[: 6 * shard_rows]
    gain_grad = gain_grad.reshape(6, shard_rows).T

    def more_grads(state):
        round_index, earlier_grad = state
        slot, asked = ask(round_index)
        returned_rows = links.to_all(give(slot, grad_embed_low))
        return (round_index + 1, earlier_grad + take(asked, returned_rows))

    unused_round, table_grad = lax.while_loop(
        lambda state: state[0] < rounds,
        more_grads,
        (
            jnp.ones((), jnp.int32),
            table_head + take(asked_first, returned),
        ),
    )

    all_grads = (table_grad, qkv_grad, out_grad, up_grad, down_grad, gain_grad)
    firsts = (table_first_moment, first_qkv, first_out, first_up, first_down, first_norms)
    seconds = (table_second_moment, second_qkv, second_out, second_up, second_down, second_norms)
    totals = links.to_all(sum_squares(all_grads, weight_row, target_sum, devices))
    new_firsts, new_seconds, directions, update_rows = lamb_directions(
        totals, all_grads, firsts, seconds, masters
    )
    new_weights, facts = lamb_weights(totals, links.to_all(update_rows), directions, masters)
    return (
        (jnp.sum(log_total) - facts[4, 0]) / count_all,
        facts[3, 0],
        facts[:3, :6],
        *new_weights,
        *new_firsts,
        *new_seconds,
    )


def solution(mesh):
    rows = P(("wide", "narrow"), None)
    ids = P(None, ("wide", "narrow"), None)
    return jax.shard_map(
        per_device,
        mesh=mesh,
        in_specs=(ids,) * 3 + (rows,) * 18,
        out_specs=(P(),) * 3 + (rows,) * 18,
        check_vma=False,
    )
```

```python
import math

import jax
import jax.numpy as jnp
from jax import lax
from jax.experimental import pallas as pl
from jax.experimental.pallas import tpu as pltpu
from jax.sharding import PartitionSpec as P

HEAD_DIM = 64
VOCAB = 50257

neg_fill = -1e30
beta_first = 0.9
beta_second = 0.999
adam_epsilon = 1e-12
decay_rates = (0.01, 0.01, 0.01, 0.01, 0.01, 0.0)
learn_rate = 0.5
clip_limit = 0.01
norm_epsilon = 1e-05
step_count = 5.0
bf16 = jnp.bfloat16
f32 = jnp.float32


def layer_norm(values, gain_row, offset):
    centered = values - jnp.mean(values, axis=-1, keepdims=True)
    spread = jnp.mean(centered * centered, axis=-1, keepdims=True)
    return centered * lax.rsqrt(spread + norm_epsilon) * gain_row + offset


def norm_backward(values, gain_row, offset, grad_output):
    unused, pullback = jax.vjp(layer_norm, values, gain_row, offset)
    return pullback(grad_output)


def gelu_tanh(values):
    return jax.nn.gelu(values, approximate=True)


def matmul(left_side, right_side):
    return jnp.dot(left_side, right_side, preferred_element_type=f32)


def contract_rows(left_side, right_side):
    return lax.dot_general(
        left_side, right_side, (((0,), (0,)), ((), ())), preferred_element_type=f32
    )


def contract_cols(left_side, right_side):
    return lax.dot_general(
        left_side, right_side, (((1,), (1,)), ((), ())), preferred_element_type=f32
    )


class Links:
    def __init__(self):
        self.wide = lax.axis_size("wide")
        self.narrow = lax.axis_size("narrow")
        self.depth = self.wide // 2
        wide_place = lax.axis_index("wide")
        narrow_place = lax.axis_index("narrow")
        self.device = wide_place * self.narrow + narrow_place
        self.z = wide_place // 2
        self.place = {"x": wide_place % 2, "y": narrow_place // 2, "c": narrow_place % 2}

    def swap(self, values, axis):
        if axis == "x":
            return lax.ppermute(values, "wide", [(i, i ^ 1) for i in range(self.wide)])
        step = 2 if axis == "y" else 1
        return lax.ppermute(values, "narrow", [(i, i ^ step) for i in range(self.narrow)])

    def cross(self, values, step):
        return lax.ppermute(values, "wide", [(i, i ^ (2 * step)) for i in range(self.wide)])

    def exchange(self, values, combine):
        for step in (1, 2):
            other = lax.ppermute(values, "narrow", [(i, i ^ step) for i in range(self.narrow)])
            values = combine(values, other)
        step = 1
        while step < self.wide:
            other = lax.ppermute(values, "wide", [(i, i ^ step) for i in range(self.wide)])
            values = combine(values, other)
            step *= 2
        return values

    def to_all(self, values):
        return lax.all_to_all(values, ("wide", "narrow"), 0, 0, tiled=True)

    def gather_early(self, shard, *before):
        near = shard[None]
        for step in self.bits()[:0:-1]:
            near = jnp.concatenate([near, after(self.cross(near, step), *before)])
        return near

    def gather_late(self, near):
        return jnp.concatenate([near, self.cross(near, 1)])

    def gather_depth(self, shard):
        return self.gather_late(self.gather_early(shard))

    def bits(self):
        return [1 << number for number in range(self.depth.bit_length() - 1)]

    def steps(self):
        found = [0]
        for step in self.bits()[::-1]:
            found = found + [number ^ step for number in found]
        return found

    def plane_first(self, near):
        cut = halves(near.shape[-1])
        left, right = near[..., :cut], near[..., cut:]
        return left, right, self.swap(left, "x"), self.swap(right, "y")

    def plane_second(self, left, right, left_x, right_y):
        left, right = jnp.stack([left, left_x]), jnp.stack([right, right_y])
        return [left, self.swap(left, "y"), right, self.swap(right, "x")]

    def plane_core(self, pieces):
        return pieces + [self.swap(piece, "c") for piece in pieces]

    def gather_plane(self, near):
        return self.plane_core(self.plane_second(*self.plane_first(near)))

    def assemble(self, pieces, core_first=False, folded=None):
        depth = self.depth
        unused, unused_depth, rows, cut = pieces[0].shape
        count, fold = folded or (0, 0)
        width = cut + pieces[2].shape[3] - count * fold

        def kernel(place, *refs):
            sources, target = refs[: len(pieces)], refs[len(pieces)]
            x, y, c = place[0], place[1], place[2]
            for number, source in enumerate(sources):
                far_core, far, second = number // 4, number % 2, number // 2 % 2
                to_c = 1 - c if far_core else c
                columns = slice(cut, width) if second else slice(0, cut)
                for side in range(2):
                    across_x, across_y = (far, side) if second else (side, far)
                    to_x = 1 - x if across_x else x
                    to_y = 1 - y if across_y else y
                    if core_first:
                        target[to_c, to_x, to_y, 0, :, columns] = source[side, 0]
                    elif second:
                        target[0, to_x, to_y, to_c, :, columns] = source[side, 0, :, : width - cut]
                        for number_in in range(count):
                            start = width - cut + number_in * fold
                            refs[-1][
                                0, to_x, to_y, to_c, number_in * rows : (number_in + 1) * rows
                            ] = source[side, 0, :, start : start + fold]
                    else:
                        target[0, to_x, to_y, to_c, :, columns] = source[side, 0]

        place = [self.place["x"], self.place["y"], self.place["c"]]
        place = jnp.stack(place + [self.z ^ step for step in self.steps()]).astype(jnp.int32)
        if core_first:
            shape = (2, 2, 2, depth, rows, width)
            target_spec = pl.BlockSpec(
                (2, 2, 2, 1, rows, width), lambda k, place: (0, 0, 0, place[3 + k], 0, 0)
            )
        else:
            shape = (depth, 2, 2, 2, rows, width)
            target_spec = pl.BlockSpec(
                (1, 2, 2, 2, rows, width), lambda k, place: (place[3 + k], 0, 0, 0, 0, 0)
            )
        shapes, target_specs = [jax.ShapeDtypeStruct(shape, pieces[0].dtype)], [target_spec]
        if count:
            shapes.append(
                jax.ShapeDtypeStruct((depth, 2, 2, 2, count * rows, fold), pieces[0].dtype)
            )
            target_specs.append(
                pl.BlockSpec(
                    (1, 2, 2, 2, count * rows, fold),
                    lambda k, place: (place[3 + k], 0, 0, 0, 0, 0),
                )
            )
        wholes = pl.pallas_call(
            kernel,
            out_shape=shapes,
            grid_spec=pltpu.PrefetchScalarGridSpec(
                num_scalar_prefetch=1,
                grid=(depth,),
                in_specs=[
                    pl.BlockSpec((2, 1, rows, piece.shape[3]), lambda k, place: (0, k, 0, 0))
                    for piece in pieces
                ],
                out_specs=target_specs,
            ),
            compiler_params=pltpu.CompilerParams(vmem_limit_bytes=40 * 2**20),
            name="assemble",
        )(place, *pieces)
        wholes = [whole.reshape(-1, whole.shape[-1]) for whole in wholes]
        return wholes if count else wholes[0]

    def exchange_plane(self, values):
        for axis in "xyc":
            dim = " xyc".index(axis) - 1
            mine = lax.dynamic_index_in_dim(values, self.place[axis], dim, keepdims=False)
            other = lax.dynamic_index_in_dim(values, 1 - self.place[axis], dim, keepdims=False)
            values = jnp.stack([mine, self.swap(other, axis)], axis=dim)
        return values.transpose(2, 0, 1, 3, 4).reshape(-1, values.shape[-1])

    def share_direct(self, values):
        pairs = []
        for wide in range(self.wide):
            for narrow in range(self.narrow):
                pairs.append((wide * self.narrow + narrow, (wide ^ 1) * self.narrow + (narrow ^ 2)))
        across = lax.ppermute(values, ("wide", "narrow"), pairs)
        return [values, self.swap(values, "y"), self.swap(values, "x"), across]

    def share_first(self, values):
        cut = halves(values.shape[-1])
        left, right = values[:, :cut], values[:, cut:]
        return left, right, self.swap(left, "x"), self.swap(right, "y")

    def share_second(self, left, right, left_x, right_y):
        left, right = jnp.stack([left, left_x]), jnp.stack([right, right_y])
        return left, right, self.swap(left, "y"), self.swap(right, "x")

    def share_last(self, *pieces):
        return list(pieces) + [self.swap(piece, "c") for piece in pieces]

    def scatter_plane(self, full, *before_second):
        cut = halves(full.shape[-1])
        x, y = self.place["x"], self.place["y"]

        def pick(values, spot, dim):
            return lax.dynamic_index_in_dim(values, spot, dim, keepdims=False)

        left, right = full[..., :cut], full[..., cut:]
        from_x = self.swap(pick(left, 1 - x, 0), "x")
        from_y = self.swap(pick(right, 1 - y, 1), "y")
        left = (pick(left, x, 0).astype(f32) + from_x.astype(f32)).astype(bf16)
        right = (pick(right, y, 1).astype(f32) + from_y.astype(f32)).astype(bf16)
        left, right = after(left, *before_second), after(right, *before_second)
        from_y = self.swap(pick(left, 1 - y, 0), "y")
        from_x = self.swap(pick(right, 1 - x, 0), "x")
        left = pick(left, y, 0).astype(f32) + from_y.astype(f32)
        right = pick(right, x, 0).astype(f32) + from_x.astype(f32)
        return jnp.concatenate([left, right], axis=-1).astype(bf16)

    def scatter_depth(self, near, *before_last):
        for step in self.bits():
            if step == self.bits()[-1]:
                near = after(near, *before_last)
            pairs = near.reshape((-1, 2) + near.shape[1:])
            bit = self.z // step % 2
            other = lax.dynamic_index_in_dim(pairs, 1 - bit, 1, keepdims=False)
            mine = lax.dynamic_index_in_dim(pairs, bit, 1, keepdims=False)
            other = self.cross(other.astype(bf16), step)
            near = mine.astype(f32) + other.astype(f32)
        return near[0]


def halves(width):
    return width // 256 * 128


def tie(*values):
    return lax.optimization_barrier(values)


def after(values, *others):
    return lax.optimization_barrier((values, *others))[0]


def lane_halves(values, first):
    lane = lax.broadcasted_iota(jnp.int32, values.shape, 1)
    return jnp.where((lane < HEAD_DIM) == first, values, jnp.zeros_like(values))


def attend(qkv_all, pick_rows, allowed, micro_count):
    token_count = qkv_all.shape[0]
    width = qkv_all.shape[1] // 3
    pick_total = pick_rows.shape[0]
    length, picked = token_count // micro_count, pick_total // micro_count
    pair = 2 * HEAD_DIM
    scale = HEAD_DIM ** (-0.5)

    def kernel(qkv_ref, pick_ref, allowed_ref, context_ref, query_ref, prob_ref):
        query_ref[...] = jnp.dot(
            pick_ref[...], qkv_ref[:, :width], preferred_element_type=f32
        ).astype(bf16)
        for micro in range(micro_count):
            rows = slice(micro * picked, (micro + 1) * picked)
            keep = allowed_ref[rows] > 0.5
            keep = jnp.concatenate([keep, keep], axis=0)
            for number in range(width // pair):
                columns = slice(number * pair, (number + 1) * pair)
                keys = qkv_ref[
                    micro * length : (micro + 1) * length,
                    width + number * pair : width + (number + 1) * pair,
                ]
                values = qkv_ref[
                    micro * length : (micro + 1) * length,
                    2 * width + number * pair : 2 * width + (number + 1) * pair,
                ]
                query = query_ref[rows, columns]
                both = jnp.concatenate(
                    [lane_halves(query, True), lane_halves(query, False)], axis=0
                )
                scores = contract_cols(both, keys) * scale
                scores = jnp.where(keep, scores, neg_fill)
                shifted = jnp.exp(scores - jnp.max(scores, axis=1, keepdims=True))
                probs = shifted / jnp.sum(shifted, axis=1, keepdims=True)
                prob_ref[micro, number] = probs
                mixed = jnp.dot(probs.astype(bf16), values, preferred_element_type=f32)
                context_ref[rows, columns] = (
                    lane_halves(mixed[:picked], True) + lane_halves(mixed[picked:], False)
                ).astype(bf16)

    return pl.pallas_call(
        kernel,
        out_shape=(
            jax.ShapeDtypeStruct((pick_total, width), bf16),
            jax.ShapeDtypeStruct((pick_total, width), bf16),
            jax.ShapeDtypeStruct((micro_count, width // pair, 2 * picked, length), f32),
        ),
        compiler_params=pltpu.CompilerParams(vmem_limit_bytes=32 * 2**20),
        name="attend",
    )(qkv_all, pick_rows, allowed)


def attend_backward(qkv_all, pick_rows, query_all, probs_all, grad_context, micro_count):
    token_count = qkv_all.shape[0]
    width = qkv_all.shape[1] // 3
    pick_total = pick_rows.shape[0]
    length, picked = token_count // micro_count, pick_total // micro_count
    pair = 2 * HEAD_DIM
    scale = HEAD_DIM ** (-0.5)

    def kernel(qkv_ref, pick_ref, query_ref, prob_ref, grad_ref, out_ref, query_grad_ref):
        for micro in range(micro_count):
            rows = slice(micro * picked, (micro + 1) * picked)
            tokens = slice(micro * length, (micro + 1) * length)
            for number in range(width // pair):
                columns = slice(number * pair, (number + 1) * pair)
                key_columns = slice(width + number * pair, width + (number + 1) * pair)
                value_columns = slice(2 * width + number * pair, 2 * width + (number + 1) * pair)
                query, grad = query_ref[rows, columns], grad_ref[rows, columns]
                queries = jnp.concatenate(
                    [lane_halves(query, True), lane_halves(query, False)], axis=0
                )
                grads = jnp.concatenate(
                    [lane_halves(grad, True), lane_halves(grad, False)], axis=0
                )
                probs = prob_ref[micro, number]
                grad_probs = contract_cols(grads, qkv_ref[tokens, value_columns])
                inner = jnp.sum(probs * grad_probs, axis=1, keepdims=True)
                grad_scores = (probs * (grad_probs - inner)).astype(bf16)
                mixed = (
                    jnp.dot(
                        grad_scores, qkv_ref[tokens, key_columns], preferred_element_type=f32
                    )
                    * scale
                )
                query_grad_ref[rows, columns] = (
                    lane_halves(mixed[:picked], True) + lane_halves(mixed[picked:], False)
                ).astype(bf16)
                out_ref[tokens, key_columns] = (
                    contract_rows(grad_scores, queries) * scale
                ).astype(bf16)
                out_ref[tokens, value_columns] = contract_rows(probs.astype(bf16), grads).astype(
                    bf16
                )
        out_ref[:, :width] = contract_rows(pick_ref[...], query_grad_ref[...]).astype(bf16)

    return pl.pallas_call(
        kernel,
        out_shape=jax.ShapeDtypeStruct(qkv_all.shape, bf16),
        scratch_shapes=[pltpu.VMEM((pick_total, width), bf16)],
        compiler_params=pltpu.CompilerParams(vmem_limit_bytes=32 * 2**20),
        name="attend_backward",
    )(qkv_all, pick_rows, query_all, probs_all, grad_context)


def plane_products(known, grads, attn_grads, depth, widths):
    hidden, model = widths
    rows = grads[0].shape[-2]
    width = hidden + 2 * model
    down_rows, model_rows = hidden // (8 * depth), model // (8 * depth)
    down_width, model_width = hidden // 8, model // 8

    def kernel(known_ref, *refs):
        down_ref, up_ref, out_ref, grads_ref = refs[10:]
        cut = grads[0].shape[-1]
        for far_core in range(2):
            left, right, left_y, right_x = refs[4 * far_core : 4 * far_core + 4]
            attn = refs[8 + far_core]
            for x in range(2):
                for y in range(2):
                    spot = pl.ds(((far_core * 2 + x) * 2 + y) * rows, rows)
                    grads_ref[spot, :cut] = (left_y if y else left)[x]
                    grads_ref[spot, cut : hidden + model] = (right_x if x else right)[y]
                    grads_ref[spot, hidden + model :] = attn[2 * x + y]
        down_ref[...] = contract_rows(
            known_ref[:, :down_width], grads_ref[:, hidden : hidden + model]
        ).astype(bf16)
        up_ref[...] = contract_rows(
            known_ref[:, down_width : down_width + model_width], grads_ref[:, :hidden]
        ).astype(bf16)
        out_ref[...] = contract_rows(
            known_ref[:, down_width + model_width :], grads_ref[:, hidden + model :]
        ).astype(bf16)

    in_vmem = pl.BlockSpec(memory_space=pltpu.VMEM)
    down, up, out = pl.pallas_call(
        kernel,
        in_specs=[in_vmem] * 11,
        out_shape=(
            jax.ShapeDtypeStruct((depth * down_rows, model), bf16),
            jax.ShapeDtypeStruct((depth * model_rows, hidden), bf16),
            jax.ShapeDtypeStruct((depth * model_rows, model), bf16),
        ),
        scratch_shapes=[
            pltpu.VMEM((8 * rows, width), bf16),
        ],
        compiler_params=pltpu.CompilerParams(vmem_limit_bytes=48 * 2**20),
        name="plane_products",
    )(known, *grads, *attn_grads)
    return (
        down.reshape(depth, down_rows, model),
        up.reshape(depth, model_rows, hidden),
        out.reshape(depth, model_rows, model),
    )


def on_lane(place, value):
    lane = lax.broadcasted_iota(jnp.int32, (1, 128), 1)
    return jnp.where(lane == place, value, 0.0)


def whole_sum(values):
    return jnp.sum(jnp.sum(values, axis=0, keepdims=True), axis=1, keepdims=True)


def sum_squares(all_grads, weight_row, target_sum, devices):
    def kernel(table_ref, target_ref, weight_ref, *refs):
        grads, rows_ref = refs[:-1], refs[-1]
        row = on_lane(0, table_ref[...])
        for place, grad in enumerate(grads):
            row = row + on_lane(place + 1, whole_sum(grad[...] * grad[...]))
        rows_ref[:, :128] = jnp.broadcast_to(row, (devices, 128))
        rows_ref[:, 128:] = jnp.broadcast_to(
            weight_ref[...] + on_lane(64, target_ref[...]), (devices, 128)
        )

    table_square = jnp.sum(all_grads[0] * all_grads[0]).reshape(1, 1)
    return pl.pallas_call(
        kernel,
        out_shape=jax.ShapeDtypeStruct((devices, 256), f32),
        name="sum_squares",
    )(table_square, target_sum.reshape(1, 1), weight_row, *all_grads[1:])


grid_steps = 8


def weight_squares(masters):
    table_rows = -(-masters[0].shape[0] // (8 * grid_steps)) * 8
    table_count = masters[0].shape[0]

    def kernel(table_ref, *refs):
        others, row_ref = refs[:-1], refs[-1]
        step = pl.program_id(0)

        @pl.when(step == 0)
        def _():
            row = jnp.zeros((1, 128), f32)
            for place, other in enumerate(others):
                row = row + on_lane(place + 1, whole_sum(other[...] * other[...]))
            row_ref[...] = row

        place = step * table_rows + lax.broadcasted_iota(jnp.int32, (table_rows, 1), 0)
        square = jnp.where(place < table_count, table_ref[...] * table_ref[...], 0.0)
        row_ref[...] += on_lane(0, whole_sum(square))

    return pl.pallas_call(
        kernel,
        grid=(grid_steps,),
        in_specs=[pl.BlockSpec((table_rows, masters[0].shape[1]), lambda k: (k, 0))]
        + [
            pl.BlockSpec(array.shape, lambda k: (0, 0), pipeline_mode=pl.Buffered(1))
            for array in masters[1:]
        ],
        out_specs=pl.BlockSpec((1, 128), lambda k: (0, 0)),
        out_shape=jax.ShapeDtypeStruct((1, 128), f32),
        compiler_params=pltpu.CompilerParams(vmem_limit_bytes=32 * 2**20),
        name="weight_squares",
    )(*masters)


def group_specs(arrays):
    table_rows = -(-arrays[0].shape[0] // (8 * grid_steps)) * 8
    specs = [pl.BlockSpec((table_rows, arrays[0].shape[1]), lambda k: (k, 0))]
    for array in arrays[1:5]:
        rows, width = array.shape
        specs.append(pl.BlockSpec((rows, width // grid_steps), lambda k: (0, k)))
    specs.append(pl.BlockSpec(arrays[5].shape, lambda k: (0, 0)))
    return specs


def lamb_directions(totals, all_grads, firsts, seconds, masters):
    devices = totals.shape[0]
    table_count = all_grads[0].shape[0]
    specs = group_specs(all_grads)
    table_rows = specs[0].block_shape[0]
    first_scale = 1.0 / (1.0 - beta_first**step_count)
    second_scale = 1.0 / (1.0 - beta_second**step_count)

    def kernel(totals_ref, *refs):
        grads, olds, squares, weights = refs[:6], refs[6:12], refs[12:18], refs[18:24]
        new_olds, new_squares, directions, rows_ref = refs[24:30], refs[30:36], refs[36:42], refs[42]
        step = pl.program_id(0)
        grad_total = jnp.sum(totals_ref[:, :128], axis=0, keepdims=True)
        factor = jnp.minimum(
            1.0, clip_limit * lax.rsqrt(jnp.sum(grad_total, axis=1, keepdims=True))
        )

        @pl.when(step == 0)
        def _():
            rows_ref[...] = jnp.zeros_like(rows_ref)

        def update(group, rows, live=None):
            clipped = factor * grads[group][rows]
            new_old = beta_first * olds[group][rows] + (1.0 - beta_first) * clipped
            new_square = beta_second * squares[group][rows] + (1.0 - beta_second) * clipped * clipped
            direction = (new_old * first_scale) / (
                jnp.sqrt(new_square * second_scale) + adam_epsilon
            ) + decay_rates[group] * weights[group][rows]
            new_olds[group][rows] = new_old
            new_squares[group][rows] = new_square
            directions[group][rows] = direction
            square = direction * direction
            return square if live is None else jnp.where(live, square, 0.0)

        def table_part(part, total):
            rows = pl.ds(pl.multiple_of(part * 8, 8), 8)
            place = step * table_rows + part * 8 + lax.broadcasted_iota(
                jnp.int32, (8, 1), 0
            )
            return total + update(0, (rows, slice(None)), place < table_count)

        table_total = lax.fori_loop(
            0, table_rows // 8, table_part, jnp.zeros((8, all_grads[0].shape[1]), f32)
        )
        row = on_lane(0, whole_sum(table_total))
        for group in range(1, 5):
            row = row + on_lane(group, whole_sum(update(group, (slice(None), slice(None)))))
        rows_ref[...] += jnp.broadcast_to(row, rows_ref.shape)

        @pl.when(step == 0)
        def _():
            row = on_lane(5, whole_sum(update(5, (slice(None), slice(None)))))
            rows_ref[...] += jnp.broadcast_to(row, rows_ref.shape)

    shapes = [jax.ShapeDtypeStruct(array.shape, f32) for array in all_grads]
    results = pl.pallas_call(
        kernel,
        grid=(grid_steps,),
        in_specs=[pl.BlockSpec(totals.shape, lambda k: (0, 0))] + specs * 4,
        out_specs=specs * 3 + [pl.BlockSpec((devices, 128), lambda k: (0, 0))],
        out_shape=shapes * 3 + [jax.ShapeDtypeStruct((devices, 128), f32)],
        compiler_params=pltpu.CompilerParams(vmem_limit_bytes=56 * 2**20),
        name="lamb_directions",
    )(totals, *all_grads, *firsts, *seconds, *masters)
    return results[:6], results[6:12], results[12:18], results[18]


def lamb_weights(totals, update_rows, directions, masters):
    specs = group_specs(masters)

    def kernel(totals_ref, updates_ref, *refs):
        moves, weights, news, facts_ref = refs[:6], refs[6:12], refs[12:18], refs[18]
        step = pl.program_id(0)
        lane = lax.broadcasted_iota(jnp.int32, (1, 128), 1)
        grad_total = jnp.sum(totals_ref[:, :128], axis=0, keepdims=True)
        weight_total = jnp.sum(totals_ref[:, 128:], axis=0, keepdims=True)
        update_total = jnp.sum(updates_ref[...], axis=0, keepdims=True)
        weight_norms = jnp.where(lane < 6, jnp.sqrt(jnp.maximum(weight_total, 0.0)), 0.0)
        update_norms = jnp.where(lane < 6, jnp.sqrt(update_total), 1.0)
        rates = learn_rate * weight_norms / update_norms
        for group in range(5):
            rate = jnp.sum(jnp.where(lane == group, rates, 0.0), axis=1, keepdims=True)
            news[group][...] = weights[group][...] - rate * moves[group][...]

        @pl.when(step == 0)
        def _():
            rate = jnp.sum(jnp.where(lane == 5, rates, 0.0), axis=1, keepdims=True)
            news[5][...] = weights[5][...] - rate * moves[5][...]
            grad_norm = jnp.sqrt(jnp.sum(grad_total, axis=1, keepdims=True))
            factor = jnp.minimum(1.0, clip_limit / grad_norm)
            target = jnp.sum(jnp.where(lane == 64, weight_total, 0.0), axis=1, keepdims=True)
            facts_ref[0:1] = factor * jnp.sqrt(grad_total)
            facts_ref[1:2] = weight_norms
            facts_ref[2:3] = update_norms
            facts_ref[3:4] = jnp.broadcast_to(grad_norm, (1, 128))
            facts_ref[4:5] = jnp.broadcast_to(target, (1, 128))

    results = pl.pallas_call(
        kernel,
        grid=(grid_steps,),
        in_specs=[
            pl.BlockSpec(totals.shape, lambda k: (0, 0)),
            pl.BlockSpec(update_rows.shape, lambda k: (0, 0)),
        ]
        + specs * 2,
        out_specs=specs + [pl.BlockSpec((8, 128), lambda k: (0, 0))],
        out_shape=[jax.ShapeDtypeStruct(array.shape, f32) for array in masters]
        + [jax.ShapeDtypeStruct((8, 128), f32)],
        compiler_params=pltpu.CompilerParams(vmem_limit_bytes=56 * 2**20),
        name="lamb_weights",
    )(totals, update_rows, *directions, *masters)
    return results[:6], results[6]


def per_device(
    token_ids,
    doc_ids,
    loss_positions,
    tied_table_master,
    qkv_master,
    out_master,
    up_master,
    down_master,
    norm_master,
    table_first_moment,
    first_qkv,
    first_out,
    first_up,
    first_down,
    first_norms,
    table_second_moment,
    second_qkv,
    second_out,
    second_up,
    second_down,
    second_norms,
):
    links = Links()
    devices = links.wide * links.narrow
    micro_count, unused, length = token_ids.shape
    picked_count = loss_positions.shape[2]
    token_count = micro_count * length
    pick_total = micro_count * picked_count
    model_width = tied_table_master.shape[1]
    head_count = model_width // HEAD_DIM
    block_size = tied_table_master.shape[0]
    count_all = devices * pick_total
    shard_rows = qkv_master.shape[0]

    tokens = token_ids.reshape(token_count)
    picks = loss_positions.reshape(micro_count, picked_count)
    documents = doc_ids.reshape(micro_count, length)
    mean_load = token_count / devices
    slots = int(math.ceil((mean_load + 6.0 * math.sqrt(mean_load)) / 8.0)) * 8
    owner = tokens // block_size
    local_row = tokens % block_size
    token_place = jnp.arange(token_count)
    earlier = (owner[:, None] == owner[None, :]) & (token_place[None, :] < token_place[:, None])
    rank = jnp.sum(earlier.astype(jnp.int32), axis=1)
    most = jnp.max(rank) + 1
    slot_place = jnp.arange(devices * slots)
    line = -(-(slots + 1 + pick_total) // 128) * 128

    pick_hits = picks[:, :, None] == jnp.arange(length)[None, None, :]
    next_hits = picks[:, :, None] + 1 == jnp.arange(length)[None, None, :]
    own_targets = jnp.sum(
        jnp.where(next_hits, token_ids.reshape(micro_count, 1, length), 0), axis=2
    ).reshape(-1)
    pick_docs = jnp.sum(jnp.where(pick_hits, documents[:, None, :], 0), axis=2)

    def slot_of(round_index):
        inside = (rank >= round_index * slots) & (rank < (round_index + 1) * slots)
        return jnp.where(inside, owner * slots + rank - round_index * slots, -1)

    def message_of(slot):
        wanted = jnp.sum(
            jnp.where(slot[None, :] == slot_place[:, None], local_row[None, :] + 1, 0), axis=1
        ) - 1
        wanted = wanted.reshape(devices, slots)
        return jnp.concatenate(
            [
                wanted,
                jnp.broadcast_to(most, (devices, 1)),
                jnp.broadcast_to(own_targets[None, :], (devices, pick_total)),
                jnp.zeros((devices, line - slots - 1 - pick_total), jnp.int32),
            ],
            axis=1,
        )

    def ask(round_index):
        slot = slot_of(round_index)
        return slot, links.to_all(message_of(slot))[:, :slots].reshape(-1)

    def find(asked):
        row_hits = (asked[:, None] == jnp.arange(block_size)[None, :]).astype(bf16)
        return matmul(row_hits, table_low).astype(bf16)

    def place_rows(slot, landed):
        token_hits = (slot[:, None] == slot_place[None, :]).astype(bf16)
        return matmul(token_hits, landed).astype(bf16)

    def give(slot, grad_low):
        token_hits = (slot[:, None] == slot_place[None, :]).astype(bf16)
        return contract_rows(token_hits, grad_low).astype(bf16)

    def take(asked, landed):
        row_hits = (asked[None, :] == jnp.arange(block_size)[:, None]).astype(bf16)
        return matmul(row_hits, landed)

    gain_width = 128
    qkv_width = qkv_master.shape[1]
    gain_shard = jnp.pad(norm_master, ((0, 0), (0, gain_width - norm_master.shape[1])))
    slot_first = slot_of(0)
    masters = (tied_table_master, qkv_master, out_master, up_master, down_master, norm_master)
    first_shard = jnp.concatenate([qkv_master, gain_shard], axis=1).astype(bf16)
    first_early = links.gather_early(first_shard)
    first_near = links.gather_late(first_early)
    message = message_of(slot_first)
    answer = links.to_all(message)
    table_low = after(tied_table_master, message).astype(bf16)
    asked_first = answer[:, :slots].reshape(-1)
    rounds = (jnp.max(answer[:, slots]) + slots - 1) // slots
    targets = answer[:, slots + 1 : slots + 1 + pick_total]
    targets = targets.reshape(links.depth, 2, 2, 2, pick_total).transpose(3, 1, 2, 0, 4).reshape(-1)
    fold_count = down_master.shape[0] // shard_rows
    second_shard = jnp.concatenate(
        [up_master, out_master]
        + [
            down_master[number * shard_rows : (number + 1) * shard_rows]
            for number in range(fold_count)
        ],
        axis=1,
    )
    second_near = links.gather_early(after(second_shard, first_early).astype(bf16))
    first_parts = links.plane_first(first_near)
    found = after(find(asked_first), first_near)
    landed = links.to_all(found)
    first_pieces = links.plane_second(*first_parts)
    weight_row = weight_squares(tie(*masters, found)[:6])
    first_pieces[0] = after(first_pieces[0], weight_row)
    first_whole = links.assemble(links.plane_core(first_pieces))
    second_near = links.gather_late(after(second_near, *first_parts))
    second_parts = links.plane_first(after(second_near, *first_pieces))
    qkv_weight = first_whole[:, :qkv_width]
    gain_entries = first_whole[:, qkv_width : qkv_width + 6].astype(f32).T

    def more_rows(state):
        round_index, embedded = state
        slot, asked = ask(round_index)
        return (round_index + 1, embedded + place_rows(slot, links.to_all(find(asked))))

    unused_round, x_low = lax.while_loop(
        lambda state: state[0] < rounds,
        more_rows,
        (jnp.ones((), jnp.int32), place_rows(slot_first, landed)),
    )

    x_embed = x_low.astype(f32)
    normed_one = layer_norm(x_embed, gain_entries[0], gain_entries[1]).astype(bf16)
    normed_one = after(normed_one, *second_parts)
    qkv_all = matmul(normed_one, qkv_weight).astype(bf16)
    pick_rows = (
        pick_hits[:, :, None, :] & jnp.eye(micro_count, dtype=bool)[:, None, :, None]
    ).reshape(pick_total, token_count).astype(bf16)
    x_embed_picked = matmul(pick_rows, x_low)
    allowed = (jnp.arange(length)[None, None, :] <= picks[:, :, None]) & (
        documents[:, None, :] == pick_docs[:, :, None]
    )
    context, queries, probs = attend(
        qkv_all, pick_rows, allowed.reshape(pick_total, length).astype(f32), micro_count
    )
    second_pieces = links.plane_second(*second_parts)
    second_whole, down_weight = links.assemble(
        links.plane_core([after(piece, context) for piece in second_pieces]),
        folded=(fold_count, model_width),
    )
    hidden = up_master.shape[1]
    up_weight, out_weight = second_whole[:, :hidden], second_whole[:, hidden:]
    x_attn = x_embed_picked + matmul(context, out_weight)
    normed_two = layer_norm(x_attn, gain_entries[2], gain_entries[3]).astype(bf16)
    up_value = matmul(normed_two, up_weight)
    activated = gelu_tanh(up_value).astype(bf16)
    x_out = x_attn + matmul(activated, down_weight)
    picked_low = layer_norm(x_out, gain_entries[4], gain_entries[5]).astype(bf16)

    head_pieces = links.plane_second(*links.plane_first(links.gather_depth(picked_low)))
    head_rows = links.assemble(
        links.plane_core(head_pieces), core_first=True
    )
    columns = links.device * block_size + jnp.arange(block_size)
    logits = contract_cols(head_rows, table_low)
    logits = jnp.where((columns < VOCAB)[None, :], logits, neg_fill)
    target_hits = targets[:, None] == columns[None, :]
    target_sum = jnp.sum(jnp.where(target_hits, logits, 0.0))
    local_top = jnp.max(logits, axis=1)
    local_sum = jnp.sum(jnp.exp(logits - local_top[:, None]), axis=1)

    def merge_totals(first, second):
        top = jnp.maximum(first[0], second[0])
        total = first[1] * jnp.exp(first[0] - top) + second[1] * jnp.exp(second[0] - top)
        return jnp.stack([top, total])

    merged = links.exchange(jnp.stack([local_top, local_sum]), merge_totals)
    def by_owner(values, block_rows):
        if block_rows % 128 == 0:
            blocks = values.reshape(pick_total, links.depth, 8, block_rows)
            blocks = blocks.transpose(2, 0, 1, 3).reshape(8 * pick_total, -1)
            return blocks.reshape(8, pick_total, -1)
        count = values.shape[1]
        place = jnp.arange(count)
        source = place % (count // 8) // block_rows * 8 + place // (count // 8)
        source = source * block_rows + place % block_rows
        order = (jnp.arange(count)[:, None] == source[None, :]).astype(bf16)
        ordered = matmul(values, order).astype(bf16)
        return ordered.reshape(pick_total, 8, count // 8).transpose(1, 0, 2)

    known = jnp.concatenate(
        [
            by_owner(activated, down_master.shape[0]),
            by_owner(normed_two, shard_rows),
            by_owner(context, shard_rows),
        ],
        axis=2,
    )
    known = known.reshape(2, 2, 2, pick_total, -1)
    log_total = merged[0] + jnp.log(merged[1])
    grad_logits = (
        (jnp.exp(logits - log_total[:, None]) - target_hits.astype(f32)) / count_all
    ).astype(bf16)

    half_rows = head_rows.shape[0] // 2
    core = links.place["c"]

    def picked_part(spot):
        part = lax.dynamic_slice_in_dim(grad_logits, spot * half_rows, half_rows, 0)
        return matmul(part, table_low)

    to_core = picked_part(1 - core).astype(bf16)
    to_core, grad_logits = tie(to_core, grad_logits)
    from_core = links.swap(to_core, "c")
    grad_near = links.scatter_plane(
        (picked_part(core) + from_core.astype(f32))
        .astype(bf16)
        .reshape(2, 2, links.depth, pick_total, model_width),
        known,
    )
    known = links.exchange_plane(after(known, grad_near))
    grad_picked = links.scatter_depth(grad_near)

    grad_x_out, gain_last, shift_last = norm_backward(
        x_out, gain_entries[4], gain_entries[5], grad_picked
    )
    grad_mlp = grad_x_out.astype(bf16)
    unused, gelu_pull = jax.vjp(gelu_tanh, up_value)
    grad_up_low = gelu_pull(contract_cols(grad_mlp, down_weight))[0].astype(bf16)
    grad_parts = links.share_first(jnp.concatenate([grad_up_low, grad_mlp], axis=1))
    grad_x_attn, gain_two, shift_two = norm_backward(
        x_attn, gain_entries[2], gain_entries[3], contract_cols(grad_up_low, up_weight)
    )
    grad_x_attn = grad_x_out + grad_x_attn
    grad_x_attn = after(grad_x_attn, *grad_parts)
    grad_attn_low = grad_x_attn.astype(bf16)
    grad_context = contract_cols(grad_attn_low, out_weight).astype(bf16)
    attn_parts = links.share_direct(grad_attn_low)
    grad_parts = links.share_second(*grad_parts)
    grad_qkv_low = attend_backward(
        qkv_all, pick_rows, queries, probs, grad_context, micro_count
    )
    late = grad_qkv_low
    grad_x_one, gain_one, shift_one = norm_backward(
        x_embed, gain_entries[0], gain_entries[1], contract_cols(late, qkv_weight)
    )
    grad_x_embed = grad_x_one + lax.dot_general(
        pick_rows.astype(f32),
        grad_x_attn,
        (((0,), (0,)), ((), ())),
        precision=lax.Precision.HIGHEST,
        preferred_element_type=f32,
    )
    grad_embed_low = grad_x_embed.astype(bf16)
    sent = give(slot_first, grad_embed_low)
    grad_qkv_low = after(grad_qkv_low, sent, known, *grad_parts, *attn_parts)
    returned = links.to_all(sent)
    table_head = contract_rows(after(grad_logits, returned), head_rows)
    half_place = jnp.arange(model_width // 2)
    half_row = half_place % shard_rows
    half_z = half_place // shard_rows % links.depth
    half_plane = half_place // shard_rows // links.depth

    def qkv_part(spot):
        source = ((half_z * 4 + half_plane) * 2 + spot) * shard_rows + half_row
        columns = (jnp.arange(model_width)[:, None] == source[None, :]).astype(bf16)
        return contract_rows(matmul(normed_one, columns).astype(bf16), grad_qkv_low)

    to_core = qkv_part(1 - core).astype(bf16)
    from_core = links.swap(to_core, "c")
    last_mine = (qkv_part(core) + from_core.astype(f32)).astype(bf16)
    last_near = links.scatter_plane(
        last_mine.reshape(2, 2, links.depth, shard_rows, qkv_width), returned
    )
    down_near, up_near, out_near = plane_products(
        known,
        links.share_last(*[after(part, last_mine) for part in grad_parts]),
        links.share_last(after(jnp.stack(attn_parts), last_mine)),
        links.depth,
        (activated.shape[1], model_width),
    )

    last_near = jnp.concatenate([last_near, out_near], axis=-1)
    down_grad = links.scatter_depth(down_near, returned)
    up_grad = links.scatter_depth(up_near, returned)
    last_grad = links.scatter_depth(last_near)
    qkv_grad, out_grad = last_grad[:, :qkv_width], last_grad[:, qkv_width:]
    gain_one = after(gain_one, returned)
    gain_grads = jnp.stack(
        [gain_one, shift_one, gain_two, shift_two, gain_last, shift_last]
    ).reshape(6, devices, shard_rows)
    gain_grads = jnp.pad(
        gain_grads.transpose(1, 0, 2).reshape(devices, 6 * shard_rows),
        ((0, 0), (0, -6 * shard_rows % 128)),
    )
    gain_grad = jnp.sum(links.to_all(after(gain_grads, returned)), axis=0)[: 6 * shard_rows]
    gain_grad = gain_grad.reshape(6, shard_rows).T

    def more_grads(state):
        round_index, earlier_grad = state
        slot, asked = ask(round_index)
        returned_rows = links.to_all(give(slot, grad_embed_low))
        return (round_index + 1, earlier_grad + take(asked, returned_rows))

    unused_round, table_grad = lax.while_loop(
        lambda state: state[0] < rounds,
        more_grads,
        (
            jnp.ones((), jnp.int32),
            table_head + take(asked_first, returned),
        ),
    )

    all_grads = (table_grad, qkv_grad, out_grad, up_grad, down_grad, gain_grad)
    firsts = (table_first_moment, first_qkv, first_out, first_up, first_down, first_norms)
    seconds = (table_second_moment, second_qkv, second_out, second_up, second_down, second_norms)
    totals = links.to_all(sum_squares(all_grads, weight_row, target_sum, devices))
    new_firsts, new_seconds, directions, update_rows = lamb_directions(
        totals, all_grads, firsts, seconds, masters
    )
    new_weights, facts = lamb_weights(totals, links.to_all(update_rows), directions, masters)
    return (
        (jnp.sum(log_total) - facts[4, 0]) / count_all,
        facts[3, 0],
        facts[:3, :6],
        *new_weights,
        *new_firsts,
        *new_seconds,
    )


def solution(mesh):
    rows = P(("wide", "narrow"), None)
    ids = P(None, ("wide", "narrow"), None)
    return jax.shard_map(
        per_device,
        mesh=mesh,
        in_specs=(ids,) * 3 + (rows,) * 18,
        out_specs=(P(),) * 3 + (rows,) * 18,
        check_vma=False,
    )
```

```python
import math

import jax
import jax.numpy as jnp
from jax import lax
from jax.experimental import pallas as pl
from jax.experimental.pallas import tpu as pltpu
from jax.sharding import PartitionSpec as P

HEAD_DIM = 64
VOCAB = 50257

neg_fill = -1e30
beta_first = 0.9
beta_second = 0.999
adam_epsilon = 1e-12
decay_rates = (0.01, 0.01, 0.01, 0.01, 0.01, 0.0)
learn_rate = 0.5
clip_limit = 0.01
norm_epsilon = 1e-05
step_count = 5.0
bf16 = jnp.bfloat16
f32 = jnp.float32


def layer_norm(values, gain_row, offset):
    centered = values - jnp.mean(values, axis=-1, keepdims=True)
    spread = jnp.mean(centered * centered, axis=-1, keepdims=True)
    return centered * lax.rsqrt(spread + norm_epsilon) * gain_row + offset


def norm_backward(values, gain_row, offset, grad_output):
    unused, pullback = jax.vjp(layer_norm, values, gain_row, offset)
    return pullback(grad_output)


def gelu_tanh(values):
    return jax.nn.gelu(values, approximate=True)


def matmul(left_side, right_side):
    return jnp.dot(left_side, right_side, preferred_element_type=f32)


def contract_rows(left_side, right_side):
    return lax.dot_general(
        left_side, right_side, (((0,), (0,)), ((), ())), preferred_element_type=f32
    )


def contract_cols(left_side, right_side):
    return lax.dot_general(
        left_side, right_side, (((1,), (1,)), ((), ())), preferred_element_type=f32
    )


class Links:
    def __init__(self):
        self.wide = lax.axis_size("wide")
        self.narrow = lax.axis_size("narrow")
        self.depth = self.wide // 2
        wide_place = lax.axis_index("wide")
        narrow_place = lax.axis_index("narrow")
        self.device = wide_place * self.narrow + narrow_place
        self.z = wide_place // 2
        self.place = {"x": wide_place % 2, "y": narrow_place // 2, "c": narrow_place % 2}

    def swap(self, values, axis):
        if axis == "x":
            return lax.ppermute(values, "wide", [(i, i ^ 1) for i in range(self.wide)])
        step = 2 if axis == "y" else 1
        return lax.ppermute(values, "narrow", [(i, i ^ step) for i in range(self.narrow)])

    def cross(self, values, step):
        return lax.ppermute(values, "wide", [(i, i ^ (2 * step)) for i in range(self.wide)])

    def exchange(self, values, combine):
        for step in (1, 2):
            other = lax.ppermute(values, "narrow", [(i, i ^ step) for i in range(self.narrow)])
            values = combine(values, other)
        step = 1
        while step < self.wide:
            other = lax.ppermute(values, "wide", [(i, i ^ step) for i in range(self.wide)])
            values = combine(values, other)
            step *= 2
        return values

    def to_all(self, values):
        return lax.all_to_all(values, ("wide", "narrow"), 0, 0, tiled=True)

    def gather_early(self, shard, *before):
        near = shard[None]
        for step in self.bits()[:0:-1]:
            near = jnp.concatenate([near, after(self.cross(near, step), *before)])
        return near

    def gather_late(self, near):
        return jnp.concatenate([near, self.cross(near, 1)])

    def gather_depth(self, shard):
        return self.gather_late(self.gather_early(shard))

    def bits(self):
        return [1 << number for number in range(self.depth.bit_length() - 1)]

    def steps(self):
        found = [0]
        for step in self.bits()[::-1]:
            found = found + [number ^ step for number in found]
        return found

    def plane_first(self, near):
        cut = halves(near.shape[-1])
        left, right = near[..., :cut], near[..., cut:]
        return left, right, self.swap(left, "x"), self.swap(right, "y")

    def plane_second(self, left, right, left_x, right_y):
        left, right = jnp.stack([left, left_x]), jnp.stack([right, right_y])
        return [left, self.swap(left, "y"), right, self.swap(right, "x")]

    def plane_core(self, pieces):
        return pieces + [self.swap(piece, "c") for piece in pieces]

    def gather_plane(self, near):
        return self.plane_core(self.plane_second(*self.plane_first(near)))

    def assemble(self, pieces, core_first=False, folded=None):
        depth = self.depth
        unused, unused_depth, rows, cut = pieces[0].shape
        count, fold = folded or (0, 0)
        width = cut + pieces[2].shape[3] - count * fold

        def kernel(place, *refs):
            sources, target = refs[: len(pieces)], refs[len(pieces)]
            x, y, c = place[0], place[1], place[2]
            for number, source in enumerate(sources):
                far_core, far, second = number // 4, number % 2, number // 2 % 2
                to_c = 1 - c if far_core else c
                columns = slice(cut, width) if second else slice(0, cut)
                for side in range(2):
                    across_x, across_y = (far, side) if second else (side, far)
                    to_x = 1 - x if across_x else x
                    to_y = 1 - y if across_y else y
                    if core_first:
                        target[to_c, to_x, to_y, 0, :, columns] = source[side, 0]
                    elif second:
                        target[0, to_x, to_y, to_c, :, columns] = source[side, 0, :, : width - cut]
                        for number_in in range(count):
                            start = width - cut + number_in * fold
                            refs[-1][
                                0, to_x, to_y, to_c, number_in * rows : (number_in + 1) * rows
                            ] = source[side, 0, :, start : start + fold]
                    else:
                        target[0, to_x, to_y, to_c, :, columns] = source[side, 0]

        place = [self.place["x"], self.place["y"], self.place["c"]]
        place = jnp.stack(place + [self.z ^ step for step in self.steps()]).astype(jnp.int32)
        if core_first:
            shape = (2, 2, 2, depth, rows, width)
            target_spec = pl.BlockSpec(
                (2, 2, 2, 1, rows, width), lambda k, place: (0, 0, 0, place[3 + k], 0, 0)
            )
        else:
            shape = (depth, 2, 2, 2, rows, width)
            target_spec = pl.BlockSpec(
                (1, 2, 2, 2, rows, width), lambda k, place: (place[3 + k], 0, 0, 0, 0, 0)
            )
        shapes, target_specs = [jax.ShapeDtypeStruct(shape, pieces[0].dtype)], [target_spec]
        if count:
            shapes.append(
                jax.ShapeDtypeStruct((depth, 2, 2, 2, count * rows, fold), pieces[0].dtype)
            )
            target_specs.append(
                pl.BlockSpec(
                    (1, 2, 2, 2, count * rows, fold),
                    lambda k, place: (place[3 + k], 0, 0, 0, 0, 0),
                )
            )
        wholes = pl.pallas_call(
            kernel,
            out_shape=shapes,
            grid_spec=pltpu.PrefetchScalarGridSpec(
                num_scalar_prefetch=1,
                grid=(depth,),
                in_specs=[
                    pl.BlockSpec((2, 1, rows, piece.shape[3]), lambda k, place: (0, k, 0, 0))
                    for piece in pieces
                ],
                out_specs=target_specs,
            ),
            compiler_params=pltpu.CompilerParams(vmem_limit_bytes=24 * 2**20),
            name="assemble",
        )(place, *pieces)
        wholes = [whole.reshape(-1, whole.shape[-1]) for whole in wholes]
        return wholes if count else wholes[0]

    def exchange_plane(self, values):
        for axis in "xyc":
            dim = " xyc".index(axis) - 1
            mine = lax.dynamic_index_in_dim(values, self.place[axis], dim, keepdims=False)
            other = lax.dynamic_index_in_dim(values, 1 - self.place[axis], dim, keepdims=False)
            values = jnp.stack([mine, self.swap(other, axis)], axis=dim)
        return values.transpose(2, 0, 1, 3, 4).reshape(-1, values.shape[-1])

    def share_direct(self, values):
        pairs = []
        for wide in range(self.wide):
            for narrow in range(self.narrow):
                pairs.append((wide * self.narrow + narrow, (wide ^ 1) * self.narrow + (narrow ^ 2)))
        across = lax.ppermute(values, ("wide", "narrow"), pairs)
        return [values, self.swap(values, "y"), self.swap(values, "x"), across]

    def share_first(self, values):
        cut = halves(values.shape[-1])
        left, right = values[:, :cut], values[:, cut:]
        return left, right, self.swap(left, "x"), self.swap(right, "y")

    def share_second(self, left, right, left_x, right_y):
        left, right = jnp.stack([left, left_x]), jnp.stack([right, right_y])
        return left, right, self.swap(left, "y"), self.swap(right, "x")

    def share_last(self, *pieces):
        return list(pieces) + [self.swap(piece, "c") for piece in pieces]

    def scatter_plane(self, full, *before_second):
        cut = halves(full.shape[-1])
        x, y = self.place["x"], self.place["y"]

        def pick(values, spot, dim):
            return lax.dynamic_index_in_dim(values, spot, dim, keepdims=False)

        left, right = full[..., :cut], full[..., cut:]
        from_x = self.swap(pick(left, 1 - x, 0), "x")
        from_y = self.swap(pick(right, 1 - y, 1), "y")
        left = (pick(left, x, 0).astype(f32) + from_x.astype(f32)).astype(bf16)
        right = (pick(right, y, 1).astype(f32) + from_y.astype(f32)).astype(bf16)
        left, right = after(left, *before_second), after(right, *before_second)
        sends = pick(left, 1 - y, 0), pick(right, 1 - x, 0)
        from_y, from_x = self.swap(sends[0], "y"), self.swap(sends[1], "x")
        left = pick(left, y, 0).astype(f32) + from_y.astype(f32)
        right = pick(right, x, 0).astype(f32) + from_x.astype(f32)
        return jnp.concatenate([left, right], axis=-1).astype(bf16), sends

    def scatter_depth(self, near, *before_last):
        for step in self.bits():
            if step == self.bits()[-1]:
                near = after(near, *before_last)
            pairs = near.reshape((-1, 2) + near.shape[1:])
            bit = self.z // step % 2
            other = lax.dynamic_index_in_dim(pairs, 1 - bit, 1, keepdims=False)
            mine = lax.dynamic_index_in_dim(pairs, bit, 1, keepdims=False)
            send = other.astype(bf16)
            near = mine.astype(f32) + self.cross(send, step).astype(f32)
        return near[0], send


def halves(width):
    return width // 256 * 128


def tie(*values):
    return lax.optimization_barrier(values)


def after(values, *others):
    return lax.optimization_barrier((values, *others))[0]


def lane_halves(values, first):
    lane = lax.broadcasted_iota(jnp.int32, values.shape, 1)
    return jnp.where((lane < HEAD_DIM) == first, values, jnp.zeros_like(values))


def attend(qkv_all, pick_rows, allowed, micro_count):
    token_count = qkv_all.shape[0]
    width = qkv_all.shape[1] // 3
    pick_total = pick_rows.shape[0]
    length, picked = token_count // micro_count, pick_total // micro_count
    pair = 2 * HEAD_DIM
    scale = HEAD_DIM ** (-0.5)

    def kernel(qkv_ref, pick_ref, allowed_ref, context_ref, query_ref, prob_ref):
        query_ref[...] = jnp.dot(
            pick_ref[...], qkv_ref[:, :width], preferred_element_type=f32
        ).astype(bf16)
        for micro in range(micro_count):
            rows = slice(micro * picked, (micro + 1) * picked)
            keep = allowed_ref[rows] > 0.5
            keep = jnp.concatenate([keep, keep], axis=0)
            for number in range(width // pair):
                columns = slice(number * pair, (number + 1) * pair)
                keys = qkv_ref[
                    micro * length : (micro + 1) * length,
                    width + number * pair : width + (number + 1) * pair,
                ]
                values = qkv_ref[
                    micro * length : (micro + 1) * length,
                    2 * width + number * pair : 2 * width + (number + 1) * pair,
                ]
                query = query_ref[rows, columns]
                both = jnp.concatenate(
                    [lane_halves(query, True), lane_halves(query, False)], axis=0
                )
                scores = contract_cols(both, keys) * scale
                scores = jnp.where(keep, scores, neg_fill)
                shifted = jnp.exp(scores - jnp.max(scores, axis=1, keepdims=True))
                probs = shifted / jnp.sum(shifted, axis=1, keepdims=True)
                prob_ref[micro, number] = probs
                mixed = jnp.dot(probs.astype(bf16), values, preferred_element_type=f32)
                context_ref[rows, columns] = (
                    lane_halves(mixed[:picked], True) + lane_halves(mixed[picked:], False)
                ).astype(bf16)

    return pl.pallas_call(
        kernel,
        out_shape=(
            jax.ShapeDtypeStruct((pick_total, width), bf16),
            jax.ShapeDtypeStruct((pick_total, width), bf16),
            jax.ShapeDtypeStruct((micro_count, width // pair, 2 * picked, length), f32),
        ),
        compiler_params=pltpu.CompilerParams(vmem_limit_bytes=32 * 2**20),
        name="attend",
    )(qkv_all, pick_rows, allowed)


def attend_backward(qkv_all, pick_rows, query_all, probs_all, grad_context, micro_count):
    token_count = qkv_all.shape[0]
    width = qkv_all.shape[1] // 3
    pick_total = pick_rows.shape[0]
    length, picked = token_count // micro_count, pick_total // micro_count
    pair = 2 * HEAD_DIM
    scale = HEAD_DIM ** (-0.5)

    def kernel(qkv_ref, pick_ref, query_ref, prob_ref, grad_ref, out_ref, query_grad_ref):
        for micro in range(micro_count):
            rows = slice(micro * picked, (micro + 1) * picked)
            tokens = slice(micro * length, (micro + 1) * length)
            for number in range(width // pair):
                columns = slice(number * pair, (number + 1) * pair)
                key_columns = slice(width + number * pair, width + (number + 1) * pair)
                value_columns = slice(2 * width + number * pair, 2 * width + (number + 1) * pair)
                query, grad = query_ref[rows, columns], grad_ref[rows, columns]
                queries = jnp.concatenate(
                    [lane_halves(query, True), lane_halves(query, False)], axis=0
                )
                grads = jnp.concatenate(
                    [lane_halves(grad, True), lane_halves(grad, False)], axis=0
                )
                probs = prob_ref[micro, number]
                grad_probs = contract_cols(grads, qkv_ref[tokens, value_columns])
                inner = jnp.sum(probs * grad_probs, axis=1, keepdims=True)
                grad_scores = (probs * (grad_probs - inner)).astype(bf16)
                mixed = (
                    jnp.dot(
                        grad_scores, qkv_ref[tokens, key_columns], preferred_element_type=f32
                    )
                    * scale
                )
                query_grad_ref[rows, columns] = (
                    lane_halves(mixed[:picked], True) + lane_halves(mixed[picked:], False)
                ).astype(bf16)
                out_ref[tokens, key_columns] = (
                    contract_rows(grad_scores, queries) * scale
                ).astype(bf16)
                out_ref[tokens, value_columns] = contract_rows(probs.astype(bf16), grads).astype(
                    bf16
                )
        out_ref[:, :width] = contract_rows(pick_ref[...], query_grad_ref[...]).astype(bf16)

    return pl.pallas_call(
        kernel,
        out_shape=jax.ShapeDtypeStruct(qkv_all.shape, bf16),
        scratch_shapes=[pltpu.VMEM((pick_total, width), bf16)],
        compiler_params=pltpu.CompilerParams(vmem_limit_bytes=32 * 2**20),
        name="attend_backward",
    )(qkv_all, pick_rows, query_all, probs_all, grad_context)


def plane_products(known, grads, attn_grads, depth, widths):
    hidden, model = widths
    rows = grads[0].shape[-2]
    width = hidden + 2 * model
    down_rows, model_rows = hidden // (8 * depth), model // (8 * depth)
    down_width, model_width = hidden // 8, model // 8

    def kernel(known_ref, *refs):
        down_ref, up_ref, out_ref, grads_ref = refs[10:]
        cut = grads[0].shape[-1]
        for far_core in range(2):
            left, right, left_y, right_x = refs[4 * far_core : 4 * far_core + 4]
            attn = refs[8 + far_core]
            for x in range(2):
                for y in range(2):
                    spot = pl.ds(((far_core * 2 + x) * 2 + y) * rows, rows)
                    grads_ref[spot, :cut] = (left_y if y else left)[x]
                    grads_ref[spot, cut : hidden + model] = (right_x if x else right)[y]
                    grads_ref[spot, hidden + model :] = attn[2 * x + y]
        down_ref[...] = contract_rows(
            known_ref[:, :down_width], grads_ref[:, hidden : hidden + model]
        ).astype(bf16)
        up_ref[...] = contract_rows(
            known_ref[:, down_width : down_width + model_width], grads_ref[:, :hidden]
        ).astype(bf16)
        out_ref[...] = contract_rows(
            known_ref[:, down_width + model_width :], grads_ref[:, hidden + model :]
        ).astype(bf16)

    in_vmem = pl.BlockSpec(memory_space=pltpu.VMEM)
    down, up, out = pl.pallas_call(
        kernel,
        in_specs=[in_vmem] * 11,
        out_shape=(
            jax.ShapeDtypeStruct((depth * down_rows, model), bf16),
            jax.ShapeDtypeStruct((depth * model_rows, hidden), bf16),
            jax.ShapeDtypeStruct((depth * model_rows, model), bf16),
        ),
        scratch_shapes=[
            pltpu.VMEM((8 * rows, width), bf16),
        ],
        compiler_params=pltpu.CompilerParams(vmem_limit_bytes=48 * 2**20),
        name="plane_products",
    )(known, *grads, *attn_grads)
    return (
        down.reshape(depth, down_rows, model),
        up.reshape(depth, model_rows, hidden),
        out.reshape(depth, model_rows, model),
    )


def on_lane(place, value):
    lane = lax.broadcasted_iota(jnp.int32, (1, 128), 1)
    return jnp.where(lane == place, value, 0.0)


def whole_sum(values):
    return jnp.sum(jnp.sum(values, axis=0, keepdims=True), axis=1, keepdims=True)


def sum_squares(all_grads, weight_row, target_sum, devices):
    def kernel(table_ref, target_ref, weight_ref, *refs):
        grads, rows_ref = refs[:-1], refs[-1]
        row = on_lane(0, table_ref[...])
        for place, grad in enumerate(grads):
            row = row + on_lane(place + 1, whole_sum(grad[...] * grad[...]))
        rows_ref[:, :128] = jnp.broadcast_to(row, (devices, 128))
        rows_ref[:, 128:] = jnp.broadcast_to(
            weight_ref[...] + on_lane(64, target_ref[...]), (devices, 128)
        )

    table_square = jnp.sum(all_grads[0] * all_grads[0]).reshape(1, 1)
    return pl.pallas_call(
        kernel,
        out_shape=jax.ShapeDtypeStruct((devices, 256), f32),
        name="sum_squares",
    )(table_square, target_sum.reshape(1, 1), weight_row, *all_grads[1:])


grid_steps = 4


row_block = 256


def head_logits(head_rows, table_low, targets, base, block_size):
    row_count, width = head_rows.shape
    columns = table_low.shape[0]
    block = min(row_block, row_count)

    def kernel(base_ref, rows_ref, table_ref, targets_ref, logits_ref, top_ref, sum_ref, hit_ref):
        step = pl.program_id(0)
        place = lax.broadcasted_iota(jnp.int32, (1, columns), 1)
        column = jnp.where(place < block_size, place + base_ref[0], VOCAB)
        fill = jnp.where(column < VOCAB, 0.0, neg_fill)
        logits = contract_cols(rows_ref[...], table_ref[...]) + fill
        logits_ref[...] = logits
        top = jnp.max(logits, axis=1, keepdims=True)
        total = jnp.sum(jnp.exp(logits - top), axis=1, keepdims=True)
        top_ref[...] = jnp.broadcast_to(top, (block, 128)).T[:1]
        sum_ref[...] = jnp.broadcast_to(total, (block, 128)).T[:1]

        @pl.when(step == 0)
        def _():
            hit_ref[...] = jnp.zeros_like(hit_ref)

        hits = targets_ref[...] == column
        hit_ref[...] += jnp.broadcast_to(whole_sum(jnp.where(hits, logits, 0.0)), (1, 128))

    return pl.pallas_call(
        kernel,
        out_shape=(
            jax.ShapeDtypeStruct((row_count, columns), f32),
            jax.ShapeDtypeStruct((1, row_count), f32),
            jax.ShapeDtypeStruct((1, row_count), f32),
            jax.ShapeDtypeStruct((1, 128), f32),
        ),
        grid=(row_count // block,),
        in_specs=[
            pl.BlockSpec(memory_space=pltpu.SMEM),
            pl.BlockSpec((block, width), lambda k: (k, 0)),
            pl.BlockSpec((columns, width), lambda k: (0, 0)),
            pl.BlockSpec((block, 1), lambda k: (k, 0)),
        ],
        out_specs=(
            pl.BlockSpec((block, columns), lambda k: (k, 0)),
            pl.BlockSpec((1, block), lambda k: (0, k)),
            pl.BlockSpec((1, block), lambda k: (0, k)),
            pl.BlockSpec((1, 128), lambda k: (0, 0)),
        ),
        compiler_params=pltpu.CompilerParams(vmem_limit_bytes=56 * 2**20),
        name="head_logits",
    )(base.reshape(1), head_rows, table_low, targets)


def head_grads(logits, log_total, table_low, targets, base, half, count_all, block_size, add=None):
    row_count, columns = logits.shape
    width = table_low.shape[1]
    block = min(row_block, row_count // 2)
    steps = row_count // 2 // block
    scale = 1.0 / count_all

    def kernel(place_ref, logits_ref, total_ref, table_ref, targets_ref, *refs):
        grads_ref, out_ref = refs[-2:]
        place = lax.broadcasted_iota(jnp.int32, (1, columns), 1)
        column = jnp.where(place < block_size, place + place_ref[1], VOCAB)
        total = jnp.broadcast_to(total_ref[...], (128, block)).T[:, :1]
        hits = targets_ref[...] == column
        probs = jnp.exp(logits_ref[...] - total)
        grads = ((probs - jnp.where(hits, 1.0, 0.0)) * scale).astype(bf16)
        grads_ref[...] = grads
        product = matmul(grads, table_ref[...])
        if add is not None:
            product = product + refs[0][...].astype(f32)
        out_ref[...] = product.astype(bf16)

    half_spec = pl.BlockSpec((block, width), lambda k, place: (k, 0))
    return pl.pallas_call(
        kernel,
        out_shape=(
            jax.ShapeDtypeStruct((row_count // 2, columns), bf16),
            jax.ShapeDtypeStruct((row_count // 2, width), bf16),
        ),
        grid_spec=pltpu.PrefetchScalarGridSpec(
            num_scalar_prefetch=1,
            grid=(steps,),
            in_specs=[
                pl.BlockSpec((block, columns), lambda k, place: (place[0] * steps + k, 0)),
                pl.BlockSpec((1, block), lambda k, place: (0, place[0] * steps + k)),
                pl.BlockSpec((columns, width), lambda k, place: (0, 0)),
                pl.BlockSpec((block, 1), lambda k, place: (place[0] * steps + k, 0)),
            ]
            + ([] if add is None else [half_spec]),
            out_specs=(
                pl.BlockSpec((block, columns), lambda k, place: (k, 0)),
                half_spec,
            ),
        ),
        compiler_params=pltpu.CompilerParams(vmem_limit_bytes=56 * 2**20),
        name="head_grads",
    )(
        jnp.stack([half, base]).astype(jnp.int32),
        logits,
        log_total,
        table_low,
        targets,
        *(() if add is None else (add,)),
    )


def weight_squares(masters):
    table_rows = -(-masters[0].shape[0] // (8 * grid_steps)) * 8
    table_count = masters[0].shape[0]

    def kernel(table_ref, *refs):
        others, row_ref = refs[:-1], refs[-1]
        step = pl.program_id(0)

        @pl.when(step == 0)
        def _():
            row = jnp.zeros((1, 128), f32)
            for place, other in enumerate(others):
                row = row + on_lane(place + 1, whole_sum(other[...] * other[...]))
            row_ref[...] = row

        place = step * table_rows + lax.broadcasted_iota(jnp.int32, (table_rows, 1), 0)
        square = jnp.where(place < table_count, table_ref[...] * table_ref[...], 0.0)
        row_ref[...] += on_lane(0, whole_sum(square))

    return pl.pallas_call(
        kernel,
        grid=(grid_steps,),
        in_specs=[pl.BlockSpec((table_rows, masters[0].shape[1]), lambda k: (k, 0))]
        + [
            pl.BlockSpec(array.shape, lambda k: (0, 0), pipeline_mode=pl.Buffered(1))
            for array in masters[1:]
        ],
        out_specs=pl.BlockSpec((1, 128), lambda k: (0, 0)),
        out_shape=jax.ShapeDtypeStruct((1, 128), f32),
        compiler_params=pltpu.CompilerParams(vmem_limit_bytes=32 * 2**20),
        name="weight_squares",
    )(*masters)


def group_specs(arrays):
    table_rows = -(-arrays[0].shape[0] // (8 * grid_steps)) * 8
    specs = [pl.BlockSpec((table_rows, arrays[0].shape[1]), lambda k: (k, 0))]
    for array in arrays[1:5]:
        rows, width = array.shape
        specs.append(pl.BlockSpec((rows, width // grid_steps), lambda k: (0, k)))
    specs.append(pl.BlockSpec(arrays[5].shape, lambda k: (0, 0)))
    return specs


def lamb_directions(totals, all_grads, firsts, seconds, masters):
    devices = totals.shape[0]
    table_count = all_grads[0].shape[0]
    specs = group_specs(all_grads)
    table_rows = specs[0].block_shape[0]
    first_scale = 1.0 / (1.0 - beta_first**step_count)
    second_scale = 1.0 / (1.0 - beta_second**step_count)

    def kernel(totals_ref, *refs):
        grads, olds, squares, weights = refs[:6], refs[6:12], refs[12:18], refs[18:24]
        new_olds, new_squares, directions, rows_ref = refs[24:30], refs[30:36], refs[36:42], refs[42]
        step = pl.program_id(0)
        grad_total = jnp.sum(totals_ref[:, :128], axis=0, keepdims=True)
        factor = jnp.minimum(
            1.0, clip_limit * lax.rsqrt(jnp.sum(grad_total, axis=1, keepdims=True))
        )

        @pl.when(step == 0)
        def _():
            rows_ref[...] = jnp.zeros_like(rows_ref)

        def update(group, rows, live=None):
            clipped = factor * grads[group][rows]
            new_old = beta_first * olds[group][rows] + (1.0 - beta_first) * clipped
            new_square = beta_second * squares[group][rows] + (1.0 - beta_second) * clipped * clipped
            direction = (new_old * first_scale) / (
                jnp.sqrt(new_square * second_scale) + adam_epsilon
            ) + decay_rates[group] * weights[group][rows]
            new_olds[group][rows] = new_old
            new_squares[group][rows] = new_square
            directions[group][rows] = direction
            square = direction * direction
            return square if live is None else jnp.where(live, square, 0.0)

        def table_part(part, total):
            rows = pl.ds(pl.multiple_of(part * 8, 8), 8)
            place = step * table_rows + part * 8 + lax.broadcasted_iota(
                jnp.int32, (8, 1), 0
            )
            return total + update(0, (rows, slice(None)), place < table_count)

        table_total = lax.fori_loop(
            0, table_rows // 8, table_part, jnp.zeros((8, all_grads[0].shape[1]), f32)
        )
        row = on_lane(0, whole_sum(table_total))
        for group in range(1, 5):
            row = row + on_lane(group, whole_sum(update(group, (slice(None), slice(None)))))
        rows_ref[...] += jnp.broadcast_to(row, rows_ref.shape)

        @pl.when(step == 0)
        def _():
            row = on_lane(5, whole_sum(update(5, (slice(None), slice(None)))))
            rows_ref[...] += jnp.broadcast_to(row, rows_ref.shape)

    shapes = [jax.ShapeDtypeStruct(array.shape, f32) for array in all_grads]
    results = pl.pallas_call(
        kernel,
        grid=(grid_steps,),
        in_specs=[pl.BlockSpec(totals.shape, lambda k: (0, 0))] + specs * 4,
        out_specs=specs * 3 + [pl.BlockSpec((devices, 128), lambda k: (0, 0))],
        out_shape=shapes * 3 + [jax.ShapeDtypeStruct((devices, 128), f32)],
        compiler_params=pltpu.CompilerParams(vmem_limit_bytes=56 * 2**20),
        name="lamb_directions",
    )(totals, *all_grads, *firsts, *seconds, *masters)
    return results[:6], results[6:12], results[12:18], results[18]


def lamb_weights(totals, update_rows, directions, masters):
    specs = group_specs(masters)

    def kernel(totals_ref, updates_ref, *refs):
        moves, weights, news, facts_ref = refs[:6], refs[6:12], refs[12:18], refs[18]
        step = pl.program_id(0)
        lane = lax.broadcasted_iota(jnp.int32, (1, 128), 1)
        grad_total = jnp.sum(totals_ref[:, :128], axis=0, keepdims=True)
        weight_total = jnp.sum(totals_ref[:, 128:], axis=0, keepdims=True)
        update_total = jnp.sum(updates_ref[...], axis=0, keepdims=True)
        weight_norms = jnp.where(lane < 6, jnp.sqrt(jnp.maximum(weight_total, 0.0)), 0.0)
        update_norms = jnp.where(lane < 6, jnp.sqrt(update_total), 1.0)
        rates = learn_rate * weight_norms / update_norms
        for group in range(5):
            rate = jnp.sum(jnp.where(lane == group, rates, 0.0), axis=1, keepdims=True)
            news[group][...] = weights[group][...] - rate * moves[group][...]

        @pl.when(step == 0)
        def _():
            rate = jnp.sum(jnp.where(lane == 5, rates, 0.0), axis=1, keepdims=True)
            news[5][...] = weights[5][...] - rate * moves[5][...]
            grad_norm = jnp.sqrt(jnp.sum(grad_total, axis=1, keepdims=True))
            factor = jnp.minimum(1.0, clip_limit / grad_norm)
            target = jnp.sum(jnp.where(lane == 64, weight_total, 0.0), axis=1, keepdims=True)
            facts_ref[0:1] = factor * jnp.sqrt(grad_total)
            facts_ref[1:2] = weight_norms
            facts_ref[2:3] = update_norms
            facts_ref[3:4] = jnp.broadcast_to(grad_norm, (1, 128))
            facts_ref[4:5] = jnp.broadcast_to(target, (1, 128))

    results = pl.pallas_call(
        kernel,
        grid=(grid_steps,),
        in_specs=[
            pl.BlockSpec(totals.shape, lambda k: (0, 0)),
            pl.BlockSpec(update_rows.shape, lambda k: (0, 0)),
        ]
        + specs * 2,
        out_specs=specs + [pl.BlockSpec((8, 128), lambda k: (0, 0))],
        out_shape=[jax.ShapeDtypeStruct(array.shape, f32) for array in masters]
        + [jax.ShapeDtypeStruct((8, 128), f32)],
        compiler_params=pltpu.CompilerParams(vmem_limit_bytes=56 * 2**20),
        name="lamb_weights",
    )(totals, update_rows, *directions, *masters)
    return results[:6], results[6]


def per_device(
    token_ids,
    doc_ids,
    loss_positions,
    tied_table_master,
    qkv_master,
    out_master,
    up_master,
    down_master,
    norm_master,
    table_first_moment,
    first_qkv,
    first_out,
    first_up,
    first_down,
    first_norms,
    table_second_moment,
    second_qkv,
    second_out,
    second_up,
    second_down,
    second_norms,
):
    links = Links()
    devices = links.wide * links.narrow
    micro_count, unused, length = token_ids.shape
    picked_count = loss_positions.shape[2]
    token_count = micro_count * length
    pick_total = micro_count * picked_count
    model_width = tied_table_master.shape[1]
    head_count = model_width // HEAD_DIM
    block_size = tied_table_master.shape[0]
    count_all = devices * pick_total
    shard_rows = qkv_master.shape[0]

    tokens = token_ids.reshape(token_count)
    picks = loss_positions.reshape(micro_count, picked_count)
    documents = doc_ids.reshape(micro_count, length)
    mean_load = token_count / devices
    slots = int(math.ceil((mean_load + 6.0 * math.sqrt(mean_load)) / 8.0)) * 8
    owner = tokens // block_size
    local_row = tokens % block_size
    token_place = jnp.arange(token_count)
    earlier = (owner[:, None] == owner[None, :]) & (token_place[None, :] < token_place[:, None])
    rank = jnp.sum(earlier.astype(jnp.int32), axis=1)
    most = jnp.max(rank) + 1
    slot_place = jnp.arange(devices * slots)
    line = -(-(slots + 1 + pick_total) // 128) * 128

    pick_hits = picks[:, :, None] == jnp.arange(length)[None, None, :]
    next_hits = picks[:, :, None] + 1 == jnp.arange(length)[None, None, :]
    own_targets = jnp.sum(
        jnp.where(next_hits, token_ids.reshape(micro_count, 1, length), 0), axis=2
    ).reshape(-1)
    pick_docs = jnp.sum(jnp.where(pick_hits, documents[:, None, :], 0), axis=2)

    def slot_of(round_index):
        inside = (rank >= round_index * slots) & (rank < (round_index + 1) * slots)
        return jnp.where(inside, owner * slots + rank - round_index * slots, -1)

    def message_of(slot):
        wanted = jnp.sum(
            jnp.where(slot[None, :] == slot_place[:, None], local_row[None, :] + 1, 0), axis=1
        ) - 1
        wanted = wanted.reshape(devices, slots)
        return jnp.concatenate(
            [
                wanted,
                jnp.broadcast_to(most, (devices, 1)),
                jnp.broadcast_to(own_targets[None, :], (devices, pick_total)),
                jnp.zeros((devices, line - slots - 1 - pick_total), jnp.int32),
            ],
            axis=1,
        )

    def ask(round_index):
        slot = slot_of(round_index)
        return slot, links.to_all(message_of(slot))[:, :slots].reshape(-1)

    def find(asked):
        row_hits = (asked[:, None] == jnp.arange(padded_rows)[None, :]).astype(bf16)
        return matmul(row_hits, table_low).astype(bf16)

    def place_rows(slot, landed):
        token_hits = (slot[:, None] == slot_place[None, :]).astype(bf16)
        return matmul(token_hits, landed).astype(bf16)

    def give(slot, grad_low):
        token_hits = (slot[:, None] == slot_place[None, :]).astype(bf16)
        return contract_rows(token_hits, grad_low).astype(bf16)

    def take(asked, landed):
        row_hits = (asked[None, :] == jnp.arange(block_size)[:, None]).astype(bf16)
        return matmul(row_hits, landed)

    gain_width = 128
    qkv_width = qkv_master.shape[1]
    gain_shard = jnp.pad(norm_master, ((0, 0), (0, gain_width - norm_master.shape[1])))
    slot_first = slot_of(0)
    masters = (tied_table_master, qkv_master, out_master, up_master, down_master, norm_master)
    first_shard = jnp.concatenate([qkv_master, gain_shard], axis=1).astype(bf16)
    first_early = links.gather_early(first_shard)
    first_near = links.gather_late(first_early)
    message = message_of(slot_first)
    answer = links.to_all(message)
    padded_rows = -(-block_size // 128) * 128
    table_low = jnp.pad(
        after(tied_table_master, message), ((0, padded_rows - block_size), (0, 0))
    ).astype(bf16)
    asked_first = answer[:, :slots].reshape(-1)
    rounds = (jnp.max(answer[:, slots]) + slots - 1) // slots
    targets = answer[:, slots + 1 : slots + 1 + pick_total]
    targets = targets.reshape(links.depth, 2, 2, 2, pick_total).transpose(3, 1, 2, 0, 4).reshape(-1)
    fold_count = down_master.shape[0] // shard_rows
    second_shard = jnp.concatenate(
        [up_master, out_master]
        + [
            down_master[number * shard_rows : (number + 1) * shard_rows]
            for number in range(fold_count)
        ],
        axis=1,
    )
    second_near = links.gather_early(after(second_shard, first_early).astype(bf16))
    first_parts = links.plane_first(first_near)
    found = after(find(asked_first), first_near)
    landed = links.to_all(found)
    first_pieces = links.plane_second(*first_parts)
    weight_row = weight_squares(tie(*masters, found)[:6])
    first_pieces[0] = after(first_pieces[0], weight_row, table_low)
    first_whole = links.assemble(links.plane_core(first_pieces))
    second_near = links.gather_late(after(second_near, *first_parts))
    second_parts = links.plane_first(after(second_near, *first_pieces))
    qkv_weight = first_whole[:, :qkv_width]
    gain_entries = first_whole[:, qkv_width : qkv_width + 6].astype(f32).T

    def more_rows(state):
        round_index, embedded = state
        slot, asked = ask(round_index)
        return (round_index + 1, embedded + place_rows(slot, links.to_all(find(asked))))

    unused_round, x_low = lax.while_loop(
        lambda state: state[0] < rounds,
        more_rows,
        (jnp.ones((), jnp.int32), place_rows(slot_first, landed)),
    )

    x_embed = x_low.astype(f32)
    normed_one = layer_norm(x_embed, gain_entries[0], gain_entries[1]).astype(bf16)
    normed_one = after(normed_one, *second_parts)
    qkv_all = matmul(normed_one, qkv_weight).astype(bf16)
    pick_rows = (
        pick_hits[:, :, None, :] & jnp.eye(micro_count, dtype=bool)[:, None, :, None]
    ).reshape(pick_total, token_count).astype(bf16)
    x_embed_picked = matmul(pick_rows, x_low)
    allowed = (jnp.arange(length)[None, None, :] <= picks[:, :, None]) & (
        documents[:, None, :] == pick_docs[:, :, None]
    )
    context, queries, probs = attend(
        qkv_all, pick_rows, allowed.reshape(pick_total, length).astype(f32), micro_count
    )
    second_pieces = links.plane_second(*second_parts)
    second_whole, down_weight = links.assemble(
        links.plane_core([after(piece, context) for piece in second_pieces]),
        folded=(fold_count, model_width),
    )
    hidden = up_master.shape[1]
    up_weight, out_weight = second_whole[:, :hidden], second_whole[:, hidden:]
    x_attn = x_embed_picked + matmul(context, out_weight)
    normed_two = layer_norm(x_attn, gain_entries[2], gain_entries[3]).astype(bf16)
    up_value = matmul(normed_two, up_weight)
    activated = gelu_tanh(up_value).astype(bf16)
    x_out = x_attn + matmul(activated, down_weight)
    picked_low = layer_norm(x_out, gain_entries[4], gain_entries[5]).astype(bf16)

    head_pieces = links.plane_second(*links.plane_first(links.gather_depth(picked_low)))
    head_rows = links.assemble(
        links.plane_core(head_pieces), core_first=True
    )
    base = links.device * block_size
    target_column = targets[:, None]
    logits, local_top, local_sum, target_sum = head_logits(
        head_rows, table_low, target_column, base, block_size
    )
    target_sum = target_sum[:, :1]

    def merge_totals(first, second):
        top = jnp.maximum(first[0], second[0])
        total = first[1] * jnp.exp(first[0] - top) + second[1] * jnp.exp(second[0] - top)
        return jnp.stack([top, total])

    merged = links.exchange(jnp.concatenate([local_top, local_sum]), merge_totals)
    def by_owner(values, block_rows):
        if block_rows % 128 == 0:
            blocks = values.reshape(pick_total, links.depth, 8, block_rows)
            blocks = blocks.transpose(2, 0, 1, 3).reshape(8 * pick_total, -1)
            return blocks.reshape(8, pick_total, -1)
        count = values.shape[1]
        place = jnp.arange(count)
        source = place % (count // 8) // block_rows * 8 + place // (count // 8)
        source = source * block_rows + place % block_rows
        order = (jnp.arange(count)[:, None] == source[None, :]).astype(bf16)
        ordered = matmul(values, order).astype(bf16)
        return ordered.reshape(pick_total, 8, count // 8).transpose(1, 0, 2)

    known = jnp.concatenate(
        [
            by_owner(activated, down_master.shape[0]),
            by_owner(normed_two, shard_rows),
            by_owner(context, shard_rows),
        ],
        axis=2,
    )
    known = known.reshape(2, 2, 2, pick_total, -1)
    log_total = merged[0] + jnp.log(merged[1])
    core = links.place["c"]
    log_row = log_total[None]
    far_grads, to_core = head_grads(
        logits, log_row, table_low, target_column, base, 1 - core, count_all, block_size
    )
    from_core = links.swap(to_core, "c")
    own_grads, near_sum = head_grads(
        logits, log_row, table_low, target_column, base, core, count_all, block_size, from_core
    )
    own_rows = [
        lax.dynamic_slice_in_dim(head_rows, spot * far_grads.shape[0], far_grads.shape[0], 0)
        for spot in (1 - core, core)
    ]
    grad_near, unused = links.scatter_plane(
        near_sum.reshape(2, 2, links.depth, pick_total, model_width),
        known,
    )
    known = links.exchange_plane(after(known, grad_near))
    grad_picked, unused = links.scatter_depth(grad_near)

    grad_x_out, gain_last, shift_last = norm_backward(
        x_out, gain_entries[4], gain_entries[5], grad_picked
    )
    grad_mlp = grad_x_out.astype(bf16)
    unused, gelu_pull = jax.vjp(gelu_tanh, up_value)
    grad_up_low = gelu_pull(contract_cols(grad_mlp, down_weight))[0].astype(bf16)
    grad_parts = links.share_first(jnp.concatenate([grad_up_low, grad_mlp], axis=1))
    grad_x_attn, gain_two, shift_two = norm_backward(
        x_attn, gain_entries[2], gain_entries[3], contract_cols(grad_up_low, up_weight)
    )
    grad_x_attn = grad_x_out + grad_x_attn
    grad_attn_low = grad_x_attn.astype(bf16)
    grad_context = contract_cols(grad_attn_low, out_weight).astype(bf16)
    attn_parts = links.share_direct(grad_attn_low)
    grad_context = after(grad_context, *grad_parts)
    grad_parts = links.share_second(*grad_parts)
    grad_qkv_low = attend_backward(
        qkv_all, pick_rows, queries, probs, grad_context, micro_count
    )
    late = grad_qkv_low
    grad_x_one, gain_one, shift_one = norm_backward(
        x_embed, gain_entries[0], gain_entries[1], contract_cols(late, qkv_weight)
    )
    grad_x_embed = grad_x_one + lax.dot_general(
        pick_rows.astype(f32),
        grad_x_attn,
        (((0,), (0,)), ((), ())),
        precision=lax.Precision.HIGHEST,
        preferred_element_type=f32,
    )
    grad_embed_low = grad_x_embed.astype(bf16)
    sent = give(slot_first, grad_embed_low)
    returned = links.to_all(after(sent, known, *grad_parts, *attn_parts))
    half_place = jnp.arange(model_width // 2)
    half_row = half_place % shard_rows
    half_z = half_place // shard_rows % links.depth
    half_plane = half_place // shard_rows // links.depth

    def qkv_part(spot):
        source = ((half_z * 4 + half_plane) * 2 + spot) * shard_rows + half_row
        columns = (jnp.arange(model_width)[:, None] == source[None, :]).astype(bf16)
        return contract_rows(matmul(normed_one, columns).astype(bf16), grad_qkv_low)

    to_core = qkv_part(1 - core).astype(bf16)
    from_core = links.swap(to_core, "c")
    last_mine = (qkv_part(core) + from_core.astype(f32)).astype(bf16)
    last_near, last_sends = links.scatter_plane(
        last_mine.reshape(2, 2, links.depth, shard_rows, qkv_width), returned
    )
    down_near, up_near, out_near = plane_products(
        known,
        links.share_last(*[after(part, last_mine) for part in grad_parts]),
        links.share_last(after(jnp.stack(attn_parts), last_mine)),
        links.depth,
        (activated.shape[1], model_width),
    )

    last_near = jnp.concatenate([last_near, out_near], axis=-1)
    down_grad, down_send = links.scatter_depth(down_near, returned)
    up_grad, up_send = links.scatter_depth(up_near, returned)
    last_grad, unused = links.scatter_depth(last_near)
    qkv_grad, out_grad = last_grad[:, :qkv_width], last_grad[:, qkv_width:]
    far_grads = after(far_grads, returned, down_send, up_send, *last_sends)
    own_grads = after(own_grads, far_grads)
    table_head = contract_rows(far_grads[:, :block_size], own_rows[0]) + contract_rows(
        own_grads[:, :block_size], own_rows[1]
    )
    gain_one = after(gain_one, returned, down_send, up_send, *last_sends)
    gain_grads = jnp.stack(
        [gain_one, shift_one, gain_two, shift_two, gain_last, shift_last]
    ).reshape(6, devices, shard_rows)
    gain_grads = jnp.pad(
        gain_grads.transpose(1, 0, 2).reshape(devices, 6 * shard_rows),
        ((0, 0), (0, -6 * shard_rows % 128)),
    )
    gain_grad = jnp.sum(links.to_all(after(gain_grads, returned)), axis=0)[: 6 * shard_rows]
    gain_grad = gain_grad.reshape(6, shard_rows).T

    def more_grads(state):
        round_index, earlier_grad = state
        slot, asked = ask(round_index)
        returned_rows = links.to_all(give(slot, grad_embed_low))
        return (round_index + 1, earlier_grad + take(asked, returned_rows))

    unused_round, table_grad = lax.while_loop(
        lambda state: state[0] < rounds,
        more_grads,
        (
            jnp.ones((), jnp.int32),
            table_head + take(asked_first, after(returned, down_send, up_send, *last_sends)),
        ),
    )

    all_grads = (table_grad, qkv_grad, out_grad, up_grad, down_grad, gain_grad)
    firsts = (table_first_moment, first_qkv, first_out, first_up, first_down, first_norms)
    seconds = (table_second_moment, second_qkv, second_out, second_up, second_down, second_norms)
    totals = links.to_all(sum_squares(all_grads, weight_row, target_sum, devices))
    new_firsts, new_seconds, directions, update_rows = lamb_directions(
        totals, all_grads, firsts, seconds, masters
    )
    new_weights, facts = lamb_weights(totals, links.to_all(update_rows), directions, masters)
    return (
        (jnp.sum(log_total) - facts[4, 0]) / count_all,
        facts[3, 0],
        facts[:3, :6],
        *new_weights,
        *new_firsts,
        *new_seconds,
    )


def solution(mesh):
    rows = P(("wide", "narrow"), None)
    ids = P(None, ("wide", "narrow"), None)
    return jax.shard_map(
        per_device,
        mesh=mesh,
        in_specs=(ids,) * 3 + (rows,) * 18,
        out_specs=(P(),) * 3 + (rows,) * 18,
        check_vma=False,
    )
```

```python
import math

import jax
import jax.numpy as jnp
from jax import lax
from jax.experimental import pallas as pl
from jax.experimental.pallas import tpu as pltpu
from jax.sharding import PartitionSpec as P

HEAD_DIM = 64
VOCAB = 50257

neg_fill = -1e30
beta_first = 0.9
beta_second = 0.999
adam_epsilon = 1e-12
decay_rates = (0.01, 0.01, 0.01, 0.01, 0.01, 0.0)
learn_rate = 0.5
clip_limit = 0.01
norm_epsilon = 1e-05
step_count = 5.0
bf16 = jnp.bfloat16
f32 = jnp.float32


def layer_norm(values, gain_row, offset):
    centered = values - jnp.mean(values, axis=-1, keepdims=True)
    spread = jnp.mean(centered * centered, axis=-1, keepdims=True)
    return centered * lax.rsqrt(spread + norm_epsilon) * gain_row + offset


def norm_backward(values, gain_row, offset, grad_output):
    unused, pullback = jax.vjp(layer_norm, values, gain_row, offset)
    return pullback(grad_output)


def gelu_tanh(values):
    return jax.nn.gelu(values, approximate=True)


def matmul(left_side, right_side):
    return jnp.dot(left_side, right_side, preferred_element_type=f32)


def contract_rows(left_side, right_side):
    return lax.dot_general(
        left_side, right_side, (((0,), (0,)), ((), ())), preferred_element_type=f32
    )


def contract_cols(left_side, right_side):
    return lax.dot_general(
        left_side, right_side, (((1,), (1,)), ((), ())), preferred_element_type=f32
    )


class Links:
    def __init__(self):
        self.wide = lax.axis_size("wide")
        self.narrow = lax.axis_size("narrow")
        self.depth = self.wide // 2
        wide_place = lax.axis_index("wide")
        narrow_place = lax.axis_index("narrow")
        self.device = wide_place * self.narrow + narrow_place
        self.z = wide_place // 2
        self.place = {"x": wide_place % 2, "y": narrow_place // 2, "c": narrow_place % 2}

    def swap(self, values, axis):
        if axis == "x":
            return lax.ppermute(values, "wide", [(i, i ^ 1) for i in range(self.wide)])
        step = 2 if axis == "y" else 1
        return lax.ppermute(values, "narrow", [(i, i ^ step) for i in range(self.narrow)])

    def cross(self, values, step):
        return lax.ppermute(values, "wide", [(i, i ^ (2 * step)) for i in range(self.wide)])

    def exchange(self, values, combine):
        for step in (1, 2):
            other = lax.ppermute(values, "narrow", [(i, i ^ step) for i in range(self.narrow)])
            values = combine(values, other)
        step = 1
        while step < self.wide:
            other = lax.ppermute(values, "wide", [(i, i ^ step) for i in range(self.wide)])
            values = combine(values, other)
            step *= 2
        return values

    def to_all(self, values):
        return lax.all_to_all(values, ("wide", "narrow"), 0, 0, tiled=True)

    def gather_early(self, shard, *before):
        near = shard[None]
        for step in self.bits()[:0:-1]:
            near = jnp.concatenate([near, after(self.cross(near, step), *before)])
        return near

    def gather_late(self, near):
        return jnp.concatenate([near, self.cross(near, 1)])

    def gather_depth(self, shard):
        return self.gather_late(self.gather_early(shard))

    def bits(self):
        return [1 << number for number in range(self.depth.bit_length() - 1)]

    def steps(self):
        found = [0]
        for step in self.bits()[::-1]:
            found = found + [number ^ step for number in found]
        return found

    def plane_first(self, near):
        cut = halves(near.shape[-1])
        left, right = near[..., :cut], near[..., cut:]
        return left, right, self.swap(left, "x"), self.swap(right, "y")

    def plane_second(self, left, right, left_x, right_y):
        left, right = jnp.stack([left, left_x]), jnp.stack([right, right_y])
        return [left, self.swap(left, "y"), right, self.swap(right, "x")]

    def plane_core(self, pieces):
        return pieces + [self.swap(piece, "c") for piece in pieces]

    def gather_plane(self, near):
        return self.plane_core(self.plane_second(*self.plane_first(near)))

    def assemble(self, pieces, core_first=False, folded=None):
        depth = self.depth
        unused, unused_depth, rows, cut = pieces[0].shape
        count, fold = folded or (0, 0)
        width = cut + pieces[2].shape[3] - count * fold

        def kernel(place, *refs):
            sources, target = refs[: len(pieces)], refs[len(pieces)]
            x, y, c = place[0], place[1], place[2]
            for number, source in enumerate(sources):
                far_core, far, second = number // 4, number % 2, number // 2 % 2
                to_c = 1 - c if far_core else c
                columns = slice(cut, width) if second else slice(0, cut)
                for side in range(2):
                    across_x, across_y = (far, side) if second else (side, far)
                    to_x = 1 - x if across_x else x
                    to_y = 1 - y if across_y else y
                    if core_first:
                        target[to_c, to_x, to_y, 0, :, columns] = source[side, 0]
                    elif second:
                        target[0, to_x, to_y, to_c, :, columns] = source[side, 0, :, : width - cut]
                        for number_in in range(count):
                            start = width - cut + number_in * fold
                            refs[-1][
                                0, to_x, to_y, to_c, number_in * rows : (number_in + 1) * rows
                            ] = source[side, 0, :, start : start + fold]
                    else:
                        target[0, to_x, to_y, to_c, :, columns] = source[side, 0]

        place = [self.place["x"], self.place["y"], self.place["c"]]
        place = jnp.stack(place + [self.z ^ step for step in self.steps()]).astype(jnp.int32)
        if core_first:
            shape = (2, 2, 2, depth, rows, width)
            target_spec = pl.BlockSpec(
                (2, 2, 2, 1, rows, width), lambda k, place: (0, 0, 0, place[3 + k], 0, 0)
            )
        else:
            shape = (depth, 2, 2, 2, rows, width)
            target_spec = pl.BlockSpec(
                (1, 2, 2, 2, rows, width), lambda k, place: (place[3 + k], 0, 0, 0, 0, 0)
            )
        shapes, target_specs = [jax.ShapeDtypeStruct(shape, pieces[0].dtype)], [target_spec]
        if count:
            shapes.append(
                jax.ShapeDtypeStruct((depth, 2, 2, 2, count * rows, fold), pieces[0].dtype)
            )
            target_specs.append(
                pl.BlockSpec(
                    (1, 2, 2, 2, count * rows, fold),
                    lambda k, place: (place[3 + k], 0, 0, 0, 0, 0),
                )
            )
        wholes = pl.pallas_call(
            kernel,
            out_shape=shapes,
            grid_spec=pltpu.PrefetchScalarGridSpec(
                num_scalar_prefetch=1,
                grid=(depth,),
                in_specs=[
                    pl.BlockSpec((2, 1, rows, piece.shape[3]), lambda k, place: (0, k, 0, 0))
                    for piece in pieces
                ],
                out_specs=target_specs,
            ),
            compiler_params=pltpu.CompilerParams(vmem_limit_bytes=24 * 2**20),
            name="assemble",
        )(place, *pieces)
        wholes = [whole.reshape(-1, whole.shape[-1]) for whole in wholes]
        return wholes if count else wholes[0]

    def exchange_plane(self, values):
        for axis in "xyc":
            dim = " xyc".index(axis) - 1
            mine = lax.dynamic_index_in_dim(values, self.place[axis], dim, keepdims=False)
            other = lax.dynamic_index_in_dim(values, 1 - self.place[axis], dim, keepdims=False)
            values = jnp.stack([mine, self.swap(other, axis)], axis=dim)
        return values.transpose(2, 0, 1, 3, 4).reshape(-1, values.shape[-1])

    def share_direct(self, values):
        pairs = []
        for wide in range(self.wide):
            for narrow in range(self.narrow):
                pairs.append((wide * self.narrow + narrow, (wide ^ 1) * self.narrow + (narrow ^ 2)))
        across = lax.ppermute(values, ("wide", "narrow"), pairs)
        return [values, self.swap(values, "y"), self.swap(values, "x"), across]

    def share_first(self, values):
        cut = halves(values.shape[-1])
        left, right = values[:, :cut], values[:, cut:]
        return left, right, self.swap(left, "x"), self.swap(right, "y")

    def share_second(self, left, right, left_x, right_y):
        left, right = jnp.stack([left, left_x]), jnp.stack([right, right_y])
        return left, right, self.swap(left, "y"), self.swap(right, "x")

    def share_last(self, *pieces):
        return list(pieces) + [self.swap(piece, "c") for piece in pieces]

    def scatter_plane(self, full, *before_second):
        cut = halves(full.shape[-1])
        x, y = self.place["x"], self.place["y"]

        def pick(values, spot, dim):
            return lax.dynamic_index_in_dim(values, spot, dim, keepdims=False)

        left, right = full[..., :cut], full[..., cut:]
        from_x = self.swap(pick(left, 1 - x, 0), "x")
        from_y = self.swap(pick(right, 1 - y, 1), "y")
        left = (pick(left, x, 0).astype(f32) + from_x.astype(f32)).astype(bf16)
        right = (pick(right, y, 1).astype(f32) + from_y.astype(f32)).astype(bf16)
        left, right = after(left, *before_second), after(right, *before_second)
        sends = pick(left, 1 - y, 0), pick(right, 1 - x, 0)
        from_y, from_x = self.swap(sends[0], "y"), self.swap(sends[1], "x")
        left = pick(left, y, 0).astype(f32) + from_y.astype(f32)
        right = pick(right, x, 0).astype(f32) + from_x.astype(f32)
        return jnp.concatenate([left, right], axis=-1).astype(bf16), sends

    def scatter_depth(self, near, *before_last):
        for step in self.bits():
            if step == self.bits()[-1]:
                near = after(near, *before_last)
            pairs = near.reshape((-1, 2) + near.shape[1:])
            bit = self.z // step % 2
            other = lax.dynamic_index_in_dim(pairs, 1 - bit, 1, keepdims=False)
            mine = lax.dynamic_index_in_dim(pairs, bit, 1, keepdims=False)
            send = other.astype(bf16)
            near = mine.astype(f32) + self.cross(send, step).astype(f32)
        return near[0], send


def halves(width):
    return width // 256 * 128


def tie(*values):
    return lax.optimization_barrier(values)


def after(values, *others):
    return lax.optimization_barrier((values, *others))[0]


def lane_halves(values, first):
    lane = lax.broadcasted_iota(jnp.int32, values.shape, 1)
    return jnp.where((lane < HEAD_DIM) == first, values, jnp.zeros_like(values))


def attend(qkv_all, pick_rows, allowed, micro_count):
    token_count = qkv_all.shape[0]
    width = qkv_all.shape[1] // 3
    pick_total = pick_rows.shape[0]
    length, picked = token_count // micro_count, pick_total // micro_count
    pair = 2 * HEAD_DIM
    scale = HEAD_DIM ** (-0.5)

    def kernel(qkv_ref, pick_ref, allowed_ref, context_ref, query_ref, prob_ref):
        query_ref[...] = jnp.dot(
            pick_ref[...], qkv_ref[:, :width], preferred_element_type=f32
        ).astype(bf16)
        for micro in range(micro_count):
            rows = slice(micro * picked, (micro + 1) * picked)
            keep = allowed_ref[rows] > 0.5
            keep = jnp.concatenate([keep, keep], axis=0)
            for number in range(width // pair):
                columns = slice(number * pair, (number + 1) * pair)
                keys = qkv_ref[
                    micro * length : (micro + 1) * length,
                    width + number * pair : width + (number + 1) * pair,
                ]
                values = qkv_ref[
                    micro * length : (micro + 1) * length,
                    2 * width + number * pair : 2 * width + (number + 1) * pair,
                ]
                query = query_ref[rows, columns]
                both = jnp.concatenate(
                    [lane_halves(query, True), lane_halves(query, False)], axis=0
                )
                scores = contract_cols(both, keys) * scale
                scores = jnp.where(keep, scores, neg_fill)
                shifted = jnp.exp(scores - jnp.max(scores, axis=1, keepdims=True))
                probs = shifted / jnp.sum(shifted, axis=1, keepdims=True)
                prob_ref[micro, number] = probs
                mixed = jnp.dot(probs.astype(bf16), values, preferred_element_type=f32)
                context_ref[rows, columns] = (
                    lane_halves(mixed[:picked], True) + lane_halves(mixed[picked:], False)
                ).astype(bf16)

    return pl.pallas_call(
        kernel,
        out_shape=(
            jax.ShapeDtypeStruct((pick_total, width), bf16),
            jax.ShapeDtypeStruct((pick_total, width), bf16),
            jax.ShapeDtypeStruct((micro_count, width // pair, 2 * picked, length), f32),
        ),
        compiler_params=pltpu.CompilerParams(vmem_limit_bytes=32 * 2**20),
        name="attend",
    )(qkv_all, pick_rows, allowed)


def attend_backward(qkv_all, pick_rows, query_all, probs_all, grad_context, micro_count):
    token_count = qkv_all.shape[0]
    width = qkv_all.shape[1] // 3
    pick_total = pick_rows.shape[0]
    length, picked = token_count // micro_count, pick_total // micro_count
    pair = 2 * HEAD_DIM
    scale = HEAD_DIM ** (-0.5)

    def kernel(qkv_ref, pick_ref, query_ref, prob_ref, grad_ref, out_ref, query_grad_ref):
        for micro in range(micro_count):
            rows = slice(micro * picked, (micro + 1) * picked)
            tokens = slice(micro * length, (micro + 1) * length)
            for number in range(width // pair):
                columns = slice(number * pair, (number + 1) * pair)
                key_columns = slice(width + number * pair, width + (number + 1) * pair)
                value_columns = slice(2 * width + number * pair, 2 * width + (number + 1) * pair)
                query, grad = query_ref[rows, columns], grad_ref[rows, columns]
                queries = jnp.concatenate(
                    [lane_halves(query, True), lane_halves(query, False)], axis=0
                )
                grads = jnp.concatenate(
                    [lane_halves(grad, True), lane_halves(grad, False)], axis=0
                )
                probs = prob_ref[micro, number]
                grad_probs = contract_cols(grads, qkv_ref[tokens, value_columns])
                inner = jnp.sum(probs * grad_probs, axis=1, keepdims=True)
                grad_scores = (probs * (grad_probs - inner)).astype(bf16)
                mixed = (
                    jnp.dot(
                        grad_scores, qkv_ref[tokens, key_columns], preferred_element_type=f32
                    )
                    * scale
                )
                query_grad_ref[rows, columns] = (
                    lane_halves(mixed[:picked], True) + lane_halves(mixed[picked:], False)
                ).astype(bf16)
                out_ref[tokens, key_columns] = (
                    contract_rows(grad_scores, queries) * scale
                ).astype(bf16)
                out_ref[tokens, value_columns] = contract_rows(probs.astype(bf16), grads).astype(
                    bf16
                )
        out_ref[:, :width] = contract_rows(pick_ref[...], query_grad_ref[...]).astype(bf16)

    return pl.pallas_call(
        kernel,
        out_shape=jax.ShapeDtypeStruct(qkv_all.shape, bf16),
        scratch_shapes=[pltpu.VMEM((pick_total, width), bf16)],
        compiler_params=pltpu.CompilerParams(vmem_limit_bytes=32 * 2**20),
        name="attend_backward",
    )(qkv_all, pick_rows, query_all, probs_all, grad_context)


def plane_products(known, grads, attn_grads, depth, widths):
    hidden, model = widths
    rows = grads[0].shape[-2]
    width = hidden + 2 * model
    down_rows, model_rows = hidden // (8 * depth), model // (8 * depth)
    down_width, model_width = hidden // 8, model // 8

    def kernel(known_ref, *refs):
        down_ref, up_ref, out_ref, grads_ref = refs[10:]
        cut = grads[0].shape[-1]
        for far_core in range(2):
            left, right, left_y, right_x = refs[4 * far_core : 4 * far_core + 4]
            attn = refs[8 + far_core]
            for x in range(2):
                for y in range(2):
                    spot = pl.ds(((far_core * 2 + x) * 2 + y) * rows, rows)
                    grads_ref[spot, :cut] = (left_y if y else left)[x]
                    grads_ref[spot, cut : hidden + model] = (right_x if x else right)[y]
                    grads_ref[spot, hidden + model :] = attn[2 * x + y]
        down_ref[...] = contract_rows(
            known_ref[:, :down_width], grads_ref[:, hidden : hidden + model]
        ).astype(bf16)
        up_ref[...] = contract_rows(
            known_ref[:, down_width : down_width + model_width], grads_ref[:, :hidden]
        ).astype(bf16)
        out_ref[...] = contract_rows(
            known_ref[:, down_width + model_width :], grads_ref[:, hidden + model :]
        ).astype(bf16)

    in_vmem = pl.BlockSpec(memory_space=pltpu.VMEM)
    down, up, out = pl.pallas_call(
        kernel,
        in_specs=[in_vmem] * 11,
        out_shape=(
            jax.ShapeDtypeStruct((depth * down_rows, model), bf16),
            jax.ShapeDtypeStruct((depth * model_rows, hidden), bf16),
            jax.ShapeDtypeStruct((depth * model_rows, model), bf16),
        ),
        scratch_shapes=[
            pltpu.VMEM((8 * rows, width), bf16),
        ],
        compiler_params=pltpu.CompilerParams(vmem_limit_bytes=48 * 2**20),
        name="plane_products",
    )(known, *grads, *attn_grads)
    return (
        down.reshape(depth, down_rows, model),
        up.reshape(depth, model_rows, hidden),
        out.reshape(depth, model_rows, model),
    )


def on_lane(place, value):
    lane = lax.broadcasted_iota(jnp.int32, (1, 128), 1)
    return jnp.where(lane == place, value, 0.0)


def whole_sum(values):
    return jnp.sum(jnp.sum(values, axis=0, keepdims=True), axis=1, keepdims=True)


def sum_squares(all_grads, weight_row, target_sum, devices):
    def kernel(table_ref, target_ref, weight_ref, *refs):
        grads, rows_ref = refs[:-1], refs[-1]
        row = on_lane(0, table_ref[...])
        for place, grad in enumerate(grads):
            row = row + on_lane(place + 1, whole_sum(grad[...] * grad[...]))
        rows_ref[:, :128] = jnp.broadcast_to(row, (devices, 128))
        rows_ref[:, 128:] = jnp.broadcast_to(
            weight_ref[...] + on_lane(64, target_ref[...]), (devices, 128)
        )

    table_square = jnp.sum(all_grads[0] * all_grads[0]).reshape(1, 1)
    return pl.pallas_call(
        kernel,
        out_shape=jax.ShapeDtypeStruct((devices, 256), f32),
        name="sum_squares",
    )(table_square, target_sum.reshape(1, 1), weight_row, *all_grads[1:])


grid_steps = 4


def unfold(whole, count, width, shard_rows):
    devices = whole.shape[0] // shard_rows
    group = max(1, min(devices, 256 // shard_rows))

    def kernel(source_ref, target_ref):
        for number in range(count):
            block = source_ref[:, number * width : (number + 1) * width]
            target_ref[:, number] = block.reshape(group, shard_rows, width)

    rows = pl.pallas_call(
        kernel,
        grid=(devices // group,),
        in_specs=[pl.BlockSpec((group * shard_rows, count * width), lambda i: (i, 0))],
        out_specs=pl.BlockSpec((group, count, shard_rows, width), lambda i: (i, 0, 0, 0)),
        out_shape=jax.ShapeDtypeStruct((devices, count, shard_rows, width), whole.dtype),
        compiler_params=pltpu.CompilerParams(vmem_limit_bytes=32 * 2**20),
        name="unfold",
    )(whole)
    return rows.reshape(-1, width)


row_block = 256


def head_logits(head_rows, table_low, targets, base, block_size):
    row_count, width = head_rows.shape
    columns = table_low.shape[0]
    block = min(row_block, row_count)

    def kernel(base_ref, rows_ref, table_ref, targets_ref, logits_ref, top_ref, sum_ref, hit_ref):
        step = pl.program_id(0)
        place = lax.broadcasted_iota(jnp.int32, (1, columns), 1)
        column = jnp.where(place < block_size, place + base_ref[0], VOCAB)
        fill = jnp.where(column < VOCAB, 0.0, neg_fill)
        logits = contract_cols(rows_ref[...], table_ref[...]) + fill
        logits_ref[...] = logits
        top = jnp.max(logits, axis=1, keepdims=True)
        total = jnp.sum(jnp.exp(logits - top), axis=1, keepdims=True)
        top_ref[...] = jnp.broadcast_to(top, (block, 128)).T[:1]
        sum_ref[...] = jnp.broadcast_to(total, (block, 128)).T[:1]

        @pl.when(step == 0)
        def _():
            hit_ref[...] = jnp.zeros_like(hit_ref)

        hits = targets_ref[...] == column
        hit_ref[...] += jnp.broadcast_to(whole_sum(jnp.where(hits, logits, 0.0)), (1, 128))

    return pl.pallas_call(
        kernel,
        out_shape=(
            jax.ShapeDtypeStruct((row_count, columns), f32),
            jax.ShapeDtypeStruct((1, row_count), f32),
            jax.ShapeDtypeStruct((1, row_count), f32),
            jax.ShapeDtypeStruct((1, 128), f32),
        ),
        grid=(row_count // block,),
        in_specs=[
            pl.BlockSpec(memory_space=pltpu.SMEM),
            pl.BlockSpec((block, width), lambda k: (k, 0)),
            pl.BlockSpec((columns, width), lambda k: (0, 0)),
            pl.BlockSpec((block, 1), lambda k: (k, 0)),
        ],
        out_specs=(
            pl.BlockSpec((block, columns), lambda k: (k, 0)),
            pl.BlockSpec((1, block), lambda k: (0, k)),
            pl.BlockSpec((1, block), lambda k: (0, k)),
            pl.BlockSpec((1, 128), lambda k: (0, 0)),
        ),
        compiler_params=pltpu.CompilerParams(vmem_limit_bytes=56 * 2**20),
        name="head_logits",
    )(base.reshape(1), head_rows, table_low, targets)


def head_grads(logits, log_total, table_low, targets, base, half, count_all, block_size, add=None):
    row_count, columns = logits.shape
    width = table_low.shape[1]
    block = min(row_block, row_count // 2)
    steps = row_count // 2 // block
    scale = 1.0 / count_all

    def kernel(place_ref, logits_ref, total_ref, table_ref, targets_ref, *refs):
        grads_ref, out_ref = refs[-2:]
        place = lax.broadcasted_iota(jnp.int32, (1, columns), 1)
        column = jnp.where(place < block_size, place + place_ref[1], VOCAB)
        total = jnp.broadcast_to(total_ref[...], (128, block)).T[:, :1]
        hits = targets_ref[...] == column
        probs = jnp.exp(logits_ref[...] - total)
        grads = ((probs - jnp.where(hits, 1.0, 0.0)) * scale).astype(bf16)
        grads_ref[...] = grads
        product = matmul(grads, table_ref[...])
        if add is not None:
            product = product + refs[0][...].astype(f32)
        out_ref[...] = product.astype(bf16)

    half_spec = pl.BlockSpec((block, width), lambda k, place: (k, 0))
    return pl.pallas_call(
        kernel,
        out_shape=(
            jax.ShapeDtypeStruct((row_count // 2, columns), bf16),
            jax.ShapeDtypeStruct((row_count // 2, width), bf16),
        ),
        grid_spec=pltpu.PrefetchScalarGridSpec(
            num_scalar_prefetch=1,
            grid=(steps,),
            in_specs=[
                pl.BlockSpec((block, columns), lambda k, place: (place[0] * steps + k, 0)),
                pl.BlockSpec((1, block), lambda k, place: (0, place[0] * steps + k)),
                pl.BlockSpec((columns, width), lambda k, place: (0, 0)),
                pl.BlockSpec((block, 1), lambda k, place: (place[0] * steps + k, 0)),
            ]
            + ([] if add is None else [half_spec]),
            out_specs=(
                pl.BlockSpec((block, columns), lambda k, place: (k, 0)),
                half_spec,
            ),
        ),
        compiler_params=pltpu.CompilerParams(vmem_limit_bytes=56 * 2**20),
        name="head_grads",
    )(
        jnp.stack([half, base]).astype(jnp.int32),
        logits,
        log_total,
        table_low,
        targets,
        *(() if add is None else (add,)),
    )


def weight_squares(masters):
    table_rows = -(-masters[0].shape[0] // (8 * grid_steps)) * 8
    table_count = masters[0].shape[0]

    def kernel(table_ref, *refs):
        others, row_ref = refs[:-1], refs[-1]
        step = pl.program_id(0)

        @pl.when(step == 0)
        def _():
            row = jnp.zeros((1, 128), f32)
            for place, other in enumerate(others):
                row = row + on_lane(place + 1, whole_sum(other[...] * other[...]))
            row_ref[...] = row

        place = step * table_rows + lax.broadcasted_iota(jnp.int32, (table_rows, 1), 0)
        square = jnp.where(place < table_count, table_ref[...] * table_ref[...], 0.0)
        row_ref[...] += on_lane(0, whole_sum(square))

    return pl.pallas_call(
        kernel,
        grid=(grid_steps,),
        in_specs=[pl.BlockSpec((table_rows, masters[0].shape[1]), lambda k: (k, 0))]
        + [
            pl.BlockSpec(array.shape, lambda k: (0, 0), pipeline_mode=pl.Buffered(1))
            for array in masters[1:]
        ],
        out_specs=pl.BlockSpec((1, 128), lambda k: (0, 0)),
        out_shape=jax.ShapeDtypeStruct((1, 128), f32),
        compiler_params=pltpu.CompilerParams(vmem_limit_bytes=32 * 2**20),
        name="weight_squares",
    )(*masters)


def group_specs(arrays):
    table_rows = -(-arrays[0].shape[0] // (8 * grid_steps)) * 8
    specs = [pl.BlockSpec((table_rows, arrays[0].shape[1]), lambda k: (k, 0))]
    for array in arrays[1:5]:
        rows, width = array.shape
        specs.append(pl.BlockSpec((rows, width // grid_steps), lambda k: (0, k)))
    specs.append(pl.BlockSpec(arrays[5].shape, lambda k: (0, 0)))
    return specs


def lamb_directions(totals, all_grads, firsts, seconds, masters):
    devices = totals.shape[0]
    table_count = all_grads[0].shape[0]
    specs = group_specs(all_grads)
    table_rows = specs[0].block_shape[0]
    first_scale = 1.0 / (1.0 - beta_first**step_count)
    second_scale = 1.0 / (1.0 - beta_second**step_count)

    def kernel(totals_ref, *refs):
        grads, olds, squares, weights = refs[:6], refs[6:12], refs[12:18], refs[18:24]
        new_olds, new_squares, directions, rows_ref = refs[24:30], refs[30:36], refs[36:42], refs[42]
        step = pl.program_id(0)
        grad_total = jnp.sum(totals_ref[:, :128], axis=0, keepdims=True)
        factor = jnp.minimum(
            1.0, clip_limit * lax.rsqrt(jnp.sum(grad_total, axis=1, keepdims=True))
        )

        @pl.when(step == 0)
        def _():
            rows_ref[...] = jnp.zeros_like(rows_ref)

        def update(group, rows, live=None):
            clipped = factor * grads[group][rows]
            new_old = beta_first * olds[group][rows] + (1.0 - beta_first) * clipped
            new_square = beta_second * squares[group][rows] + (1.0 - beta_second) * clipped * clipped
            direction = (new_old * first_scale) / (
                jnp.sqrt(new_square * second_scale) + adam_epsilon
            ) + decay_rates[group] * weights[group][rows]
            new_olds[group][rows] = new_old
            new_squares[group][rows] = new_square
            directions[group][rows] = direction
            square = direction * direction
            return square if live is None else jnp.where(live, square, 0.0)

        def table_part(part, total):
            rows = pl.ds(pl.multiple_of(part * 8, 8), 8)
            place = step * table_rows + part * 8 + lax.broadcasted_iota(
                jnp.int32, (8, 1), 0
            )
            return total + update(0, (rows, slice(None)), place < table_count)

        table_total = lax.fori_loop(
            0, table_rows // 8, table_part, jnp.zeros((8, all_grads[0].shape[1]), f32)
        )
        row = on_lane(0, whole_sum(table_total))
        for group in range(1, 5):
            row = row + on_lane(group, whole_sum(update(group, (slice(None), slice(None)))))
        rows_ref[...] += jnp.broadcast_to(row, rows_ref.shape)

        @pl.when(step == 0)
        def _():
            row = on_lane(5, whole_sum(update(5, (slice(None), slice(None)))))
            rows_ref[...] += jnp.broadcast_to(row, rows_ref.shape)

    shapes = [jax.ShapeDtypeStruct(array.shape, f32) for array in all_grads]
    results = pl.pallas_call(
        kernel,
        grid=(grid_steps,),
        in_specs=[pl.BlockSpec(totals.shape, lambda k: (0, 0))] + specs * 4,
        out_specs=specs * 3 + [pl.BlockSpec((devices, 128), lambda k: (0, 0))],
        out_shape=shapes * 3 + [jax.ShapeDtypeStruct((devices, 128), f32)],
        compiler_params=pltpu.CompilerParams(vmem_limit_bytes=56 * 2**20),
        name="lamb_directions",
    )(totals, *all_grads, *firsts, *seconds, *masters)
    return results[:6], results[6:12], results[12:18], results[18]


def lamb_weights(totals, update_rows, directions, masters):
    specs = group_specs(masters)

    def kernel(totals_ref, updates_ref, *refs):
        moves, weights, news, facts_ref = refs[:6], refs[6:12], refs[12:18], refs[18]
        step = pl.program_id(0)
        lane = lax.broadcasted_iota(jnp.int32, (1, 128), 1)
        grad_total = jnp.sum(totals_ref[:, :128], axis=0, keepdims=True)
        weight_total = jnp.sum(totals_ref[:, 128:], axis=0, keepdims=True)
        update_total = jnp.sum(updates_ref[...], axis=0, keepdims=True)
        weight_norms = jnp.where(lane < 6, jnp.sqrt(jnp.maximum(weight_total, 0.0)), 0.0)
        update_norms = jnp.where(lane < 6, jnp.sqrt(update_total), 1.0)
        rates = learn_rate * weight_norms / update_norms
        for group in range(5):
            rate = jnp.sum(jnp.where(lane == group, rates, 0.0), axis=1, keepdims=True)
            news[group][...] = weights[group][...] - rate * moves[group][...]

        @pl.when(step == 0)
        def _():
            rate = jnp.sum(jnp.where(lane == 5, rates, 0.0), axis=1, keepdims=True)
            news[5][...] = weights[5][...] - rate * moves[5][...]
            grad_norm = jnp.sqrt(jnp.sum(grad_total, axis=1, keepdims=True))
            factor = jnp.minimum(1.0, clip_limit / grad_norm)
            target = jnp.sum(jnp.where(lane == 64, weight_total, 0.0), axis=1, keepdims=True)
            facts_ref[0:1] = factor * jnp.sqrt(grad_total)
            facts_ref[1:2] = weight_norms
            facts_ref[2:3] = update_norms
            facts_ref[3:4] = jnp.broadcast_to(grad_norm, (1, 128))
            facts_ref[4:5] = jnp.broadcast_to(target, (1, 128))

    results = pl.pallas_call(
        kernel,
        grid=(grid_steps,),
        in_specs=[
            pl.BlockSpec(totals.shape, lambda k: (0, 0)),
            pl.BlockSpec(update_rows.shape, lambda k: (0, 0)),
        ]
        + specs * 2,
        out_specs=specs + [pl.BlockSpec((8, 128), lambda k: (0, 0))],
        out_shape=[jax.ShapeDtypeStruct(array.shape, f32) for array in masters]
        + [jax.ShapeDtypeStruct((8, 128), f32)],
        compiler_params=pltpu.CompilerParams(vmem_limit_bytes=56 * 2**20),
        name="lamb_weights",
    )(totals, update_rows, *directions, *masters)
    return results[:6], results[6]


def per_device(
    token_ids,
    doc_ids,
    loss_positions,
    tied_table_master,
    qkv_master,
    out_master,
    up_master,
    down_master,
    norm_master,
    table_first_moment,
    first_qkv,
    first_out,
    first_up,
    first_down,
    first_norms,
    table_second_moment,
    second_qkv,
    second_out,
    second_up,
    second_down,
    second_norms,
):
    links = Links()
    devices = links.wide * links.narrow
    micro_count, unused, length = token_ids.shape
    picked_count = loss_positions.shape[2]
    token_count = micro_count * length
    pick_total = micro_count * picked_count
    model_width = tied_table_master.shape[1]
    head_count = model_width // HEAD_DIM
    block_size = tied_table_master.shape[0]
    count_all = devices * pick_total
    shard_rows = qkv_master.shape[0]

    tokens = token_ids.reshape(token_count)
    picks = loss_positions.reshape(micro_count, picked_count)
    documents = doc_ids.reshape(micro_count, length)
    mean_load = token_count / devices
    slots = int(math.ceil((mean_load + 6.0 * math.sqrt(mean_load)) / 8.0)) * 8
    owner = tokens // block_size
    local_row = tokens % block_size
    token_place = jnp.arange(token_count)
    earlier = (owner[:, None] == owner[None, :]) & (token_place[None, :] < token_place[:, None])
    rank = jnp.sum(earlier.astype(jnp.int32), axis=1)
    most = jnp.max(rank) + 1
    slot_place = jnp.arange(devices * slots)
    line = -(-(slots + 1 + pick_total) // 128) * 128

    pick_hits = picks[:, :, None] == jnp.arange(length)[None, None, :]
    next_hits = picks[:, :, None] + 1 == jnp.arange(length)[None, None, :]
    own_targets = jnp.sum(
        jnp.where(next_hits, token_ids.reshape(micro_count, 1, length), 0), axis=2
    ).reshape(-1)
    pick_docs = jnp.sum(jnp.where(pick_hits, documents[:, None, :], 0), axis=2)

    def slot_of(round_index):
        inside = (rank >= round_index * slots) & (rank < (round_index + 1) * slots)
        return jnp.where(inside, owner * slots + rank - round_index * slots, -1)

    def message_of(slot):
        wanted = jnp.sum(
            jnp.where(slot[None, :] == slot_place[:, None], local_row[None, :] + 1, 0), axis=1
        ) - 1
        wanted = wanted.reshape(devices, slots)
        return jnp.concatenate(
            [
                wanted,
                jnp.broadcast_to(most, (devices, 1)),
                jnp.broadcast_to(own_targets[None, :], (devices, pick_total)),
                jnp.zeros((devices, line - slots - 1 - pick_total), jnp.int32),
            ],
            axis=1,
        )

    def ask(round_index):
        slot = slot_of(round_index)
        return slot, links.to_all(message_of(slot))[:, :slots].reshape(-1)

    def find(asked):
        row_hits = (asked[:, None] == jnp.arange(padded_rows)[None, :]).astype(bf16)
        return matmul(row_hits, table_low).astype(bf16)

    def place_rows(slot, landed):
        token_hits = (slot[:, None] == slot_place[None, :]).astype(bf16)
        return matmul(token_hits, landed).astype(bf16)

    def give(slot, grad_low):
        token_hits = (slot[:, None] == slot_place[None, :]).astype(bf16)
        return contract_rows(token_hits, grad_low).astype(bf16)

    def take(asked, landed):
        row_hits = (asked[None, :] == jnp.arange(block_size)[:, None]).astype(bf16)
        return matmul(row_hits, landed)

    gain_width = 128
    qkv_width = qkv_master.shape[1]
    gain_shard = jnp.pad(norm_master, ((0, 0), (0, gain_width - norm_master.shape[1])))
    slot_first = slot_of(0)
    masters = (tied_table_master, qkv_master, out_master, up_master, down_master, norm_master)
    first_shard = jnp.concatenate([qkv_master, gain_shard], axis=1).astype(bf16)
    first_early = links.gather_early(first_shard)
    first_near = links.gather_late(first_early)
    message = message_of(slot_first)
    answer = links.to_all(message)
    padded_rows = -(-block_size // 128) * 128
    table_low = jnp.pad(
        after(tied_table_master, message), ((0, padded_rows - block_size), (0, 0))
    ).astype(bf16)
    asked_first = answer[:, :slots].reshape(-1)
    rounds = (jnp.max(answer[:, slots]) + slots - 1) // slots
    targets = answer[:, slots + 1 : slots + 1 + pick_total]
    targets = targets.reshape(links.depth, 2, 2, 2, pick_total).transpose(3, 1, 2, 0, 4).reshape(-1)
    fold_count = down_master.shape[0] // shard_rows
    second_shard = jnp.concatenate(
        [
            down_master[number * shard_rows : (number + 1) * shard_rows]
            for number in range(fold_count)
        ]
        + [up_master, out_master],
        axis=1,
    )
    second_whole = lax.all_gather(
        second_shard.astype(bf16), ("wide", "narrow"), axis=0, tiled=True
    )
    first_parts = links.plane_first(first_near)
    found = after(find(asked_first), first_near)
    landed = links.to_all(found)
    first_pieces = links.plane_second(*first_parts)
    weight_row = weight_squares(tie(*masters, found)[:6])
    first_pieces[0] = after(first_pieces[0], weight_row, table_low)
    first_whole = links.assemble(links.plane_core(first_pieces))
    qkv_weight = first_whole[:, :qkv_width]
    gain_entries = first_whole[:, qkv_width : qkv_width + 6].astype(f32).T

    def more_rows(state):
        round_index, embedded = state
        slot, asked = ask(round_index)
        return (round_index + 1, embedded + place_rows(slot, links.to_all(find(asked))))

    unused_round, x_low = lax.while_loop(
        lambda state: state[0] < rounds,
        more_rows,
        (jnp.ones((), jnp.int32), place_rows(slot_first, landed)),
    )

    x_embed = x_low.astype(f32)
    normed_one = layer_norm(x_embed, gain_entries[0], gain_entries[1]).astype(bf16)
    qkv_all = matmul(normed_one, qkv_weight).astype(bf16)
    pick_rows = (
        pick_hits[:, :, None, :] & jnp.eye(micro_count, dtype=bool)[:, None, :, None]
    ).reshape(pick_total, token_count).astype(bf16)
    x_embed_picked = matmul(pick_rows, x_low)
    allowed = (jnp.arange(length)[None, None, :] <= picks[:, :, None]) & (
        documents[:, None, :] == pick_docs[:, :, None]
    )
    context, queries, probs = attend(
        qkv_all, pick_rows, allowed.reshape(pick_total, length).astype(f32), micro_count
    )
    down_weight = unfold(second_whole, fold_count, model_width, shard_rows)
    hidden = up_master.shape[1]
    folded = fold_count * model_width
    up_weight = second_whole[:, folded : folded + hidden]
    out_weight = second_whole[:, folded + hidden :]
    x_attn = x_embed_picked + matmul(context, out_weight)
    normed_two = layer_norm(x_attn, gain_entries[2], gain_entries[3]).astype(bf16)
    up_value = matmul(normed_two, up_weight)
    activated = gelu_tanh(up_value).astype(bf16)
    x_out = x_attn + matmul(activated, down_weight)
    picked_low = layer_norm(x_out, gain_entries[4], gain_entries[5]).astype(bf16)

    head_pieces = links.plane_second(*links.plane_first(links.gather_depth(picked_low)))
    head_rows = links.assemble(
        links.plane_core(head_pieces), core_first=True
    )
    base = links.device * block_size
    target_column = targets[:, None]
    logits, local_top, local_sum, target_sum = head_logits(
        head_rows, table_low, target_column, base, block_size
    )
    target_sum = target_sum[:, :1]

    def merge_totals(first, second):
        top = jnp.maximum(first[0], second[0])
        total = first[1] * jnp.exp(first[0] - top) + second[1] * jnp.exp(second[0] - top)
        return jnp.stack([top, total])

    merged = links.exchange(jnp.concatenate([local_top, local_sum]), merge_totals)
    def by_owner(values, block_rows):
        if block_rows % 128 == 0:
            blocks = values.reshape(pick_total, links.depth, 8, block_rows)
            blocks = blocks.transpose(2, 0, 1, 3).reshape(8 * pick_total, -1)
            return blocks.reshape(8, pick_total, -1)
        count = values.shape[1]
        place = jnp.arange(count)
        source = place % (count // 8) // block_rows * 8 + place // (count // 8)
        source = source * block_rows + place % block_rows
        order = (jnp.arange(count)[:, None] == source[None, :]).astype(bf16)
        ordered = matmul(values, order).astype(bf16)
        return ordered.reshape(pick_total, 8, count // 8).transpose(1, 0, 2)

    known = jnp.concatenate(
        [
            by_owner(activated, down_master.shape[0]),
            by_owner(normed_two, shard_rows),
            by_owner(context, shard_rows),
        ],
        axis=2,
    )
    known = known.reshape(2, 2, 2, pick_total, -1)
    log_total = merged[0] + jnp.log(merged[1])
    core = links.place["c"]
    log_row = log_total[None]
    far_grads, to_core = head_grads(
        logits, log_row, table_low, target_column, base, 1 - core, count_all, block_size
    )
    from_core = links.swap(to_core, "c")
    own_grads, near_sum = head_grads(
        logits, log_row, table_low, target_column, base, core, count_all, block_size, from_core
    )
    own_rows = [
        lax.dynamic_slice_in_dim(head_rows, spot * far_grads.shape[0], far_grads.shape[0], 0)
        for spot in (1 - core, core)
    ]
    grad_near, unused = links.scatter_plane(
        near_sum.reshape(2, 2, links.depth, pick_total, model_width),
        known,
    )
    known = links.exchange_plane(after(known, grad_near))
    grad_picked, unused = links.scatter_depth(grad_near)

    grad_x_out, gain_last, shift_last = norm_backward(
        x_out, gain_entries[4], gain_entries[5], grad_picked
    )
    grad_mlp = grad_x_out.astype(bf16)
    unused, gelu_pull = jax.vjp(gelu_tanh, up_value)
    grad_up_low = gelu_pull(contract_cols(grad_mlp, down_weight))[0].astype(bf16)
    grad_parts = links.share_first(jnp.concatenate([grad_up_low, grad_mlp], axis=1))
    grad_x_attn, gain_two, shift_two = norm_backward(
        x_attn, gain_entries[2], gain_entries[3], contract_cols(grad_up_low, up_weight)
    )
    grad_x_attn = grad_x_out + grad_x_attn
    grad_attn_low = grad_x_attn.astype(bf16)
    grad_context = contract_cols(grad_attn_low, out_weight).astype(bf16)
    attn_parts = links.share_direct(grad_attn_low)
    grad_context = after(grad_context, *grad_parts)
    grad_parts = links.share_second(*grad_parts)
    grad_qkv_low = attend_backward(
        qkv_all, pick_rows, queries, probs, grad_context, micro_count
    )
    late = grad_qkv_low
    grad_x_one, gain_one, shift_one = norm_backward(
        x_embed, gain_entries[0], gain_entries[1], contract_cols(late, qkv_weight)
    )
    grad_x_embed = grad_x_one + lax.dot_general(
        pick_rows.astype(f32),
        grad_x_attn,
        (((0,), (0,)), ((), ())),
        precision=lax.Precision.HIGHEST,
        preferred_element_type=f32,
    )
    grad_embed_low = grad_x_embed.astype(bf16)
    sent = give(slot_first, grad_embed_low)
    returned = links.to_all(after(sent, known, *grad_parts, *attn_parts))
    half_place = jnp.arange(model_width // 2)
    half_row = half_place % shard_rows
    half_z = half_place // shard_rows % links.depth
    half_plane = half_place // shard_rows // links.depth

    def qkv_part(spot):
        source = ((half_z * 4 + half_plane) * 2 + spot) * shard_rows + half_row
        columns = (jnp.arange(model_width)[:, None] == source[None, :]).astype(bf16)
        return contract_rows(matmul(normed_one, columns).astype(bf16), grad_qkv_low)

    to_core = qkv_part(1 - core).astype(bf16)
    from_core = links.swap(to_core, "c")
    last_mine = (qkv_part(core) + from_core.astype(f32)).astype(bf16)
    last_near, last_sends = links.scatter_plane(
        last_mine.reshape(2, 2, links.depth, shard_rows, qkv_width), returned
    )
    down_near, up_near, out_near = plane_products(
        known,
        links.share_last(*[after(part, last_mine) for part in grad_parts]),
        links.share_last(after(jnp.stack(attn_parts), last_mine)),
        links.depth,
        (activated.shape[1], model_width),
    )

    last_near = jnp.concatenate([last_near, out_near], axis=-1)
    down_grad, down_send = links.scatter_depth(down_near, returned)
    up_grad, up_send = links.scatter_depth(up_near, returned)
    last_grad, unused = links.scatter_depth(last_near)
    qkv_grad, out_grad = last_grad[:, :qkv_width], last_grad[:, qkv_width:]
    far_grads = after(far_grads, returned, down_send, up_send, *last_sends)
    own_grads = after(own_grads, far_grads)
    table_head = contract_rows(far_grads[:, :block_size], own_rows[0]) + contract_rows(
        own_grads[:, :block_size], own_rows[1]
    )
    gain_one = after(gain_one, returned, down_send, up_send, *last_sends)
    gain_grads = jnp.stack(
        [gain_one, shift_one, gain_two, shift_two, gain_last, shift_last]
    ).reshape(6, devices, shard_rows)
    gain_grads = jnp.pad(
        gain_grads.transpose(1, 0, 2).reshape(devices, 6 * shard_rows),
        ((0, 0), (0, -6 * shard_rows % 128)),
    )
    gain_grad = jnp.sum(links.to_all(after(gain_grads, returned)), axis=0)[: 6 * shard_rows]
    gain_grad = gain_grad.reshape(6, shard_rows).T

    def more_grads(state):
        round_index, earlier_grad = state
        slot, asked = ask(round_index)
        returned_rows = links.to_all(give(slot, grad_embed_low))
        return (round_index + 1, earlier_grad + take(asked, returned_rows))

    unused_round, table_grad = lax.while_loop(
        lambda state: state[0] < rounds,
        more_grads,
        (
            jnp.ones((), jnp.int32),
            table_head + take(asked_first, after(returned, down_send, up_send, *last_sends)),
        ),
    )

    all_grads = (table_grad, qkv_grad, out_grad, up_grad, down_grad, gain_grad)
    firsts = (table_first_moment, first_qkv, first_out, first_up, first_down, first_norms)
    seconds = (table_second_moment, second_qkv, second_out, second_up, second_down, second_norms)
    totals = links.to_all(sum_squares(all_grads, weight_row, target_sum, devices))
    new_firsts, new_seconds, directions, update_rows = lamb_directions(
        totals, all_grads, firsts, seconds, masters
    )
    new_weights, facts = lamb_weights(totals, links.to_all(update_rows), directions, masters)
    return (
        (jnp.sum(log_total) - facts[4, 0]) / count_all,
        facts[3, 0],
        facts[:3, :6],
        *new_weights,
        *new_firsts,
        *new_seconds,
    )


def solution(mesh):
    rows = P(("wide", "narrow"), None)
    ids = P(None, ("wide", "narrow"), None)
    return jax.shard_map(
        per_device,
        mesh=mesh,
        in_specs=(ids,) * 3 + (rows,) * 18,
        out_specs=(P(),) * 3 + (rows,) * 18,
        check_vma=False,
    )
```

```python
import math

import jax
import jax.numpy as jnp
from jax import lax
from jax.experimental import pallas as pl
from jax.experimental.pallas import tpu as pltpu
from jax.sharding import PartitionSpec as P

HEAD_DIM = 64
VOCAB = 50257

neg_fill = -1e30
beta_first = 0.9
beta_second = 0.999
adam_epsilon = 1e-12
decay_rates = (0.01, 0.01, 0.01, 0.01, 0.01, 0.0)
learn_rate = 0.5
clip_limit = 0.01
norm_epsilon = 1e-05
step_count = 5.0
bf16 = jnp.bfloat16
f32 = jnp.float32


def layer_norm(values, gain_row, offset):
    centered = values - jnp.mean(values, axis=-1, keepdims=True)
    spread = jnp.mean(centered * centered, axis=-1, keepdims=True)
    return centered * lax.rsqrt(spread + norm_epsilon) * gain_row + offset


def norm_backward(values, gain_row, offset, grad_output):
    unused, pullback = jax.vjp(layer_norm, values, gain_row, offset)
    return pullback(grad_output)


def gelu_tanh(values):
    return jax.nn.gelu(values, approximate=True)


def matmul(left_side, right_side):
    return jnp.dot(left_side, right_side, preferred_element_type=f32)


def contract_rows(left_side, right_side):
    return lax.dot_general(
        left_side, right_side, (((0,), (0,)), ((), ())), preferred_element_type=f32
    )


def contract_cols(left_side, right_side):
    return lax.dot_general(
        left_side, right_side, (((1,), (1,)), ((), ())), preferred_element_type=f32
    )


class Links:
    def __init__(self):
        self.wide = lax.axis_size("wide")
        self.narrow = lax.axis_size("narrow")
        self.depth = self.wide // 2
        wide_place = lax.axis_index("wide")
        narrow_place = lax.axis_index("narrow")
        self.device = wide_place * self.narrow + narrow_place
        self.z = wide_place // 2
        self.place = {"x": wide_place % 2, "y": narrow_place // 2, "c": narrow_place % 2}

    def swap(self, values, axis):
        if axis == "x":
            return lax.ppermute(values, "wide", [(i, i ^ 1) for i in range(self.wide)])
        step = 2 if axis == "y" else 1
        return lax.ppermute(values, "narrow", [(i, i ^ step) for i in range(self.narrow)])

    def cross(self, values, step):
        return lax.ppermute(values, "wide", [(i, i ^ (2 * step)) for i in range(self.wide)])

    def exchange(self, values, combine):
        for step in (1, 2):
            other = lax.ppermute(values, "narrow", [(i, i ^ step) for i in range(self.narrow)])
            values = combine(values, other)
        step = 1
        while step < self.wide:
            other = lax.ppermute(values, "wide", [(i, i ^ step) for i in range(self.wide)])
            values = combine(values, other)
            step *= 2
        return values

    def to_all(self, values):
        return lax.all_to_all(values, ("wide", "narrow"), 0, 0, tiled=True)

    def gather_early(self, shard, *before):
        near = shard[None]
        for step in self.bits()[:0:-1]:
            near = jnp.concatenate([near, after(self.cross(near, step), *before)])
        return near

    def gather_late(self, near):
        return jnp.concatenate([near, self.cross(near, 1)])

    def gather_depth(self, shard):
        return self.gather_late(self.gather_early(shard))

    def bits(self):
        return [1 << number for number in range(self.depth.bit_length() - 1)]

    def steps(self):
        found = [0]
        for step in self.bits()[::-1]:
            found = found + [number ^ step for number in found]
        return found

    def plane_first(self, near):
        cut = halves(near.shape[-1])
        left, right = near[..., :cut], near[..., cut:]
        return left, right, self.swap(left, "x"), self.swap(right, "y")

    def plane_second(self, left, right, left_x, right_y):
        left, right = jnp.stack([left, left_x]), jnp.stack([right, right_y])
        return [left, self.swap(left, "y"), right, self.swap(right, "x")]

    def plane_core(self, pieces):
        return pieces + [self.swap(piece, "c") for piece in pieces]

    def gather_plane(self, near):
        return self.plane_core(self.plane_second(*self.plane_first(near)))

    def assemble(self, pieces, core_first=False, folded=None):
        depth = self.depth
        unused, unused_depth, rows, cut = pieces[0].shape
        count, fold = folded or (0, 0)
        width = cut + pieces[2].shape[3] - count * fold

        def kernel(place, *refs):
            sources, target = refs[: len(pieces)], refs[len(pieces)]
            x, y, c = place[0], place[1], place[2]
            for number, source in enumerate(sources):
                far_core, far, second = number // 4, number % 2, number // 2 % 2
                to_c = 1 - c if far_core else c
                columns = slice(cut, width) if second else slice(0, cut)
                for side in range(2):
                    across_x, across_y = (far, side) if second else (side, far)
                    to_x = 1 - x if across_x else x
                    to_y = 1 - y if across_y else y
                    if core_first:
                        target[to_c, to_x, to_y, 0, :, columns] = source[side, 0]
                    elif second:
                        target[0, to_x, to_y, to_c, :, columns] = source[side, 0, :, : width - cut]
                        for number_in in range(count):
                            start = width - cut + number_in * fold
                            refs[-1][
                                0, to_x, to_y, to_c, number_in * rows : (number_in + 1) * rows
                            ] = source[side, 0, :, start : start + fold]
                    else:
                        target[0, to_x, to_y, to_c, :, columns] = source[side, 0]

        place = [self.place["x"], self.place["y"], self.place["c"]]
        place = jnp.stack(place + [self.z ^ step for step in self.steps()]).astype(jnp.int32)
        if core_first:
            shape = (2, 2, 2, depth, rows, width)
            target_spec = pl.BlockSpec(
                (2, 2, 2, 1, rows, width), lambda k, place: (0, 0, 0, place[3 + k], 0, 0)
            )
        else:
            shape = (depth, 2, 2, 2, rows, width)
            target_spec = pl.BlockSpec(
                (1, 2, 2, 2, rows, width), lambda k, place: (place[3 + k], 0, 0, 0, 0, 0)
            )
        shapes, target_specs = [jax.ShapeDtypeStruct(shape, pieces[0].dtype)], [target_spec]
        if count:
            shapes.append(
                jax.ShapeDtypeStruct((depth, 2, 2, 2, count * rows, fold), pieces[0].dtype)
            )
            target_specs.append(
                pl.BlockSpec(
                    (1, 2, 2, 2, count * rows, fold),
                    lambda k, place: (place[3 + k], 0, 0, 0, 0, 0),
                )
            )
        wholes = pl.pallas_call(
            kernel,
            out_shape=shapes,
            grid_spec=pltpu.PrefetchScalarGridSpec(
                num_scalar_prefetch=1,
                grid=(depth,),
                in_specs=[
                    pl.BlockSpec((2, 1, rows, piece.shape[3]), lambda k, place: (0, k, 0, 0))
                    for piece in pieces
                ],
                out_specs=target_specs,
            ),
            compiler_params=pltpu.CompilerParams(vmem_limit_bytes=24 * 2**20),
            name="assemble",
        )(place, *pieces)
        wholes = [whole.reshape(-1, whole.shape[-1]) for whole in wholes]
        return wholes if count else wholes[0]

    def exchange_plane(self, values):
        for axis in "xyc":
            dim = " xyc".index(axis) - 1
            mine = lax.dynamic_index_in_dim(values, self.place[axis], dim, keepdims=False)
            other = lax.dynamic_index_in_dim(values, 1 - self.place[axis], dim, keepdims=False)
            values = jnp.stack([mine, self.swap(other, axis)], axis=dim)
        return values.transpose(2, 0, 1, 3, 4).reshape(-1, values.shape[-1])

    def share_direct(self, values):
        pairs = []
        for wide in range(self.wide):
            for narrow in range(self.narrow):
                pairs.append((wide * self.narrow + narrow, (wide ^ 1) * self.narrow + (narrow ^ 2)))
        across = lax.ppermute(values, ("wide", "narrow"), pairs)
        return [values, self.swap(values, "y"), self.swap(values, "x"), across]

    def share_first(self, values):
        cut = halves(values.shape[-1])
        left, right = values[:, :cut], values[:, cut:]
        return left, right, self.swap(left, "x"), self.swap(right, "y")

    def share_second(self, left, right, left_x, right_y):
        left, right = jnp.stack([left, left_x]), jnp.stack([right, right_y])
        return left, right, self.swap(left, "y"), self.swap(right, "x")

    def share_last(self, *pieces):
        return list(pieces) + [self.swap(piece, "c") for piece in pieces]

    def scatter_plane(self, full, *before_second):
        cut = halves(full.shape[-1])
        x, y = self.place["x"], self.place["y"]

        def pick(values, spot, dim):
            return lax.dynamic_index_in_dim(values, spot, dim, keepdims=False)

        left, right = full[..., :cut], full[..., cut:]
        from_x = self.swap(pick(left, 1 - x, 0), "x")
        from_y = self.swap(pick(right, 1 - y, 1), "y")
        left = (pick(left, x, 0).astype(f32) + from_x.astype(f32)).astype(bf16)
        right = (pick(right, y, 1).astype(f32) + from_y.astype(f32)).astype(bf16)
        left, right = after(left, *before_second), after(right, *before_second)
        sends = pick(left, 1 - y, 0), pick(right, 1 - x, 0)
        from_y, from_x = self.swap(sends[0], "y"), self.swap(sends[1], "x")
        left = pick(left, y, 0).astype(f32) + from_y.astype(f32)
        right = pick(right, x, 0).astype(f32) + from_x.astype(f32)
        return jnp.concatenate([left, right], axis=-1).astype(bf16), sends

    def scatter_depth(self, near, *before_last):
        for step in self.bits():
            if step == self.bits()[-1]:
                near = after(near, *before_last)
            pairs = near.reshape((-1, 2) + near.shape[1:])
            bit = self.z // step % 2
            other = lax.dynamic_index_in_dim(pairs, 1 - bit, 1, keepdims=False)
            mine = lax.dynamic_index_in_dim(pairs, bit, 1, keepdims=False)
            send = other.astype(bf16)
            near = mine.astype(f32) + self.cross(send, step).astype(f32)
        return near[0], send


def halves(width):
    return width // 256 * 128


def tie(*values):
    return lax.optimization_barrier(values)


def after(values, *others):
    return lax.optimization_barrier((values, *others))[0]


def lane_halves(values, first):
    lane = lax.broadcasted_iota(jnp.int32, values.shape, 1)
    return jnp.where((lane < HEAD_DIM) == first, values, jnp.zeros_like(values))


def attend(qkv_all, pick_rows, allowed, micro_count):
    token_count = qkv_all.shape[0]
    width = qkv_all.shape[1] // 3
    pick_total = pick_rows.shape[0]
    length, picked = token_count // micro_count, pick_total // micro_count
    pair = 2 * HEAD_DIM
    scale = HEAD_DIM ** (-0.5)

    def kernel(qkv_ref, pick_ref, allowed_ref, context_ref, query_ref, prob_ref):
        query_ref[...] = jnp.dot(
            pick_ref[...], qkv_ref[:, :width], preferred_element_type=f32
        ).astype(bf16)
        for micro in range(micro_count):
            rows = slice(micro * picked, (micro + 1) * picked)
            keep = allowed_ref[rows] > 0.5
            keep = jnp.concatenate([keep, keep], axis=0)
            for number in range(width // pair):
                columns = slice(number * pair, (number + 1) * pair)
                keys = qkv_ref[
                    micro * length : (micro + 1) * length,
                    width + number * pair : width + (number + 1) * pair,
                ]
                values = qkv_ref[
                    micro * length : (micro + 1) * length,
                    2 * width + number * pair : 2 * width + (number + 1) * pair,
                ]
                query = query_ref[rows, columns]
                both = jnp.concatenate(
                    [lane_halves(query, True), lane_halves(query, False)], axis=0
                )
                scores = contract_cols(both, keys) * scale
                scores = jnp.where(keep, scores, neg_fill)
                shifted = jnp.exp(scores - jnp.max(scores, axis=1, keepdims=True))
                probs = shifted / jnp.sum(shifted, axis=1, keepdims=True)
                prob_ref[micro, number] = probs
                mixed = jnp.dot(probs.astype(bf16), values, preferred_element_type=f32)
                context_ref[rows, columns] = (
                    lane_halves(mixed[:picked], True) + lane_halves(mixed[picked:], False)
                ).astype(bf16)

    return pl.pallas_call(
        kernel,
        out_shape=(
            jax.ShapeDtypeStruct((pick_total, width), bf16),
            jax.ShapeDtypeStruct((pick_total, width), bf16),
            jax.ShapeDtypeStruct((micro_count, width // pair, 2 * picked, length), f32),
        ),
        compiler_params=pltpu.CompilerParams(vmem_limit_bytes=32 * 2**20),
        name="attend",
    )(qkv_all, pick_rows, allowed)


def attend_backward(qkv_all, pick_rows, query_all, probs_all, grad_context, micro_count):
    token_count = qkv_all.shape[0]
    width = qkv_all.shape[1] // 3
    pick_total = pick_rows.shape[0]
    length, picked = token_count // micro_count, pick_total // micro_count
    pair = 2 * HEAD_DIM
    scale = HEAD_DIM ** (-0.5)

    def kernel(qkv_ref, pick_ref, query_ref, prob_ref, grad_ref, out_ref, query_grad_ref):
        for micro in range(micro_count):
            rows = slice(micro * picked, (micro + 1) * picked)
            tokens = slice(micro * length, (micro + 1) * length)
            for number in range(width // pair):
                columns = slice(number * pair, (number + 1) * pair)
                key_columns = slice(width + number * pair, width + (number + 1) * pair)
                value_columns = slice(2 * width + number * pair, 2 * width + (number + 1) * pair)
                query, grad = query_ref[rows, columns], grad_ref[rows, columns]
                queries = jnp.concatenate(
                    [lane_halves(query, True), lane_halves(query, False)], axis=0
                )
                grads = jnp.concatenate(
                    [lane_halves(grad, True), lane_halves(grad, False)], axis=0
                )
                probs = prob_ref[micro, number]
                grad_probs = contract_cols(grads, qkv_ref[tokens, value_columns])
                inner = jnp.sum(probs * grad_probs, axis=1, keepdims=True)
                grad_scores = (probs * (grad_probs - inner)).astype(bf16)
                mixed = (
                    jnp.dot(
                        grad_scores, qkv_ref[tokens, key_columns], preferred_element_type=f32
                    )
                    * scale
                )
                query_grad_ref[rows, columns] = (
                    lane_halves(mixed[:picked], True) + lane_halves(mixed[picked:], False)
                ).astype(bf16)
                out_ref[tokens, key_columns] = (
                    contract_rows(grad_scores, queries) * scale
                ).astype(bf16)
                out_ref[tokens, value_columns] = contract_rows(probs.astype(bf16), grads).astype(
                    bf16
                )
        out_ref[:, :width] = contract_rows(pick_ref[...], query_grad_ref[...]).astype(bf16)

    return pl.pallas_call(
        kernel,
        out_shape=jax.ShapeDtypeStruct(qkv_all.shape, bf16),
        scratch_shapes=[pltpu.VMEM((pick_total, width), bf16)],
        compiler_params=pltpu.CompilerParams(vmem_limit_bytes=32 * 2**20),
        name="attend_backward",
    )(qkv_all, pick_rows, query_all, probs_all, grad_context)


def plane_products(known, grads, attn_grads, depth, widths):
    hidden, model = widths
    rows = grads[0].shape[-2]
    width = hidden + 2 * model
    down_rows, model_rows = hidden // (8 * depth), model // (8 * depth)
    down_width, model_width = hidden // 8, model // 8

    def kernel(known_ref, *refs):
        down_ref, up_ref, out_ref, grads_ref = refs[10:]
        cut = grads[0].shape[-1]
        for far_core in range(2):
            left, right, left_y, right_x = refs[4 * far_core : 4 * far_core + 4]
            attn = refs[8 + far_core]
            for x in range(2):
                for y in range(2):
                    spot = pl.ds(((far_core * 2 + x) * 2 + y) * rows, rows)
                    grads_ref[spot, :cut] = (left_y if y else left)[x]
                    grads_ref[spot, cut : hidden + model] = (right_x if x else right)[y]
                    grads_ref[spot, hidden + model :] = attn[2 * x + y]
        down_ref[...] = contract_rows(
            known_ref[:, :down_width], grads_ref[:, hidden : hidden + model]
        ).astype(bf16)
        up_ref[...] = contract_rows(
            known_ref[:, down_width : down_width + model_width], grads_ref[:, :hidden]
        ).astype(bf16)
        out_ref[...] = contract_rows(
            known_ref[:, down_width + model_width :], grads_ref[:, hidden + model :]
        ).astype(bf16)

    in_vmem = pl.BlockSpec(memory_space=pltpu.VMEM)
    down, up, out = pl.pallas_call(
        kernel,
        in_specs=[in_vmem] * 11,
        out_shape=(
            jax.ShapeDtypeStruct((depth * down_rows, model), bf16),
            jax.ShapeDtypeStruct((depth * model_rows, hidden), bf16),
            jax.ShapeDtypeStruct((depth * model_rows, model), bf16),
        ),
        scratch_shapes=[
            pltpu.VMEM((8 * rows, width), bf16),
        ],
        compiler_params=pltpu.CompilerParams(vmem_limit_bytes=48 * 2**20),
        name="plane_products",
    )(known, *grads, *attn_grads)
    return (
        down.reshape(depth, down_rows, model),
        up.reshape(depth, model_rows, hidden),
        out.reshape(depth, model_rows, model),
    )


def on_lane(place, value):
    lane = lax.broadcasted_iota(jnp.int32, (1, 128), 1)
    return jnp.where(lane == place, value, 0.0)


def whole_sum(values):
    return jnp.sum(jnp.sum(values, axis=0, keepdims=True), axis=1, keepdims=True)


def sum_squares(all_grads, weight_row, target_sum, devices):
    def kernel(table_ref, target_ref, weight_ref, *refs):
        grads, rows_ref = refs[:-1], refs[-1]
        row = on_lane(0, table_ref[...])
        for place, grad in enumerate(grads):
            row = row + on_lane(place + 1, whole_sum(grad[...] * grad[...]))
        rows_ref[:, :128] = jnp.broadcast_to(row, (devices, 128))
        rows_ref[:, 128:] = jnp.broadcast_to(
            weight_ref[...] + on_lane(64, target_ref[...]), (devices, 128)
        )

    table_square = jnp.sum(all_grads[0] * all_grads[0]).reshape(1, 1)
    return pl.pallas_call(
        kernel,
        out_shape=jax.ShapeDtypeStruct((devices, 256), f32),
        name="sum_squares",
    )(table_square, target_sum.reshape(1, 1), weight_row, *all_grads[1:])


grid_steps = 4


def unfold(whole, count, width, shard_rows):
    devices = whole.shape[0] // shard_rows
    group = max(1, min(devices, 256 // shard_rows))

    def kernel(source_ref, target_ref):
        for number in range(count):
            block = source_ref[:, number * width : (number + 1) * width]
            target_ref[:, number] = block.reshape(group, shard_rows, width)

    rows = pl.pallas_call(
        kernel,
        grid=(devices // group,),
        in_specs=[pl.BlockSpec((group * shard_rows, count * width), lambda i: (i, 0))],
        out_specs=pl.BlockSpec((group, count, shard_rows, width), lambda i: (i, 0, 0, 0)),
        out_shape=jax.ShapeDtypeStruct((devices, count, shard_rows, width), whole.dtype),
        compiler_params=pltpu.CompilerParams(vmem_limit_bytes=32 * 2**20),
        name="unfold",
    )(whole)
    return rows.reshape(-1, width)


row_block = 256


def head_logits(head_rows, table_low, targets, base, block_size):
    row_count, width = head_rows.shape
    columns = table_low.shape[0]
    block = min(row_block, row_count)

    def kernel(base_ref, rows_ref, table_ref, targets_ref, logits_ref, top_ref, sum_ref, hit_ref):
        step = pl.program_id(0)
        place = lax.broadcasted_iota(jnp.int32, (1, columns), 1)
        column = jnp.where(place < block_size, place + base_ref[0], VOCAB)
        fill = jnp.where(column < VOCAB, 0.0, neg_fill)
        logits = contract_cols(rows_ref[...], table_ref[...]) + fill
        logits_ref[...] = logits
        top = jnp.max(logits, axis=1, keepdims=True)
        total = jnp.sum(jnp.exp(logits - top), axis=1, keepdims=True)
        top_ref[...] = jnp.broadcast_to(top, (block, 128)).T[:1]
        sum_ref[...] = jnp.broadcast_to(total, (block, 128)).T[:1]

        @pl.when(step == 0)
        def _():
            hit_ref[...] = jnp.zeros_like(hit_ref)

        hits = targets_ref[...] == column
        hit_ref[...] += jnp.broadcast_to(whole_sum(jnp.where(hits, logits, 0.0)), (1, 128))

    return pl.pallas_call(
        kernel,
        out_shape=(
            jax.ShapeDtypeStruct((row_count, columns), f32),
            jax.ShapeDtypeStruct((1, row_count), f32),
            jax.ShapeDtypeStruct((1, row_count), f32),
            jax.ShapeDtypeStruct((1, 128), f32),
        ),
        grid=(row_count // block,),
        in_specs=[
            pl.BlockSpec(memory_space=pltpu.SMEM),
            pl.BlockSpec((block, width), lambda k: (k, 0)),
            pl.BlockSpec((columns, width), lambda k: (0, 0)),
            pl.BlockSpec((block, 1), lambda k: (k, 0)),
        ],
        out_specs=(
            pl.BlockSpec((block, columns), lambda k: (k, 0)),
            pl.BlockSpec((1, block), lambda k: (0, k)),
            pl.BlockSpec((1, block), lambda k: (0, k)),
            pl.BlockSpec((1, 128), lambda k: (0, 0)),
        ),
        compiler_params=pltpu.CompilerParams(vmem_limit_bytes=56 * 2**20),
        name="head_logits",
    )(base.reshape(1), head_rows, table_low, targets)


def head_grads(logits, log_total, table_low, targets, base, half, count_all, block_size, add=None):
    row_count, columns = logits.shape
    width = table_low.shape[1]
    block = min(row_block, row_count // 2)
    steps = row_count // 2 // block
    scale = 1.0 / count_all

    def kernel(place_ref, logits_ref, total_ref, table_ref, targets_ref, *refs):
        grads_ref, out_ref = refs[-2:]
        place = lax.broadcasted_iota(jnp.int32, (1, columns), 1)
        column = jnp.where(place < block_size, place + place_ref[1], VOCAB)
        total = jnp.broadcast_to(total_ref[...], (128, block)).T[:, :1]
        hits = targets_ref[...] == column
        probs = jnp.exp(logits_ref[...] - total)
        grads = ((probs - jnp.where(hits, 1.0, 0.0)) * scale).astype(bf16)
        grads_ref[...] = grads
        product = matmul(grads, table_ref[...])
        if add is not None:
            product = product + refs[0][...].astype(f32)
        out_ref[...] = product.astype(bf16)

    half_spec = pl.BlockSpec((block, width), lambda k, place: (k, 0))
    return pl.pallas_call(
        kernel,
        out_shape=(
            jax.ShapeDtypeStruct((row_count // 2, columns), bf16),
            jax.ShapeDtypeStruct((row_count // 2, width), bf16),
        ),
        grid_spec=pltpu.PrefetchScalarGridSpec(
            num_scalar_prefetch=1,
            grid=(steps,),
            in_specs=[
                pl.BlockSpec((block, columns), lambda k, place: (place[0] * steps + k, 0)),
                pl.BlockSpec((1, block), lambda k, place: (0, place[0] * steps + k)),
                pl.BlockSpec((columns, width), lambda k, place: (0, 0)),
                pl.BlockSpec((block, 1), lambda k, place: (place[0] * steps + k, 0)),
            ]
            + ([] if add is None else [half_spec]),
            out_specs=(
                pl.BlockSpec((block, columns), lambda k, place: (k, 0)),
                half_spec,
            ),
        ),
        compiler_params=pltpu.CompilerParams(vmem_limit_bytes=56 * 2**20),
        name="head_grads",
    )(
        jnp.stack([half, base]).astype(jnp.int32),
        logits,
        log_total,
        table_low,
        targets,
        *(() if add is None else (add,)),
    )


def weight_squares(masters):
    table_rows = -(-masters[0].shape[0] // (8 * grid_steps)) * 8
    table_count = masters[0].shape[0]

    def kernel(table_ref, *refs):
        others, row_ref = refs[:-1], refs[-1]
        step = pl.program_id(0)

        @pl.when(step == 0)
        def _():
            row = jnp.zeros((1, 128), f32)
            for place, other in enumerate(others):
                row = row + on_lane(place + 1, whole_sum(other[...] * other[...]))
            row_ref[...] = row

        place = step * table_rows + lax.broadcasted_iota(jnp.int32, (table_rows, 1), 0)
        square = jnp.where(place < table_count, table_ref[...] * table_ref[...], 0.0)
        row_ref[...] += on_lane(0, whole_sum(square))

    return pl.pallas_call(
        kernel,
        grid=(grid_steps,),
        in_specs=[pl.BlockSpec((table_rows, masters[0].shape[1]), lambda k: (k, 0))]
        + [
            pl.BlockSpec(array.shape, lambda k: (0, 0), pipeline_mode=pl.Buffered(1))
            for array in masters[1:]
        ],
        out_specs=pl.BlockSpec((1, 128), lambda k: (0, 0)),
        out_shape=jax.ShapeDtypeStruct((1, 128), f32),
        compiler_params=pltpu.CompilerParams(vmem_limit_bytes=32 * 2**20),
        name="weight_squares",
    )(*masters)


def group_specs(arrays):
    table_rows = -(-arrays[0].shape[0] // (8 * grid_steps)) * 8
    specs = [pl.BlockSpec((table_rows, arrays[0].shape[1]), lambda k: (k, 0))]
    for array in arrays[1:5]:
        rows, width = array.shape
        specs.append(pl.BlockSpec((rows, width // grid_steps), lambda k: (0, k)))
    specs.append(pl.BlockSpec(arrays[5].shape, lambda k: (0, 0)))
    return specs


def lamb_directions(totals, all_grads, firsts, seconds, masters):
    devices = totals.shape[0]
    table_count = all_grads[0].shape[0]
    specs = group_specs(all_grads)
    table_rows = specs[0].block_shape[0]
    first_scale = 1.0 / (1.0 - beta_first**step_count)
    second_scale = 1.0 / (1.0 - beta_second**step_count)

    def kernel(totals_ref, *refs):
        grads, olds, squares, weights = refs[:6], refs[6:12], refs[12:18], refs[18:24]
        new_olds, new_squares, directions, rows_ref = refs[24:30], refs[30:36], refs[36:42], refs[42]
        step = pl.program_id(0)
        grad_total = jnp.sum(totals_ref[:, :128], axis=0, keepdims=True)
        factor = jnp.minimum(
            1.0, clip_limit * lax.rsqrt(jnp.sum(grad_total, axis=1, keepdims=True))
        )

        @pl.when(step == 0)
        def _():
            rows_ref[...] = jnp.zeros_like(rows_ref)

        def update(group, rows, live=None):
            clipped = factor * grads[group][rows]
            new_old = beta_first * olds[group][rows] + (1.0 - beta_first) * clipped
            new_square = beta_second * squares[group][rows] + (1.0 - beta_second) * clipped * clipped
            direction = (new_old * first_scale) / (
                jnp.sqrt(new_square * second_scale) + adam_epsilon
            ) + decay_rates[group] * weights[group][rows]
            new_olds[group][rows] = new_old
            new_squares[group][rows] = new_square
            directions[group][rows] = direction
            square = direction * direction
            return square if live is None else jnp.where(live, square, 0.0)

        def table_part(part, total):
            rows = pl.ds(pl.multiple_of(part * 8, 8), 8)
            place = step * table_rows + part * 8 + lax.broadcasted_iota(
                jnp.int32, (8, 1), 0
            )
            return total + update(0, (rows, slice(None)), place < table_count)

        table_total = lax.fori_loop(
            0, table_rows // 8, table_part, jnp.zeros((8, all_grads[0].shape[1]), f32)
        )
        row = on_lane(0, whole_sum(table_total))
        for group in range(1, 5):
            row = row + on_lane(group, whole_sum(update(group, (slice(None), slice(None)))))
        rows_ref[...] += jnp.broadcast_to(row, rows_ref.shape)

        @pl.when(step == 0)
        def _():
            row = on_lane(5, whole_sum(update(5, (slice(None), slice(None)))))
            rows_ref[...] += jnp.broadcast_to(row, rows_ref.shape)

    shapes = [jax.ShapeDtypeStruct(array.shape, f32) for array in all_grads]
    results = pl.pallas_call(
        kernel,
        grid=(grid_steps,),
        in_specs=[pl.BlockSpec(totals.shape, lambda k: (0, 0))] + specs * 4,
        out_specs=specs * 3 + [pl.BlockSpec((devices, 128), lambda k: (0, 0))],
        out_shape=shapes * 3 + [jax.ShapeDtypeStruct((devices, 128), f32)],
        compiler_params=pltpu.CompilerParams(vmem_limit_bytes=56 * 2**20),
        name="lamb_directions",
    )(totals, *all_grads, *firsts, *seconds, *masters)
    return results[:6], results[6:12], results[12:18], results[18]


def lamb_weights(totals, update_rows, directions, masters):
    specs = group_specs(masters)

    def kernel(totals_ref, updates_ref, *refs):
        moves, weights, news, facts_ref = refs[:6], refs[6:12], refs[12:18], refs[18]
        step = pl.program_id(0)
        lane = lax.broadcasted_iota(jnp.int32, (1, 128), 1)
        grad_total = jnp.sum(totals_ref[:, :128], axis=0, keepdims=True)
        weight_total = jnp.sum(totals_ref[:, 128:], axis=0, keepdims=True)
        update_total = jnp.sum(updates_ref[...], axis=0, keepdims=True)
        weight_norms = jnp.where(lane < 6, jnp.sqrt(jnp.maximum(weight_total, 0.0)), 0.0)
        update_norms = jnp.where(lane < 6, jnp.sqrt(update_total), 1.0)
        rates = learn_rate * weight_norms / update_norms
        for group in range(5):
            rate = jnp.sum(jnp.where(lane == group, rates, 0.0), axis=1, keepdims=True)
            news[group][...] = weights[group][...] - rate * moves[group][...]

        @pl.when(step == 0)
        def _():
            rate = jnp.sum(jnp.where(lane == 5, rates, 0.0), axis=1, keepdims=True)
            news[5][...] = weights[5][...] - rate * moves[5][...]
            grad_norm = jnp.sqrt(jnp.sum(grad_total, axis=1, keepdims=True))
            factor = jnp.minimum(1.0, clip_limit / grad_norm)
            target = jnp.sum(jnp.where(lane == 64, weight_total, 0.0), axis=1, keepdims=True)
            facts_ref[0:1] = factor * jnp.sqrt(grad_total)
            facts_ref[1:2] = weight_norms
            facts_ref[2:3] = update_norms
            facts_ref[3:4] = jnp.broadcast_to(grad_norm, (1, 128))
            facts_ref[4:5] = jnp.broadcast_to(target, (1, 128))

    results = pl.pallas_call(
        kernel,
        grid=(grid_steps,),
        in_specs=[
            pl.BlockSpec(totals.shape, lambda k: (0, 0)),
            pl.BlockSpec(update_rows.shape, lambda k: (0, 0)),
        ]
        + specs * 2,
        out_specs=specs + [pl.BlockSpec((8, 128), lambda k: (0, 0))],
        out_shape=[jax.ShapeDtypeStruct(array.shape, f32) for array in masters]
        + [jax.ShapeDtypeStruct((8, 128), f32)],
        compiler_params=pltpu.CompilerParams(vmem_limit_bytes=56 * 2**20),
        name="lamb_weights",
    )(totals, update_rows, *directions, *masters)
    return results[:6], results[6]


def per_device(
    token_ids,
    doc_ids,
    loss_positions,
    tied_table_master,
    qkv_master,
    out_master,
    up_master,
    down_master,
    norm_master,
    table_first_moment,
    first_qkv,
    first_out,
    first_up,
    first_down,
    first_norms,
    table_second_moment,
    second_qkv,
    second_out,
    second_up,
    second_down,
    second_norms,
):
    links = Links()
    devices = links.wide * links.narrow
    micro_count, unused, length = token_ids.shape
    picked_count = loss_positions.shape[2]
    token_count = micro_count * length
    pick_total = micro_count * picked_count
    model_width = tied_table_master.shape[1]
    head_count = model_width // HEAD_DIM
    block_size = tied_table_master.shape[0]
    count_all = devices * pick_total
    shard_rows = qkv_master.shape[0]

    tokens = token_ids.reshape(token_count)
    picks = loss_positions.reshape(micro_count, picked_count)
    documents = doc_ids.reshape(micro_count, length)
    mean_load = token_count / devices
    slots = int(math.ceil((mean_load + 6.0 * math.sqrt(mean_load)) / 8.0)) * 8
    owner = tokens // block_size
    local_row = tokens % block_size
    token_place = jnp.arange(token_count)
    earlier = (owner[:, None] == owner[None, :]) & (token_place[None, :] < token_place[:, None])
    rank = jnp.sum(earlier.astype(jnp.int32), axis=1)
    most = jnp.max(rank) + 1
    slot_place = jnp.arange(devices * slots)
    line = -(-(slots + 1 + pick_total) // 128) * 128

    pick_hits = picks[:, :, None] == jnp.arange(length)[None, None, :]
    next_hits = picks[:, :, None] + 1 == jnp.arange(length)[None, None, :]
    own_targets = jnp.sum(
        jnp.where(next_hits, token_ids.reshape(micro_count, 1, length), 0), axis=2
    ).reshape(-1)
    pick_docs = jnp.sum(jnp.where(pick_hits, documents[:, None, :], 0), axis=2)

    def slot_of(round_index):
        inside = (rank >= round_index * slots) & (rank < (round_index + 1) * slots)
        return jnp.where(inside, owner * slots + rank - round_index * slots, -1)

    def message_of(slot):
        wanted = jnp.sum(
            jnp.where(slot[None, :] == slot_place[:, None], local_row[None, :] + 1, 0), axis=1
        ) - 1
        wanted = wanted.reshape(devices, slots)
        return jnp.concatenate(
            [
                wanted,
                jnp.broadcast_to(most, (devices, 1)),
                jnp.broadcast_to(own_targets[None, :], (devices, pick_total)),
                jnp.zeros((devices, line - slots - 1 - pick_total), jnp.int32),
            ],
            axis=1,
        )

    def ask(round_index):
        slot = slot_of(round_index)
        return slot, links.to_all(message_of(slot))[:, :slots].reshape(-1)

    def find(asked):
        row_hits = (asked[:, None] == jnp.arange(padded_rows)[None, :]).astype(bf16)
        return matmul(row_hits, table_low).astype(bf16)

    def place_rows(slot, landed):
        token_hits = (slot[:, None] == slot_place[None, :]).astype(bf16)
        return matmul(token_hits, landed).astype(bf16)

    def give(slot, grad_low):
        token_hits = (slot[:, None] == slot_place[None, :]).astype(bf16)
        return contract_rows(token_hits, grad_low).astype(bf16)

    def take(asked, landed):
        row_hits = (asked[None, :] == jnp.arange(block_size)[:, None]).astype(bf16)
        return matmul(row_hits, landed)

    gain_width = 128
    qkv_width = qkv_master.shape[1]
    gain_shard = jnp.pad(norm_master, ((0, 0), (0, gain_width - norm_master.shape[1])))
    slot_first = slot_of(0)
    masters = (tied_table_master, qkv_master, out_master, up_master, down_master, norm_master)
    first_shard = jnp.concatenate([qkv_master, gain_shard], axis=1).astype(bf16)
    first_early = links.gather_early(first_shard)
    first_near = links.gather_late(first_early)
    message = message_of(slot_first)
    answer = links.to_all(message)
    padded_rows = -(-block_size // 128) * 128
    table_low = jnp.pad(
        after(tied_table_master, message), ((0, padded_rows - block_size), (0, 0))
    ).astype(bf16)
    asked_first = answer[:, :slots].reshape(-1)
    rounds = (jnp.max(answer[:, slots]) + slots - 1) // slots
    targets = answer[:, slots + 1 : slots + 1 + pick_total]
    targets = targets.reshape(links.depth, 2, 2, 2, pick_total).transpose(3, 1, 2, 0, 4).reshape(-1)
    fold_count = down_master.shape[0] // shard_rows
    second_shard = jnp.concatenate(
        [
            down_master[number * shard_rows : (number + 1) * shard_rows]
            for number in range(fold_count)
        ]
        + [up_master, out_master],
        axis=1,
    )
    second_whole = lax.all_gather(
        second_shard.astype(bf16), ("wide", "narrow"), axis=0, tiled=True
    )
    first_parts = links.plane_first(first_near)
    found = after(find(asked_first), first_near)
    landed = links.to_all(found)
    first_pieces = links.plane_second(*first_parts)
    weight_row = weight_squares(tie(*masters, found)[:6])
    first_pieces[0] = after(first_pieces[0], weight_row, table_low)
    first_whole = links.assemble(links.plane_core(first_pieces))
    qkv_weight = first_whole[:, :qkv_width]
    gain_entries = first_whole[:, qkv_width : qkv_width + 6].astype(f32).T

    def more_rows(state):
        round_index, embedded = state
        slot, asked = ask(round_index)
        return (round_index + 1, embedded + place_rows(slot, links.to_all(find(asked))))

    unused_round, x_low = lax.while_loop(
        lambda state: state[0] < rounds,
        more_rows,
        (jnp.ones((), jnp.int32), place_rows(slot_first, landed)),
    )

    x_embed = x_low.astype(f32)
    normed_one = layer_norm(x_embed, gain_entries[0], gain_entries[1]).astype(bf16)
    qkv_all = matmul(normed_one, qkv_weight).astype(bf16)
    pick_rows = (
        pick_hits[:, :, None, :] & jnp.eye(micro_count, dtype=bool)[:, None, :, None]
    ).reshape(pick_total, token_count).astype(bf16)
    x_embed_picked = matmul(pick_rows, x_low)
    allowed = (jnp.arange(length)[None, None, :] <= picks[:, :, None]) & (
        documents[:, None, :] == pick_docs[:, :, None]
    )
    context, queries, probs = attend(
        qkv_all, pick_rows, allowed.reshape(pick_total, length).astype(f32), micro_count
    )
    down_weight = unfold(second_whole, fold_count, model_width, shard_rows)
    hidden = up_master.shape[1]
    folded = fold_count * model_width
    up_weight = second_whole[:, folded : folded + hidden]
    out_weight = second_whole[:, folded + hidden :]
    x_attn = x_embed_picked + matmul(context, out_weight)
    normed_two = layer_norm(x_attn, gain_entries[2], gain_entries[3]).astype(bf16)
    up_value = matmul(normed_two, up_weight)
    activated = gelu_tanh(up_value).astype(bf16)
    x_out = x_attn + matmul(activated, down_weight)
    picked_low = layer_norm(x_out, gain_entries[4], gain_entries[5]).astype(bf16)

    head_pieces = links.plane_second(*links.plane_first(links.gather_depth(picked_low)))
    head_rows = links.assemble(
        links.plane_core(head_pieces), core_first=True
    )
    base = links.device * block_size
    target_column = targets[:, None]
    logits, local_top, local_sum, target_sum = head_logits(
        head_rows, table_low, target_column, base, block_size
    )
    target_sum = target_sum[:, :1]

    def merge_totals(first, second):
        top = jnp.maximum(first[0], second[0])
        total = first[1] * jnp.exp(first[0] - top) + second[1] * jnp.exp(second[0] - top)
        return jnp.stack([top, total])

    merged = links.exchange(jnp.concatenate([local_top, local_sum]), merge_totals)
    def by_owner(values, block_rows):
        if block_rows % 128 == 0:
            blocks = values.reshape(pick_total, links.depth, 8, block_rows)
            blocks = blocks.transpose(2, 0, 1, 3).reshape(8 * pick_total, -1)
            return blocks.reshape(8, pick_total, -1)
        count = values.shape[1]
        place = jnp.arange(count)
        source = place % (count // 8) // block_rows * 8 + place // (count // 8)
        source = source * block_rows + place % block_rows
        order = (jnp.arange(count)[:, None] == source[None, :]).astype(bf16)
        ordered = matmul(values, order).astype(bf16)
        return ordered.reshape(pick_total, 8, count // 8).transpose(1, 0, 2)

    known = jnp.concatenate(
        [
            by_owner(activated, down_master.shape[0]),
            by_owner(normed_two, shard_rows),
            by_owner(context, shard_rows),
        ],
        axis=2,
    )
    known = known.reshape(2, 2, 2, pick_total, -1)
    log_total = merged[0] + jnp.log(merged[1])
    core = links.place["c"]
    log_row = log_total[None]
    far_grads, to_core = head_grads(
        logits, log_row, table_low, target_column, base, 1 - core, count_all, block_size
    )
    from_core = links.swap(to_core, "c")
    own_grads, near_sum = head_grads(
        logits, log_row, table_low, target_column, base, core, count_all, block_size, from_core
    )
    own_rows = [
        lax.dynamic_slice_in_dim(head_rows, spot * far_grads.shape[0], far_grads.shape[0], 0)
        for spot in (1 - core, core)
    ]
    grad_near, unused = links.scatter_plane(
        near_sum.reshape(2, 2, links.depth, pick_total, model_width),
        known,
    )
    known = links.exchange_plane(after(known, grad_near))
    grad_picked, unused = links.scatter_depth(grad_near)

    grad_x_out, gain_last, shift_last = norm_backward(
        x_out, gain_entries[4], gain_entries[5], grad_picked
    )
    grad_mlp = grad_x_out.astype(bf16)
    unused, gelu_pull = jax.vjp(gelu_tanh, up_value)
    grad_up_low = gelu_pull(contract_cols(grad_mlp, down_weight))[0].astype(bf16)
    grad_parts = links.share_first(jnp.concatenate([grad_up_low, grad_mlp], axis=1))
    grad_x_attn, gain_two, shift_two = norm_backward(
        x_attn, gain_entries[2], gain_entries[3], contract_cols(grad_up_low, up_weight)
    )
    grad_x_attn = grad_x_out + grad_x_attn
    grad_attn_low = grad_x_attn.astype(bf16)
    grad_context = contract_cols(grad_attn_low, out_weight).astype(bf16)
    attn_parts = links.share_direct(grad_attn_low)
    grad_context = after(grad_context, *grad_parts)
    grad_parts = links.share_second(*grad_parts)
    grad_qkv_low = attend_backward(
        qkv_all, pick_rows, queries, probs, grad_context, micro_count
    )
    late = after(grad_qkv_low, known, *attn_parts)
    grad_x_one, gain_one, shift_one = norm_backward(
        x_embed, gain_entries[0], gain_entries[1], contract_cols(late, qkv_weight)
    )
    grad_x_embed = grad_x_one + lax.dot_general(
        pick_rows.astype(f32),
        grad_x_attn,
        (((0,), (0,)), ((), ())),
        precision=lax.Precision.HIGHEST,
        preferred_element_type=f32,
    )
    grad_embed_low = grad_x_embed.astype(bf16)
    sent = give(slot_first, grad_embed_low)
    returned = links.to_all(sent)
    half_place = jnp.arange(model_width // 2)
    half_row = half_place % shard_rows
    half_z = half_place // shard_rows % links.depth
    half_plane = half_place // shard_rows // links.depth

    def qkv_part(spot):
        source = ((half_z * 4 + half_plane) * 2 + spot) * shard_rows + half_row
        columns = (jnp.arange(model_width)[:, None] == source[None, :]).astype(bf16)
        return contract_rows(matmul(normed_one, columns).astype(bf16), grad_qkv_low)

    grad_qkv_low = after(grad_qkv_low, sent, *attn_parts, *grad_parts)
    to_core = qkv_part(1 - core).astype(bf16)
    from_core = links.swap(to_core, "c")
    last_mine = (qkv_part(core) + from_core.astype(f32)).astype(bf16)
    last_near, last_sends = links.scatter_plane(
        last_mine.reshape(2, 2, links.depth, shard_rows, qkv_width), returned
    )
    down_near, up_near, out_near = plane_products(
        known,
        links.share_last(*[after(part, last_mine) for part in grad_parts]),
        links.share_last(after(jnp.stack(attn_parts), last_mine)),
        links.depth,
        (activated.shape[1], model_width),
    )

    last_near = jnp.concatenate([last_near, out_near], axis=-1)
    down_grad, down_send = links.scatter_depth(down_near, returned)
    up_grad, up_send = links.scatter_depth(up_near, returned)
    last_grad, unused = links.scatter_depth(last_near)
    qkv_grad, out_grad = last_grad[:, :qkv_width], last_grad[:, qkv_width:]
    far_grads = after(far_grads, returned, down_send, up_send, *last_sends)
    own_grads = after(own_grads, far_grads)
    table_head = contract_rows(far_grads[:, :block_size], own_rows[0]) + contract_rows(
        own_grads[:, :block_size], own_rows[1]
    )
    gain_one = after(gain_one, returned, down_send, up_send, *last_sends)
    gain_grads = jnp.stack(
        [gain_one, shift_one, gain_two, shift_two, gain_last, shift_last]
    ).reshape(6, devices, shard_rows)
    gain_grads = jnp.pad(
        gain_grads.transpose(1, 0, 2).reshape(devices, 6 * shard_rows),
        ((0, 0), (0, -6 * shard_rows % 128)),
    )
    gain_grad = jnp.sum(links.to_all(after(gain_grads, returned)), axis=0)[: 6 * shard_rows]
    gain_grad = gain_grad.reshape(6, shard_rows).T

    def more_grads(state):
        round_index, earlier_grad = state
        slot, asked = ask(round_index)
        returned_rows = links.to_all(give(slot, grad_embed_low))
        return (round_index + 1, earlier_grad + take(asked, returned_rows))

    unused_round, table_grad = lax.while_loop(
        lambda state: state[0] < rounds,
        more_grads,
        (
            jnp.ones((), jnp.int32),
            table_head + take(asked_first, after(returned, down_send, up_send, *last_sends)),
        ),
    )

    all_grads = (table_grad, qkv_grad, out_grad, up_grad, down_grad, gain_grad)
    firsts = (table_first_moment, first_qkv, first_out, first_up, first_down, first_norms)
    seconds = (table_second_moment, second_qkv, second_out, second_up, second_down, second_norms)
    totals = links.to_all(sum_squares(all_grads, weight_row, target_sum, devices))
    new_firsts, new_seconds, directions, update_rows = lamb_directions(
        totals, all_grads, firsts, seconds, masters
    )
    new_weights, facts = lamb_weights(totals, links.to_all(update_rows), directions, masters)
    return (
        (jnp.sum(log_total) - facts[4, 0]) / count_all,
        facts[3, 0],
        facts[:3, :6],
        *new_weights,
        *new_firsts,
        *new_seconds,
    )


def solution(mesh):
    rows = P(("wide", "narrow"), None)
    ids = P(None, ("wide", "narrow"), None)
    return jax.shard_map(
        per_device,
        mesh=mesh,
        in_specs=(ids,) * 3 + (rows,) * 18,
        out_specs=(P(),) * 3 + (rows,) * 18,
        check_vma=False,
    )
```

```python
import math

import jax
import jax.numpy as jnp
from jax import lax
from jax.experimental import pallas as pl
from jax.experimental.pallas import tpu as pltpu
from jax.sharding import PartitionSpec as P

HEAD_DIM = 64
VOCAB = 50257

neg_fill = -1e30
beta_first = 0.9
beta_second = 0.999
adam_epsilon = 1e-12
decay_rates = (0.01, 0.01, 0.01, 0.01, 0.01, 0.0)
learn_rate = 0.5
clip_limit = 0.01
norm_epsilon = 1e-05
step_count = 5.0
bf16 = jnp.bfloat16
f32 = jnp.float32


def layer_norm(values, gain_row, offset):
    centered = values - jnp.mean(values, axis=-1, keepdims=True)
    spread = jnp.mean(centered * centered, axis=-1, keepdims=True)
    return centered * lax.rsqrt(spread + norm_epsilon) * gain_row + offset


def norm_backward(values, gain_row, offset, grad_output):
    unused, pullback = jax.vjp(layer_norm, values, gain_row, offset)
    return pullback(grad_output)


def gelu_tanh(values):
    return jax.nn.gelu(values, approximate=True)


def matmul(left_side, right_side):
    return jnp.dot(left_side, right_side, preferred_element_type=f32)


def contract_rows(left_side, right_side):
    return lax.dot_general(
        left_side, right_side, (((0,), (0,)), ((), ())), preferred_element_type=f32
    )


def contract_cols(left_side, right_side):
    return lax.dot_general(
        left_side, right_side, (((1,), (1,)), ((), ())), preferred_element_type=f32
    )


class Links:
    def __init__(self):
        self.wide = lax.axis_size("wide")
        self.narrow = lax.axis_size("narrow")
        self.depth = self.wide // 2
        wide_place = lax.axis_index("wide")
        narrow_place = lax.axis_index("narrow")
        self.device = wide_place * self.narrow + narrow_place
        self.z = wide_place // 2
        self.place = {"x": wide_place % 2, "y": narrow_place // 2, "c": narrow_place % 2}

    def swap(self, values, axis):
        if axis == "x":
            return lax.ppermute(values, "wide", [(i, i ^ 1) for i in range(self.wide)])
        step = 2 if axis == "y" else 1
        return lax.ppermute(values, "narrow", [(i, i ^ step) for i in range(self.narrow)])

    def cross(self, values, step):
        return lax.ppermute(values, "wide", [(i, i ^ (2 * step)) for i in range(self.wide)])

    def exchange(self, values, combine):
        for step in (1, 2):
            other = lax.ppermute(values, "narrow", [(i, i ^ step) for i in range(self.narrow)])
            values = combine(values, other)
        step = 1
        while step < self.wide:
            other = lax.ppermute(values, "wide", [(i, i ^ step) for i in range(self.wide)])
            values = combine(values, other)
            step *= 2
        return values

    def to_all(self, values):
        return lax.all_to_all(values, ("wide", "narrow"), 0, 0, tiled=True)

    def gather_early(self, shard, *before):
        near = shard[None]
        for step in self.bits()[:0:-1]:
            near = jnp.concatenate([near, after(self.cross(near, step), *before)])
        return near

    def gather_late(self, near):
        return jnp.concatenate([near, self.cross(near, 1)])

    def gather_depth(self, shard):
        return self.gather_late(self.gather_early(shard))

    def bits(self):
        return [1 << number for number in range(self.depth.bit_length() - 1)]

    def steps(self):
        found = [0]
        for step in self.bits()[::-1]:
            found = found + [number ^ step for number in found]
        return found

    def plane_first(self, near):
        cut = halves(near.shape[-1])
        left, right = near[..., :cut], near[..., cut:]
        return left, right, self.swap(left, "x"), self.swap(right, "y")

    def plane_second(self, left, right, left_x, right_y):
        left, right = jnp.stack([left, left_x]), jnp.stack([right, right_y])
        return [left, self.swap(left, "y"), right, self.swap(right, "x")]

    def plane_core(self, pieces):
        return pieces + [self.swap(piece, "c") for piece in pieces]

    def gather_plane(self, near):
        return self.plane_core(self.plane_second(*self.plane_first(near)))

    def assemble(self, pieces, core_first=False, folded=None):
        depth = self.depth
        unused, unused_depth, rows, cut = pieces[0].shape
        count, fold = folded or (0, 0)
        width = cut + pieces[2].shape[3] - count * fold

        def kernel(place, *refs):
            sources, target = refs[: len(pieces)], refs[len(pieces)]
            x, y, c = place[0], place[1], place[2]
            for number, source in enumerate(sources):
                far_core, far, second = number // 4, number % 2, number // 2 % 2
                to_c = 1 - c if far_core else c
                columns = slice(cut, width) if second else slice(0, cut)
                for side in range(2):
                    across_x, across_y = (far, side) if second else (side, far)
                    to_x = 1 - x if across_x else x
                    to_y = 1 - y if across_y else y
                    if core_first:
                        target[to_c, to_x, to_y, 0, :, columns] = source[side, 0]
                    elif second:
                        target[0, to_x, to_y, to_c, :, columns] = source[side, 0, :, : width - cut]
                        for number_in in range(count):
                            start = width - cut + number_in * fold
                            refs[-1][
                                0, to_x, to_y, to_c, number_in * rows : (number_in + 1) * rows
                            ] = source[side, 0, :, start : start + fold]
                    else:
                        target[0, to_x, to_y, to_c, :, columns] = source[side, 0]

        place = [self.place["x"], self.place["y"], self.place["c"]]
        place = jnp.stack(place + [self.z ^ step for step in self.steps()]).astype(jnp.int32)
        if core_first:
            shape = (2, 2, 2, depth, rows, width)
            target_spec = pl.BlockSpec(
                (2, 2, 2, 1, rows, width), lambda k, place: (0, 0, 0, place[3 + k], 0, 0)
            )
        else:
            shape = (depth, 2, 2, 2, rows, width)
            target_spec = pl.BlockSpec(
                (1, 2, 2, 2, rows, width), lambda k, place: (place[3 + k], 0, 0, 0, 0, 0)
            )
        shapes, target_specs = [jax.ShapeDtypeStruct(shape, pieces[0].dtype)], [target_spec]
        if count:
            shapes.append(
                jax.ShapeDtypeStruct((depth, 2, 2, 2, count * rows, fold), pieces[0].dtype)
            )
            target_specs.append(
                pl.BlockSpec(
                    (1, 2, 2, 2, count * rows, fold),
                    lambda k, place: (place[3 + k], 0, 0, 0, 0, 0),
                )
            )
        wholes = pl.pallas_call(
            kernel,
            out_shape=shapes,
            grid_spec=pltpu.PrefetchScalarGridSpec(
                num_scalar_prefetch=1,
                grid=(depth,),
                in_specs=[
                    pl.BlockSpec((2, 1, rows, piece.shape[3]), lambda k, place: (0, k, 0, 0))
                    for piece in pieces
                ],
                out_specs=target_specs,
            ),
            compiler_params=pltpu.CompilerParams(vmem_limit_bytes=24 * 2**20),
            name="assemble",
        )(place, *pieces)
        wholes = [whole.reshape(-1, whole.shape[-1]) for whole in wholes]
        return wholes if count else wholes[0]

    def exchange_plane(self, values):
        for axis in "xyc":
            dim = " xyc".index(axis) - 1
            mine = lax.dynamic_index_in_dim(values, self.place[axis], dim, keepdims=False)
            other = lax.dynamic_index_in_dim(values, 1 - self.place[axis], dim, keepdims=False)
            values = jnp.stack([mine, self.swap(other, axis)], axis=dim)
        return values.transpose(2, 0, 1, 3, 4).reshape(-1, values.shape[-1])

    def share_direct(self, values):
        pairs = []
        for wide in range(self.wide):
            for narrow in range(self.narrow):
                pairs.append((wide * self.narrow + narrow, (wide ^ 1) * self.narrow + (narrow ^ 2)))
        across = lax.ppermute(values, ("wide", "narrow"), pairs)
        return [values, self.swap(values, "y"), self.swap(values, "x"), across]

    def share_first(self, values):
        cut = halves(values.shape[-1])
        left, right = values[:, :cut], values[:, cut:]
        return left, right, self.swap(left, "x"), self.swap(right, "y")

    def share_second(self, left, right, left_x, right_y):
        left, right = jnp.stack([left, left_x]), jnp.stack([right, right_y])
        return left, right, self.swap(left, "y"), self.swap(right, "x")

    def share_last(self, *pieces):
        return list(pieces) + [self.swap(piece, "c") for piece in pieces]

    def scatter_plane(self, full, *before_second):
        cut = halves(full.shape[-1])
        x, y = self.place["x"], self.place["y"]

        def pick(values, spot, dim):
            return lax.dynamic_index_in_dim(values, spot, dim, keepdims=False)

        left, right = full[..., :cut], full[..., cut:]
        from_x = self.swap(pick(left, 1 - x, 0), "x")
        from_y = self.swap(pick(right, 1 - y, 1), "y")
        left = (pick(left, x, 0).astype(f32) + from_x.astype(f32)).astype(bf16)
        right = (pick(right, y, 1).astype(f32) + from_y.astype(f32)).astype(bf16)
        left, right = after(left, *before_second), after(right, *before_second)
        sends = pick(left, 1 - y, 0), pick(right, 1 - x, 0)
        from_y, from_x = self.swap(sends[0], "y"), self.swap(sends[1], "x")
        left = pick(left, y, 0).astype(f32) + from_y.astype(f32)
        right = pick(right, x, 0).astype(f32) + from_x.astype(f32)
        return jnp.concatenate([left, right], axis=-1).astype(bf16), sends

    def scatter_depth(self, near, *before_last):
        for step in self.bits():
            if step == self.bits()[-1]:
                near = after(near, *before_last)
            pairs = near.reshape((-1, 2) + near.shape[1:])
            bit = self.z // step % 2
            other = lax.dynamic_index_in_dim(pairs, 1 - bit, 1, keepdims=False)
            mine = lax.dynamic_index_in_dim(pairs, bit, 1, keepdims=False)
            send = other.astype(bf16)
            near = mine.astype(f32) + self.cross(send, step).astype(f32)
        return near[0], send


def halves(width):
    return width // 256 * 128


def tie(*values):
    return lax.optimization_barrier(values)


def after(values, *others):
    return lax.optimization_barrier((values, *others))[0]


def lane_halves(values, first):
    lane = lax.broadcasted_iota(jnp.int32, values.shape, 1)
    return jnp.where((lane < HEAD_DIM) == first, values, jnp.zeros_like(values))


def attend(qkv_all, pick_rows, allowed, micro_count):
    token_count = qkv_all.shape[0]
    width = qkv_all.shape[1] // 3
    pick_total = pick_rows.shape[0]
    length, picked = token_count // micro_count, pick_total // micro_count
    pair = 2 * HEAD_DIM
    scale = HEAD_DIM ** (-0.5)

    def kernel(qkv_ref, pick_ref, allowed_ref, context_ref, query_ref, prob_ref):
        query_ref[...] = jnp.dot(
            pick_ref[...], qkv_ref[:, :width], preferred_element_type=f32
        ).astype(bf16)
        for micro in range(micro_count):
            rows = slice(micro * picked, (micro + 1) * picked)
            keep = allowed_ref[rows] > 0.5
            keep = jnp.concatenate([keep, keep], axis=0)
            for number in range(width // pair):
                columns = slice(number * pair, (number + 1) * pair)
                keys = qkv_ref[
                    micro * length : (micro + 1) * length,
                    width + number * pair : width + (number + 1) * pair,
                ]
                values = qkv_ref[
                    micro * length : (micro + 1) * length,
                    2 * width + number * pair : 2 * width + (number + 1) * pair,
                ]
                query = query_ref[rows, columns]
                both = jnp.concatenate(
                    [lane_halves(query, True), lane_halves(query, False)], axis=0
                )
                scores = contract_cols(both, keys) * scale
                scores = jnp.where(keep, scores, neg_fill)
                shifted = jnp.exp(scores - jnp.max(scores, axis=1, keepdims=True))
                probs = shifted / jnp.sum(shifted, axis=1, keepdims=True)
                prob_ref[micro, number] = probs
                mixed = jnp.dot(probs.astype(bf16), values, preferred_element_type=f32)
                context_ref[rows, columns] = (
                    lane_halves(mixed[:picked], True) + lane_halves(mixed[picked:], False)
                ).astype(bf16)

    return pl.pallas_call(
        kernel,
        out_shape=(
            jax.ShapeDtypeStruct((pick_total, width), bf16),
            jax.ShapeDtypeStruct((pick_total, width), bf16),
            jax.ShapeDtypeStruct((micro_count, width // pair, 2 * picked, length), f32),
        ),
        compiler_params=pltpu.CompilerParams(vmem_limit_bytes=32 * 2**20),
        name="attend",
    )(qkv_all, pick_rows, allowed)


def attend_backward(qkv_all, pick_rows, query_all, probs_all, grad_context, micro_count):
    token_count = qkv_all.shape[0]
    width = qkv_all.shape[1] // 3
    pick_total = pick_rows.shape[0]
    length, picked = token_count // micro_count, pick_total // micro_count
    pair = 2 * HEAD_DIM
    scale = HEAD_DIM ** (-0.5)

    def kernel(qkv_ref, pick_ref, query_ref, prob_ref, grad_ref, out_ref, query_grad_ref):
        for micro in range(micro_count):
            rows = slice(micro * picked, (micro + 1) * picked)
            tokens = slice(micro * length, (micro + 1) * length)
            for number in range(width // pair):
                columns = slice(number * pair, (number + 1) * pair)
                key_columns = slice(width + number * pair, width + (number + 1) * pair)
                value_columns = slice(2 * width + number * pair, 2 * width + (number + 1) * pair)
                query, grad = query_ref[rows, columns], grad_ref[rows, columns]
                queries = jnp.concatenate(
                    [lane_halves(query, True), lane_halves(query, False)], axis=0
                )
                grads = jnp.concatenate(
                    [lane_halves(grad, True), lane_halves(grad, False)], axis=0
                )
                probs = prob_ref[micro, number]
                grad_probs = contract_cols(grads, qkv_ref[tokens, value_columns])
                inner = jnp.sum(probs * grad_probs, axis=1, keepdims=True)
                grad_scores = (probs * (grad_probs - inner)).astype(bf16)
                mixed = (
                    jnp.dot(
                        grad_scores, qkv_ref[tokens, key_columns], preferred_element_type=f32
                    )
                    * scale
                )
                query_grad_ref[rows, columns] = (
                    lane_halves(mixed[:picked], True) + lane_halves(mixed[picked:], False)
                ).astype(bf16)
                out_ref[tokens, key_columns] = (
                    contract_rows(grad_scores, queries) * scale
                ).astype(bf16)
                out_ref[tokens, value_columns] = contract_rows(probs.astype(bf16), grads).astype(
                    bf16
                )
        out_ref[:, :width] = contract_rows(pick_ref[...], query_grad_ref[...]).astype(bf16)

    return pl.pallas_call(
        kernel,
        out_shape=jax.ShapeDtypeStruct(qkv_all.shape, bf16),
        scratch_shapes=[pltpu.VMEM((pick_total, width), bf16)],
        compiler_params=pltpu.CompilerParams(vmem_limit_bytes=32 * 2**20),
        name="attend_backward",
    )(qkv_all, pick_rows, query_all, probs_all, grad_context)


def plane_products(known, grads, attn_grads, depth, widths):
    hidden, model = widths
    rows = grads[0].shape[-2]
    width = hidden + 2 * model
    down_rows, model_rows = hidden // (8 * depth), model // (8 * depth)
    down_width, model_width = hidden // 8, model // 8

    def kernel(known_ref, *refs):
        down_ref, up_ref, out_ref, grads_ref = refs[10:]
        cut = grads[0].shape[-1]
        for far_core in range(2):
            left, right, left_y, right_x = refs[4 * far_core : 4 * far_core + 4]
            attn = refs[8 + far_core]
            for x in range(2):
                for y in range(2):
                    spot = pl.ds(((far_core * 2 + x) * 2 + y) * rows, rows)
                    grads_ref[spot, :cut] = (left_y if y else left)[x]
                    grads_ref[spot, cut : hidden + model] = (right_x if x else right)[y]
                    grads_ref[spot, hidden + model :] = attn[2 * x + y]
        down_ref[...] = contract_rows(
            known_ref[:, :down_width], grads_ref[:, hidden : hidden + model]
        ).astype(bf16)
        up_ref[...] = contract_rows(
            known_ref[:, down_width : down_width + model_width], grads_ref[:, :hidden]
        ).astype(bf16)
        out_ref[...] = contract_rows(
            known_ref[:, down_width + model_width :], grads_ref[:, hidden + model :]
        ).astype(bf16)

    in_vmem = pl.BlockSpec(memory_space=pltpu.VMEM)
    down, up, out = pl.pallas_call(
        kernel,
        in_specs=[in_vmem] * 11,
        out_shape=(
            jax.ShapeDtypeStruct((depth * down_rows, model), bf16),
            jax.ShapeDtypeStruct((depth * model_rows, hidden), bf16),
            jax.ShapeDtypeStruct((depth * model_rows, model), bf16),
        ),
        scratch_shapes=[
            pltpu.VMEM((8 * rows, width), bf16),
        ],
        compiler_params=pltpu.CompilerParams(vmem_limit_bytes=48 * 2**20),
        name="plane_products",
    )(known, *grads, *attn_grads)
    return (
        down.reshape(depth, down_rows, model),
        up.reshape(depth, model_rows, hidden),
        out.reshape(depth, model_rows, model),
    )


def on_lane(place, value):
    lane = lax.broadcasted_iota(jnp.int32, (1, 128), 1)
    return jnp.where(lane == place, value, 0.0)


def whole_sum(values):
    return jnp.sum(jnp.sum(values, axis=0, keepdims=True), axis=1, keepdims=True)


def sum_squares(all_grads, weight_row, target_sum, devices):
    def kernel(table_ref, target_ref, weight_ref, *refs):
        grads, rows_ref = refs[:-1], refs[-1]
        row = on_lane(0, table_ref[...])
        for place, grad in enumerate(grads):
            row = row + on_lane(place + 1, whole_sum(grad[...] * grad[...]))
        rows_ref[:, :128] = jnp.broadcast_to(row, (devices, 128))
        rows_ref[:, 128:] = jnp.broadcast_to(
            weight_ref[...] + on_lane(64, target_ref[...]), (devices, 128)
        )

    table_square = jnp.sum(all_grads[0] * all_grads[0]).reshape(1, 1)
    return pl.pallas_call(
        kernel,
        out_shape=jax.ShapeDtypeStruct((devices, 256), f32),
        name="sum_squares",
    )(table_square, target_sum.reshape(1, 1), weight_row, *all_grads[1:])


grid_steps = 4


def unfold(whole, count, width, shard_rows):
    devices = whole.shape[0] // shard_rows
    group = max(1, min(devices, 256 // shard_rows))

    def kernel(source_ref, target_ref):
        for number in range(count):
            block = source_ref[:, number * width : (number + 1) * width]
            target_ref[:, number] = block.reshape(group, shard_rows, width)

    rows = pl.pallas_call(
        kernel,
        grid=(devices // group,),
        in_specs=[pl.BlockSpec((group * shard_rows, count * width), lambda i: (i, 0))],
        out_specs=pl.BlockSpec((group, count, shard_rows, width), lambda i: (i, 0, 0, 0)),
        out_shape=jax.ShapeDtypeStruct((devices, count, shard_rows, width), whole.dtype),
        compiler_params=pltpu.CompilerParams(vmem_limit_bytes=32 * 2**20),
        name="unfold",
    )(whole)
    return rows.reshape(-1, width)


row_block = 256


def head_logits(head_rows, table_low, targets, base, block_size):
    row_count, width = head_rows.shape
    columns = table_low.shape[0]
    block = min(row_block, row_count)

    def kernel(base_ref, rows_ref, table_ref, targets_ref, logits_ref, top_ref, sum_ref, hit_ref):
        step = pl.program_id(0)
        place = lax.broadcasted_iota(jnp.int32, (1, columns), 1)
        column = jnp.where(place < block_size, place + base_ref[0], VOCAB)
        fill = jnp.where(column < VOCAB, 0.0, neg_fill)
        logits = contract_cols(rows_ref[...], table_ref[...]) + fill
        logits_ref[...] = logits
        top = jnp.max(logits, axis=1, keepdims=True)
        total = jnp.sum(jnp.exp(logits - top), axis=1, keepdims=True)
        top_ref[...] = jnp.broadcast_to(top, (block, 128)).T[:1]
        sum_ref[...] = jnp.broadcast_to(total, (block, 128)).T[:1]

        @pl.when(step == 0)
        def _():
            hit_ref[...] = jnp.zeros_like(hit_ref)

        hits = targets_ref[...] == column
        hit_ref[...] += jnp.broadcast_to(whole_sum(jnp.where(hits, logits, 0.0)), (1, 128))

    return pl.pallas_call(
        kernel,
        out_shape=(
            jax.ShapeDtypeStruct((row_count, columns), f32),
            jax.ShapeDtypeStruct((1, row_count), f32),
            jax.ShapeDtypeStruct((1, row_count), f32),
            jax.ShapeDtypeStruct((1, 128), f32),
        ),
        grid=(row_count // block,),
        in_specs=[
            pl.BlockSpec(memory_space=pltpu.SMEM),
            pl.BlockSpec((block, width), lambda k: (k, 0)),
            pl.BlockSpec((columns, width), lambda k: (0, 0)),
            pl.BlockSpec((block, 1), lambda k: (k, 0)),
        ],
        out_specs=(
            pl.BlockSpec((block, columns), lambda k: (k, 0)),
            pl.BlockSpec((1, block), lambda k: (0, k)),
            pl.BlockSpec((1, block), lambda k: (0, k)),
            pl.BlockSpec((1, 128), lambda k: (0, 0)),
        ),
        compiler_params=pltpu.CompilerParams(vmem_limit_bytes=56 * 2**20),
        name="head_logits",
    )(base.reshape(1), head_rows, table_low, targets)


def head_grads(logits, log_total, table_low, targets, base, half, count_all, block_size, add=None):
    row_count, columns = logits.shape
    width = table_low.shape[1]
    block = min(row_block, row_count // 2)
    steps = row_count // 2 // block
    scale = 1.0 / count_all

    def kernel(place_ref, logits_ref, total_ref, table_ref, targets_ref, *refs):
        grads_ref, out_ref = refs[-2:]
        place = lax.broadcasted_iota(jnp.int32, (1, columns), 1)
        column = jnp.where(place < block_size, place + place_ref[1], VOCAB)
        total = jnp.broadcast_to(total_ref[...], (128, block)).T[:, :1]
        hits = targets_ref[...] == column
        probs = jnp.exp(logits_ref[...] - total)
        grads = ((probs - jnp.where(hits, 1.0, 0.0)) * scale).astype(bf16)
        grads_ref[...] = grads
        product = matmul(grads, table_ref[...])
        if add is not None:
            product = product + refs[0][...].astype(f32)
        out_ref[...] = product.astype(bf16)

    half_spec = pl.BlockSpec((block, width), lambda k, place: (k, 0))
    return pl.pallas_call(
        kernel,
        out_shape=(
            jax.ShapeDtypeStruct((row_count // 2, columns), bf16),
            jax.ShapeDtypeStruct((row_count // 2, width), bf16),
        ),
        grid_spec=pltpu.PrefetchScalarGridSpec(
            num_scalar_prefetch=1,
            grid=(steps,),
            in_specs=[
                pl.BlockSpec((block, columns), lambda k, place: (place[0] * steps + k, 0)),
                pl.BlockSpec((1, block), lambda k, place: (0, place[0] * steps + k)),
                pl.BlockSpec((columns, width), lambda k, place: (0, 0)),
                pl.BlockSpec((block, 1), lambda k, place: (place[0] * steps + k, 0)),
            ]
            + ([] if add is None else [half_spec]),
            out_specs=(
                pl.BlockSpec((block, columns), lambda k, place: (k, 0)),
                half_spec,
            ),
        ),
        compiler_params=pltpu.CompilerParams(vmem_limit_bytes=56 * 2**20),
        name="head_grads",
    )(
        jnp.stack([half, base]).astype(jnp.int32),
        logits,
        log_total,
        table_low,
        targets,
        *(() if add is None else (add,)),
    )


def weight_squares(masters):
    table_rows = -(-masters[0].shape[0] // (8 * grid_steps)) * 8
    table_count = masters[0].shape[0]

    def kernel(table_ref, *refs):
        others, row_ref = refs[:-1], refs[-1]
        step = pl.program_id(0)

        @pl.when(step == 0)
        def _():
            row = jnp.zeros((1, 128), f32)
            for place, other in enumerate(others):
                row = row + on_lane(place + 1, whole_sum(other[...] * other[...]))
            row_ref[...] = row

        place = step * table_rows + lax.broadcasted_iota(jnp.int32, (table_rows, 1), 0)
        square = jnp.where(place < table_count, table_ref[...] * table_ref[...], 0.0)
        row_ref[...] += on_lane(0, whole_sum(square))

    return pl.pallas_call(
        kernel,
        grid=(grid_steps,),
        in_specs=[pl.BlockSpec((table_rows, masters[0].shape[1]), lambda k: (k, 0))]
        + [
            pl.BlockSpec(array.shape, lambda k: (0, 0), pipeline_mode=pl.Buffered(1))
            for array in masters[1:]
        ],
        out_specs=pl.BlockSpec((1, 128), lambda k: (0, 0)),
        out_shape=jax.ShapeDtypeStruct((1, 128), f32),
        compiler_params=pltpu.CompilerParams(vmem_limit_bytes=32 * 2**20),
        name="weight_squares",
    )(*masters)


def group_specs(arrays):
    table_rows = -(-arrays[0].shape[0] // (8 * grid_steps)) * 8
    specs = [pl.BlockSpec((table_rows, arrays[0].shape[1]), lambda k: (k, 0))]
    for array in arrays[1:5]:
        rows, width = array.shape
        specs.append(pl.BlockSpec((rows, width // grid_steps), lambda k: (0, k)))
    specs.append(pl.BlockSpec(arrays[5].shape, lambda k: (0, 0)))
    return specs


def lamb_directions(totals, all_grads, firsts, seconds, masters):
    devices = totals.shape[0]
    table_count = all_grads[0].shape[0]
    specs = group_specs(all_grads)
    table_rows = specs[0].block_shape[0]
    first_scale = 1.0 / (1.0 - beta_first**step_count)
    second_scale = 1.0 / (1.0 - beta_second**step_count)

    def kernel(totals_ref, *refs):
        grads, olds, squares, weights = refs[:6], refs[6:12], refs[12:18], refs[18:24]
        new_olds, new_squares, directions, rows_ref = refs[24:30], refs[30:36], refs[36:42], refs[42]
        step = pl.program_id(0)
        grad_total = jnp.sum(totals_ref[:, :128], axis=0, keepdims=True)
        factor = jnp.minimum(
            1.0, clip_limit * lax.rsqrt(jnp.sum(grad_total, axis=1, keepdims=True))
        )

        @pl.when(step == 0)
        def _():
            rows_ref[...] = jnp.zeros_like(rows_ref)

        def update(group, rows, live=None):
            clipped = factor * grads[group][rows]
            new_old = beta_first * olds[group][rows] + (1.0 - beta_first) * clipped
            new_square = beta_second * squares[group][rows] + (1.0 - beta_second) * clipped * clipped
            direction = (new_old * first_scale) / (
                jnp.sqrt(new_square * second_scale) + adam_epsilon
            ) + decay_rates[group] * weights[group][rows]
            new_olds[group][rows] = new_old
            new_squares[group][rows] = new_square
            directions[group][rows] = direction
            square = direction * direction
            return square if live is None else jnp.where(live, square, 0.0)

        def table_part(part, total):
            rows = pl.ds(pl.multiple_of(part * 8, 8), 8)
            place = step * table_rows + part * 8 + lax.broadcasted_iota(
                jnp.int32, (8, 1), 0
            )
            return total + update(0, (rows, slice(None)), place < table_count)

        table_total = lax.fori_loop(
            0, table_rows // 8, table_part, jnp.zeros((8, all_grads[0].shape[1]), f32)
        )
        row = on_lane(0, whole_sum(table_total))
        for group in range(1, 5):
            row = row + on_lane(group, whole_sum(update(group, (slice(None), slice(None)))))
        rows_ref[...] += jnp.broadcast_to(row, rows_ref.shape)

        @pl.when(step == 0)
        def _():
            row = on_lane(5, whole_sum(update(5, (slice(None), slice(None)))))
            rows_ref[...] += jnp.broadcast_to(row, rows_ref.shape)

    shapes = [jax.ShapeDtypeStruct(array.shape, f32) for array in all_grads]
    results = pl.pallas_call(
        kernel,
        grid=(grid_steps,),
        in_specs=[pl.BlockSpec(totals.shape, lambda k: (0, 0))] + specs * 4,
        out_specs=specs * 3 + [pl.BlockSpec((devices, 128), lambda k: (0, 0))],
        out_shape=shapes * 3 + [jax.ShapeDtypeStruct((devices, 128), f32)],
        compiler_params=pltpu.CompilerParams(vmem_limit_bytes=56 * 2**20),
        name="lamb_directions",
    )(totals, *all_grads, *firsts, *seconds, *masters)
    return results[:6], results[6:12], results[12:18], results[18]


def lamb_weights(totals, update_rows, directions, masters):
    specs = group_specs(masters)

    def kernel(totals_ref, updates_ref, *refs):
        moves, weights, news, facts_ref = refs[:6], refs[6:12], refs[12:18], refs[18]
        step = pl.program_id(0)
        lane = lax.broadcasted_iota(jnp.int32, (1, 128), 1)
        grad_total = jnp.sum(totals_ref[:, :128], axis=0, keepdims=True)
        weight_total = jnp.sum(totals_ref[:, 128:], axis=0, keepdims=True)
        update_total = jnp.sum(updates_ref[...], axis=0, keepdims=True)
        weight_norms = jnp.where(lane < 6, jnp.sqrt(jnp.maximum(weight_total, 0.0)), 0.0)
        update_norms = jnp.where(lane < 6, jnp.sqrt(update_total), 1.0)
        rates = learn_rate * weight_norms / update_norms
        for group in range(5):
            rate = jnp.sum(jnp.where(lane == group, rates, 0.0), axis=1, keepdims=True)
            news[group][...] = weights[group][...] - rate * moves[group][...]

        @pl.when(step == 0)
        def _():
            rate = jnp.sum(jnp.where(lane == 5, rates, 0.0), axis=1, keepdims=True)
            news[5][...] = weights[5][...] - rate * moves[5][...]
            grad_norm = jnp.sqrt(jnp.sum(grad_total, axis=1, keepdims=True))
            factor = jnp.minimum(1.0, clip_limit / grad_norm)
            target = jnp.sum(jnp.where(lane == 64, weight_total, 0.0), axis=1, keepdims=True)
            facts_ref[0:1] = factor * jnp.sqrt(grad_total)
            facts_ref[1:2] = weight_norms
            facts_ref[2:3] = update_norms
            facts_ref[3:4] = jnp.broadcast_to(grad_norm, (1, 128))
            facts_ref[4:5] = jnp.broadcast_to(target, (1, 128))

    results = pl.pallas_call(
        kernel,
        grid=(grid_steps,),
        in_specs=[
            pl.BlockSpec(totals.shape, lambda k: (0, 0)),
            pl.BlockSpec(update_rows.shape, lambda k: (0, 0)),
        ]
        + specs * 2,
        out_specs=specs + [pl.BlockSpec((8, 128), lambda k: (0, 0))],
        out_shape=[jax.ShapeDtypeStruct(array.shape, f32) for array in masters]
        + [jax.ShapeDtypeStruct((8, 128), f32)],
        compiler_params=pltpu.CompilerParams(vmem_limit_bytes=56 * 2**20),
        name="lamb_weights",
    )(totals, update_rows, *directions, *masters)
    return results[:6], results[6]


def per_device(
    token_ids,
    doc_ids,
    loss_positions,
    tied_table_master,
    qkv_master,
    out_master,
    up_master,
    down_master,
    norm_master,
    table_first_moment,
    first_qkv,
    first_out,
    first_up,
    first_down,
    first_norms,
    table_second_moment,
    second_qkv,
    second_out,
    second_up,
    second_down,
    second_norms,
):
    links = Links()
    devices = links.wide * links.narrow
    micro_count, unused, length = token_ids.shape
    picked_count = loss_positions.shape[2]
    token_count = micro_count * length
    pick_total = micro_count * picked_count
    model_width = tied_table_master.shape[1]
    head_count = model_width // HEAD_DIM
    block_size = tied_table_master.shape[0]
    count_all = devices * pick_total
    shard_rows = qkv_master.shape[0]

    tokens = token_ids.reshape(token_count)
    picks = loss_positions.reshape(micro_count, picked_count)
    documents = doc_ids.reshape(micro_count, length)
    mean_load = token_count / devices
    slots = int(math.ceil((mean_load + 6.0 * math.sqrt(mean_load)) / 8.0)) * 8
    owner = tokens // block_size
    local_row = tokens % block_size
    token_place = jnp.arange(token_count)
    earlier = (owner[:, None] == owner[None, :]) & (token_place[None, :] < token_place[:, None])
    rank = jnp.sum(earlier.astype(jnp.int32), axis=1)
    most = jnp.max(rank) + 1
    slot_place = jnp.arange(devices * slots)
    line = -(-(slots + 1 + pick_total) // 128) * 128

    pick_hits = picks[:, :, None] == jnp.arange(length)[None, None, :]
    next_hits = picks[:, :, None] + 1 == jnp.arange(length)[None, None, :]
    own_targets = jnp.sum(
        jnp.where(next_hits, token_ids.reshape(micro_count, 1, length), 0), axis=2
    ).reshape(-1)
    pick_docs = jnp.sum(jnp.where(pick_hits, documents[:, None, :], 0), axis=2)

    def slot_of(round_index):
        inside = (rank >= round_index * slots) & (rank < (round_index + 1) * slots)
        return jnp.where(inside, owner * slots + rank - round_index * slots, -1)

    def message_of(slot):
        wanted = jnp.sum(
            jnp.where(slot[None, :] == slot_place[:, None], local_row[None, :] + 1, 0), axis=1
        ) - 1
        wanted = wanted.reshape(devices, slots)
        return jnp.concatenate(
            [
                wanted,
                jnp.broadcast_to(most, (devices, 1)),
                jnp.broadcast_to(own_targets[None, :], (devices, pick_total)),
                jnp.zeros((devices, line - slots - 1 - pick_total), jnp.int32),
            ],
            axis=1,
        )

    def ask(round_index):
        slot = slot_of(round_index)
        return slot, links.to_all(message_of(slot))[:, :slots].reshape(-1)

    def find(asked):
        row_hits = (asked[:, None] == jnp.arange(padded_rows)[None, :]).astype(bf16)
        return matmul(row_hits, table_low).astype(bf16)

    def place_rows(slot, landed):
        token_hits = (slot[:, None] == slot_place[None, :]).astype(bf16)
        return matmul(token_hits, landed).astype(bf16)

    def give(slot, grad_low):
        token_hits = (slot[:, None] == slot_place[None, :]).astype(bf16)
        return contract_rows(token_hits, grad_low).astype(bf16)

    def take(asked, landed):
        row_hits = (asked[None, :] == jnp.arange(block_size)[:, None]).astype(bf16)
        return matmul(row_hits, landed)

    gain_width = 128
    qkv_width = qkv_master.shape[1]
    gain_shard = jnp.pad(norm_master, ((0, 0), (0, gain_width - norm_master.shape[1])))
    slot_first = slot_of(0)
    masters = (tied_table_master, qkv_master, out_master, up_master, down_master, norm_master)
    first_shard = jnp.concatenate([qkv_master, gain_shard], axis=1).astype(bf16)
    first_early = links.gather_early(first_shard)
    first_near = links.gather_late(first_early)
    message = message_of(slot_first)
    answer = links.to_all(message)
    padded_rows = -(-block_size // 128) * 128
    table_low = jnp.pad(
        after(tied_table_master, message), ((0, padded_rows - block_size), (0, 0))
    ).astype(bf16)
    asked_first = answer[:, :slots].reshape(-1)
    rounds = (jnp.max(answer[:, slots]) + slots - 1) // slots
    targets = answer[:, slots + 1 : slots + 1 + pick_total]
    targets = targets.reshape(links.depth, 2, 2, 2, pick_total).transpose(3, 1, 2, 0, 4).reshape(-1)
    fold_count = down_master.shape[0] // shard_rows
    second_shard = jnp.concatenate(
        [
            down_master[number * shard_rows : (number + 1) * shard_rows]
            for number in range(fold_count)
        ]
        + [up_master, out_master],
        axis=1,
    )
    second_whole = lax.all_gather(
        second_shard.astype(bf16), ("wide", "narrow"), axis=0, tiled=True
    )
    first_parts = links.plane_first(first_near)
    found = after(find(asked_first), first_near)
    landed = links.to_all(found)
    weight_row = weight_squares(tie(*masters, found)[:6])
    first_parts = [after(part, weight_row, table_low) for part in first_parts]
    first_pieces = links.plane_second(*first_parts)
    first_whole = links.assemble(links.plane_core(first_pieces))
    qkv_weight = first_whole[:, :qkv_width]
    gain_entries = first_whole[:, qkv_width : qkv_width + 6].astype(f32).T

    def more_rows(state):
        round_index, embedded = state
        slot, asked = ask(round_index)
        return (round_index + 1, embedded + place_rows(slot, links.to_all(find(asked))))

    unused_round, x_low = lax.while_loop(
        lambda state: state[0] < rounds,
        more_rows,
        (jnp.ones((), jnp.int32), place_rows(slot_first, landed)),
    )

    x_embed = x_low.astype(f32)
    normed_one = layer_norm(x_embed, gain_entries[0], gain_entries[1]).astype(bf16)
    qkv_all = matmul(normed_one, qkv_weight).astype(bf16)
    pick_rows = (
        pick_hits[:, :, None, :] & jnp.eye(micro_count, dtype=bool)[:, None, :, None]
    ).reshape(pick_total, token_count).astype(bf16)
    x_embed_picked = matmul(pick_rows, x_low)
    allowed = (jnp.arange(length)[None, None, :] <= picks[:, :, None]) & (
        documents[:, None, :] == pick_docs[:, :, None]
    )
    context, queries, probs = attend(
        qkv_all, pick_rows, allowed.reshape(pick_total, length).astype(f32), micro_count
    )
    down_weight = unfold(second_whole, fold_count, model_width, shard_rows)
    hidden = up_master.shape[1]
    folded = fold_count * model_width
    up_weight = second_whole[:, folded : folded + hidden]
    out_weight = second_whole[:, folded + hidden :]
    x_attn = x_embed_picked + matmul(context, out_weight)
    normed_two = layer_norm(x_attn, gain_entries[2], gain_entries[3]).astype(bf16)
    up_value = matmul(normed_two, up_weight)
    activated = gelu_tanh(up_value).astype(bf16)
    x_out = x_attn + matmul(activated, down_weight)
    picked_low = layer_norm(x_out, gain_entries[4], gain_entries[5]).astype(bf16)

    head_pieces = links.plane_second(*links.plane_first(links.gather_depth(picked_low)))
    head_rows = links.assemble(
        links.plane_core(head_pieces), core_first=True
    )
    base = links.device * block_size
    target_column = targets[:, None]
    logits, local_top, local_sum, target_sum = head_logits(
        head_rows, table_low, target_column, base, block_size
    )
    target_sum = target_sum[:, :1]

    def merge_totals(first, second):
        top = jnp.maximum(first[0], second[0])
        total = first[1] * jnp.exp(first[0] - top) + second[1] * jnp.exp(second[0] - top)
        return jnp.stack([top, total])

    merged = links.exchange(jnp.concatenate([local_top, local_sum]), merge_totals)
    def by_owner(values, block_rows):
        if block_rows % 128 == 0:
            blocks = values.reshape(pick_total, links.depth, 8, block_rows)
            blocks = blocks.transpose(2, 0, 1, 3).reshape(8 * pick_total, -1)
            return blocks.reshape(8, pick_total, -1)
        count = values.shape[1]
        place = jnp.arange(count)
        source = place % (count // 8) // block_rows * 8 + place // (count // 8)
        source = source * block_rows + place % block_rows
        order = (jnp.arange(count)[:, None] == source[None, :]).astype(bf16)
        ordered = matmul(values, order).astype(bf16)
        return ordered.reshape(pick_total, 8, count // 8).transpose(1, 0, 2)

    known = jnp.concatenate(
        [
            by_owner(activated, down_master.shape[0]),
            by_owner(normed_two, shard_rows),
            by_owner(context, shard_rows),
        ],
        axis=2,
    )
    known = known.reshape(2, 2, 2, pick_total, -1)
    log_total = merged[0] + jnp.log(merged[1])
    core = links.place["c"]
    log_row = log_total[None]
    far_grads, to_core = head_grads(
        logits, log_row, table_low, target_column, base, 1 - core, count_all, block_size
    )
    from_core = links.swap(to_core, "c")
    own_grads, near_sum = head_grads(
        logits, log_row, table_low, target_column, base, core, count_all, block_size, from_core
    )
    own_rows = [
        lax.dynamic_slice_in_dim(head_rows, spot * far_grads.shape[0], far_grads.shape[0], 0)
        for spot in (1 - core, core)
    ]
    grad_near, unused = links.scatter_plane(
        near_sum.reshape(2, 2, links.depth, pick_total, model_width),
        known,
    )
    known = links.exchange_plane(after(known, grad_near))
    grad_picked, unused = links.scatter_depth(grad_near)

    grad_x_out, gain_last, shift_last = norm_backward(
        x_out, gain_entries[4], gain_entries[5], grad_picked
    )
    grad_mlp = grad_x_out.astype(bf16)
    unused, gelu_pull = jax.vjp(gelu_tanh, up_value)
    grad_up_low = gelu_pull(contract_cols(grad_mlp, down_weight))[0].astype(bf16)
    grad_parts = links.share_first(jnp.concatenate([grad_up_low, grad_mlp], axis=1))
    grad_x_attn, gain_two, shift_two = norm_backward(
        x_attn, gain_entries[2], gain_entries[3], contract_cols(grad_up_low, up_weight)
    )
    grad_x_attn = grad_x_out + grad_x_attn
    grad_attn_low = grad_x_attn.astype(bf16)
    grad_context = contract_cols(grad_attn_low, out_weight).astype(bf16)
    attn_parts = links.share_direct(grad_attn_low)
    grad_context = after(grad_context, *grad_parts)
    grad_parts = links.share_second(*grad_parts)
    grad_qkv_low = attend_backward(
        qkv_all, pick_rows, queries, probs, grad_context, micro_count
    )
    late = after(grad_qkv_low, known, *attn_parts)
    grad_x_one, gain_one, shift_one = norm_backward(
        x_embed, gain_entries[0], gain_entries[1], contract_cols(late, qkv_weight)
    )
    grad_x_embed = grad_x_one + lax.dot_general(
        pick_rows.astype(f32),
        grad_x_attn,
        (((0,), (0,)), ((), ())),
        precision=lax.Precision.HIGHEST,
        preferred_element_type=f32,
    )
    grad_embed_low = grad_x_embed.astype(bf16)
    sent = give(slot_first, grad_embed_low)
    returned = links.to_all(sent)
    half_place = jnp.arange(model_width // 2)
    half_row = half_place % shard_rows
    half_z = half_place // shard_rows % links.depth
    half_plane = half_place // shard_rows // links.depth

    def qkv_part(spot):
        source = ((half_z * 4 + half_plane) * 2 + spot) * shard_rows + half_row
        columns = (jnp.arange(model_width)[:, None] == source[None, :]).astype(bf16)
        return contract_rows(matmul(normed_one, columns).astype(bf16), grad_qkv_low)

    grad_qkv_low = after(grad_qkv_low, sent, *attn_parts, *grad_parts)
    to_core = qkv_part(1 - core).astype(bf16)
    from_core = links.swap(to_core, "c")
    last_mine = (qkv_part(core) + from_core.astype(f32)).astype(bf16)
    last_near, last_sends = links.scatter_plane(
        last_mine.reshape(2, 2, links.depth, shard_rows, qkv_width), returned
    )
    down_near, up_near, out_near = plane_products(
        known,
        links.share_last(*[after(part, last_mine) for part in grad_parts]),
        links.share_last(after(jnp.stack(attn_parts), last_mine)),
        links.depth,
        (activated.shape[1], model_width),
    )

    last_near = jnp.concatenate([last_near, out_near], axis=-1)
    down_grad, down_send = links.scatter_depth(down_near, returned)
    up_grad, up_send = links.scatter_depth(up_near, returned)
    last_grad, unused = links.scatter_depth(last_near)
    qkv_grad, out_grad = last_grad[:, :qkv_width], last_grad[:, qkv_width:]
    far_grads = after(far_grads, returned, down_send, up_send, *last_sends)
    own_grads = after(own_grads, far_grads)
    table_head = contract_rows(far_grads[:, :block_size], own_rows[0]) + contract_rows(
        own_grads[:, :block_size], own_rows[1]
    )
    gain_one = after(gain_one, returned, down_send, up_send, *last_sends)
    gain_grads = jnp.stack(
        [gain_one, shift_one, gain_two, shift_two, gain_last, shift_last]
    ).reshape(6, devices, shard_rows)
    gain_grads = jnp.pad(
        gain_grads.transpose(1, 0, 2).reshape(devices, 6 * shard_rows),
        ((0, 0), (0, -6 * shard_rows % 128)),
    )
    gain_grad = jnp.sum(links.to_all(after(gain_grads, returned)), axis=0)[: 6 * shard_rows]
    gain_grad = gain_grad.reshape(6, shard_rows).T

    def more_grads(state):
        round_index, earlier_grad = state
        slot, asked = ask(round_index)
        returned_rows = links.to_all(give(slot, grad_embed_low))
        return (round_index + 1, earlier_grad + take(asked, returned_rows))

    unused_round, table_grad = lax.while_loop(
        lambda state: state[0] < rounds,
        more_grads,
        (
            jnp.ones((), jnp.int32),
            table_head + take(asked_first, after(returned, down_send, up_send, *last_sends)),
        ),
    )

    all_grads = (table_grad, qkv_grad, out_grad, up_grad, down_grad, gain_grad)
    firsts = (table_first_moment, first_qkv, first_out, first_up, first_down, first_norms)
    seconds = (table_second_moment, second_qkv, second_out, second_up, second_down, second_norms)
    totals = links.to_all(sum_squares(all_grads, weight_row, target_sum, devices))
    new_firsts, new_seconds, directions, update_rows = lamb_directions(
        totals, all_grads, firsts, seconds, masters
    )
    new_weights, facts = lamb_weights(totals, links.to_all(update_rows), directions, masters)
    return (
        (jnp.sum(log_total) - facts[4, 0]) / count_all,
        facts[3, 0],
        facts[:3, :6],
        *new_weights,
        *new_firsts,
        *new_seconds,
    )


def solution(mesh):
    rows = P(("wide", "narrow"), None)
    ids = P(None, ("wide", "narrow"), None)
    return jax.shard_map(
        per_device,
        mesh=mesh,
        in_specs=(ids,) * 3 + (rows,) * 18,
        out_specs=(P(),) * 3 + (rows,) * 18,
        check_vma=False,
    )
```
